32 devices in a mesh: wide: 8 (over z, x), narrow: 4 (over y, core).
Axes of the slice: x: 2, y: 2, z: 4, core: 2. Of those that a mesh axis runs over, the one named last changes fastest.
Arguments:
- block_input: bfloat16 [32, 1024, 256], P(('wide', 'narrow')), may hold values from -120 to 120
- prior_first: bfloat16 [32, 1024, 256], P(('wide', 'narrow')), may hold values from -120 to 120
- prior_second: bfloat16 [32, 1024, 256], P(('wide', 'narrow')), may hold values from -120 to 120
- raw_lengths: int32 [32], P(('wide', 'narrow')), may hold values from 256 to 921, as said below
- speed_index: int32 [32], P(('wide', 'narrow')), may hold values from 0 to 2
- conv_one: bfloat16 [13, 256, 384], P(None, 'wide', 'narrow'), may hold values from -0.109375 to 0.109375
- conv_two: bfloat16 [13, 384, 384], P(None, 'wide', 'narrow'), may hold values from -0.078125 to 0.078125
- conv_three: bfloat16 [13, 384, 384], P(None, 'wide', 'narrow'), may hold values from -0.078125 to 0.078125
- conv_four: bfloat16 [13, 384, 384], P(None, 'wide', 'narrow'), may hold values from -0.078125 to 0.078125
- conv_five: bfloat16 [13, 384, 384], P(None, 'wide', 'narrow'), may hold values from -0.078125 to 0.078125
- dense_input: bfloat16 [1, 256, 384], P(None, 'wide', 'narrow'), may hold values from -0.375 to 0.375
- dense_first: bfloat16 [1, 256, 384], P(None, 'wide', 'narrow'), may hold values from -0.375 to 0.375
- dense_second: bfloat16 [1, 256, 384], P(None, 'wide', 'narrow'), may hold values from -0.375 to 0.375
- norm_scale: bfloat16 [8, 384], P(None, 'narrow'), may hold values from 0.5 to 1.5
- norm_shift: bfloat16 [8, 384], P(None, 'narrow'), may hold values from -2.5 to 2.5
- out_grad: bfloat16 [32, 1024, 384], P(('wide', 'narrow')), may hold values from -6 to 6
Outputs:
- block_output: bfloat16 [32, 1024, 384], P(('wide', 'narrow'))
- input_grad: float32 [32, 1024, 256], P(('wide', 'narrow'))
- first_grad: float32 [32, 1024, 256], P(('wide', 'narrow'))
- second_grad: float32 [32, 1024, 256], P(('wide', 'narrow'))
- conv_one_grad: float32 [13, 256, 384], P(None, 'wide', 'narrow')
- conv_two_grad: float32 [13, 384, 384], P(None, 'wide', 'narrow')
- conv_three_grad: float32 [13, 384, 384], P(None, 'wide', 'narrow')
- conv_four_grad: float32 [13, 384, 384], P(None, 'wide', 'narrow')
- conv_five_grad: float32 [13, 384, 384], P(None, 'wide', 'narrow')
- dense_input_grad: float32 [1, 256, 384], P(None, 'wide', 'narrow')
- dense_first_grad: float32 [1, 256, 384], P(None, 'wide', 'narrow')
- dense_second_grad: float32 [1, 256, 384], P(None, 'wide', 'narrow')
- scale_grad: float32 [8, 384], P(None, 'narrow')
- shift_grad: float32 [8, 384], P(None, 'narrow')
The draws below stay inside these ranges and needn't reach their ends.
Inputs may be any that keep to these rules, and one draw needn't show every extreme that they name: `raw_lengths`: one utterance has exactly 921 frames before perturbation.
All inputs are finite; a program needn't handle non-finite values.
Results may differ from the reference program's by a relative error of at most 0.02.
Values may be sent and summed in bfloat16 or wider, within the bound.
A program may use at most 192 MiB of HBM per device.

```python
import jax
import jax.numpy as jnp
from jax import lax

CH = 384
C_IN = 256
KW = 13
LMAX = 1024
LMIN = 256
UTTS = 32


def field_scales(key, spread, channels):
    key_rows, key_frames, key_chans = jax.random.split(key, 3)
    rank = jnp.arange(UTTS, dtype=jnp.float32) / max(UTTS - 1, 1)
    utter = jnp.exp(rank * jnp.log(3.0)) * jnp.exp(jax.random.uniform(key_rows, (UTTS,), minval=0.0, maxval=jnp.log(spread)))
    frames = jnp.exp(jax.random.uniform(key_frames, (UTTS, LMAX), minval=0.0, maxval=jnp.log(3.0)))
    chans = jnp.exp(jax.random.uniform(key_chans, (channels,), minval=0.0, maxval=jnp.log(10.0)))
    return utter[:, None, None] * frames[:, :, None] * chans[None, None, :] / 16.0


def draw_block_input(key, part):
    key = jax.random.fold_in(key, 11)
    key_vals, key_scales = jax.random.split(key)
    values = jnp.clip(jax.random.normal(key_vals, (UTTS, LMAX, C_IN)), -4.0, 4.0)
    return (values * field_scales(key_scales, 4.0, C_IN)).astype(jnp.bfloat16)


def draw_prior_first(key, part):
    key = jax.random.fold_in(key, 12)
    key_vals, key_scales = jax.random.split(key)
    values = jnp.clip(jax.random.normal(key_vals, (UTTS, LMAX, C_IN)), -4.0, 4.0)
    return (values * field_scales(key_scales, 4.0, C_IN)).astype(jnp.bfloat16)


def draw_prior_second(key, part):
    key = jax.random.fold_in(key, 13)
    key_vals, key_scales = jax.random.split(key)
    values = jnp.clip(jax.random.normal(key_vals, (UTTS, LMAX, C_IN)), -4.0, 4.0)
    return (values * field_scales(key_scales, 4.0, C_IN)).astype(jnp.bfloat16)


def draw_raw_lengths(key, part):
    key = jax.random.fold_in(key, 14)
    key_lengths, key_pick = jax.random.split(key)
    longest = 9 * LMAX // 10
    drawn = jax.random.randint(key_lengths, (UTTS,), LMIN, longest + 1)
    chosen = jax.random.randint(key_pick, (), 0, UTTS)
    return jnp.where(jnp.arange(UTTS) == chosen, longest, drawn).astype(jnp.int32)


def set_ends(values, own_key, least, largest):
    spot = [jax.random.randint(jax.random.fold_in(own_key, axis), (), 0, length) for axis, length in enumerate(values.shape)]
    widest = values.shape.index(max(values.shape))
    next_to = spot[:widest] + [(spot[widest] + 1) % values.shape[widest]] + spot[widest + 1:]
    return values.at[tuple(spot)].set(least).at[tuple(next_to)].set(largest)


def shard_levels(rng, dims, cuts, low, top_value):
    def one(axis_at, blocks):
        heights = jax.random.uniform(jax.random.fold_in(jax.random.fold_in(rng, 6), axis_at), (blocks,), jnp.float32, low / len(cuts), top_value / len(cuts))
        return jnp.repeat(jnp.exp(heights), dims[axis_at] // blocks).reshape((-1,) + (1,) * (len(dims) - axis_at - 1))

    gain = one(*cuts[0])
    for cut in cuts[1:]:
        gain = gain * one(*cut)
    return gain


def bell_draw(own_key, dims, width, limit, cuts=(), kind=jnp.bfloat16):
    array = jax.random.normal(own_key, dims, jnp.float32) * width
    if len(cuts) > 0:
        array = shard_levels(own_key, dims, cuts, -0.22, 0.18) * array
    return jnp.clip(array, min=-limit, max=limit).astype(kind)


def setup_inputs(seed: int = 0) -> dict:
    key_list = jax.random.split(jax.random.key(seed), 17)
    return {
        "block_input": draw_block_input(jax.random.fold_in(key_list[16], 71), 0),
        "prior_first": draw_prior_first(jax.random.fold_in(key_list[16], 71), 0),
        "prior_second": draw_prior_second(jax.random.fold_in(key_list[16], 71), 0),
        "raw_lengths": draw_raw_lengths(jax.random.fold_in(key_list[16], 71), 0),
        "speed_index": set_ends(jax.random.randint(key_list[4], (UTTS,), 0, 3), jax.random.fold_in(key_list[4], 1), 0, 2).astype(jnp.int32),
        "conv_one": bell_draw(key_list[5], (KW, C_IN, CH), (KW * C_IN) ** -0.5, 0.109375, ((1, 8), (2, 4))),
        "conv_two": bell_draw(key_list[6], (KW, CH, CH), (KW * CH) ** -0.5, 0.078125, ((1, 8), (2, 4))),
        "conv_three": bell_draw(key_list[7], (KW, CH, CH), (KW * CH) ** -0.5, 0.078125, ((1, 8), (2, 4))),
        "conv_four": bell_draw(key_list[8], (KW, CH, CH), (KW * CH) ** -0.5, 0.078125, ((1, 8), (2, 4))),
        "conv_five": bell_draw(key_list[9], (KW, CH, CH), (KW * CH) ** -0.5, 0.078125, ((1, 8), (2, 4))),
        "dense_input": bell_draw(key_list[10], (1, C_IN, CH), C_IN ** -0.5, 0.375, ((1, 8), (2, 4))),
        "dense_first": bell_draw(key_list[11], (1, C_IN, CH), C_IN ** -0.5, 0.375, ((1, 8), (2, 4))),
        "dense_second": bell_draw(key_list[12], (1, C_IN, CH), C_IN ** -0.5, 0.375, ((1, 8), (2, 4))),
        "norm_scale": jnp.clip(1.0 + 0.1 * jax.random.normal(key_list[13], (8, CH), jnp.float32), 0.5, 1.5).astype(jnp.bfloat16),
        "norm_shift": bell_draw(key_list[14], (8, CH), 0.5, 2.5, ((1, 4),)),
        "out_grad": bell_draw(key_list[15], (UTTS, LMAX, CH), 1.0, 6.0, ((0, 32),)),
    }


EPS = 1e-05

@jax.custom_vjp
def low(v):
    return lax.optimization_barrier(v.astype(jnp.bfloat16)).astype(jnp.float32)

@jax.custom_vjp
def low_back(v):
    return v

def low_keep(v):
    return (low(v), None)

def low_pass(kept, grad):
    return (grad,)

def back_keep(v):
    return (v, None)

def back_low(kept, grad):
    return (low(grad),)
low.defvjp(low_keep, low_pass)
low_back.defvjp(back_keep, back_low)

def conv_apply(field, weight):
    extent = weight.shape[0]
    half = extent // 2
    length = field.shape[1]
    padded = jnp.pad(field, ((0, 0), (half, half), (0, 0)))
    total = jnp.einsum('utc,cd->utd', padded[:, 0:length], weight[0], precision=lax.Precision.HIGHEST)
    for offset in range(1, extent):
        total = total + jnp.einsum('utc,cd->utd', padded[:, offset:offset + length], weight[offset], precision=lax.Precision.HIGHEST)
    return total

def batch_norm(field, mask, count, scale, shift):
    mean = lax.optimization_barrier(jnp.sum(field * mask, axis=(0, 1))) / count
    centered = field - mean
    spread = lax.optimization_barrier(jnp.sum(mask * centered * centered, axis=(0, 1))) / count
    return scale * centered * lax.rsqrt(spread + EPS) + shift

def reference(block_input, prior_first, prior_second, raw_lengths, speed_index, conv_one, conv_two, conv_three, conv_four, conv_five, dense_input, dense_first, dense_second, norm_scale, norm_shift, out_grad):
    lengths = (raw_lengths * 10 // (9 + speed_index)).astype(jnp.int32)
    frames = lax.broadcasted_iota(jnp.int32, (block_input.shape[0], block_input.shape[1]), 1)
    mask = (frames < lengths[:, None]).astype(jnp.float32)[:, :, None]
    count = jnp.sum(lengths).astype(jnp.float32)

    def forward(sources, convs, denses, scale, shift):
        hidden = sources[0] * mask
        act = None
        for index in range(5):
            conv_out = low_back(conv_apply(hidden, convs[index]))
            act = batch_norm(conv_out, mask, count, scale[index], shift[index])
            if index < 4:
                hidden = low(jax.nn.silu(act) * mask)
        total = act
        for place in range(3):
            dense_out = low_back(jnp.einsum('utc,cd->utd', sources[place] * mask, denses[place][0], precision=lax.Precision.HIGHEST))
            total = total + batch_norm(dense_out, mask, count, scale[5 + place], shift[5 + place])
        return jax.nn.silu(total) * mask
    sources = (block_input.astype(jnp.float32), prior_first.astype(jnp.float32), prior_second.astype(jnp.float32))
    convs = (conv_one.astype(jnp.float32), conv_two.astype(jnp.float32), conv_three.astype(jnp.float32), conv_four.astype(jnp.float32), conv_five.astype(jnp.float32))
    denses = (dense_input.astype(jnp.float32), dense_first.astype(jnp.float32), dense_second.astype(jnp.float32))
    scale = norm_scale.astype(jnp.float32)
    shift = norm_shift.astype(jnp.float32)
    result, pullback = jax.vjp(forward, sources, convs, denses, scale, shift)
    source_grads, conv_grads, dense_grads, scale_grad, shift_grad = pullback(out_grad.astype(jnp.float32))
    return (result.astype(jnp.bfloat16), source_grads[0], source_grads[1], source_grads[2], conv_grads[0], conv_grads[1], conv_grads[2], conv_grads[3], conv_grads[4], dense_grads[0], dense_grads[1], dense_grads[2], scale_grad, shift_grad)
```

```python
import functools

import jax
import jax.numpy as jnp
from jax import lax
from jax.experimental import pallas as pl
from jax.experimental.pallas import tpu as pltpu
from jax.sharding import PartitionSpec as P

EPS = 1e-05
BF = jnp.bfloat16
F32 = jnp.float32
WIDE, NARROW = "wide", "narrow"
GRAD = "_grad"
APPLY, OUTER, BACK = "utc,cd->utd", "utc,utd->cd", "utd,cd->utc"
MESH = pl.DeviceIdType.MESH
SEG = 16
NT = (((1,), (1,)), ((), ()))
TN = (((0,), (0,)), ((), ()))


def al(value, to=16):
    return pl.multiple_of(value, to)


def fold(value):
    rows, lanes = value.shape
    return jnp.sum(value.reshape(rows // 8, 8, lanes), axis=0)


def wide_of(column, lanes):
    return jnp.concatenate([column] * (lanes // 128), axis=1)


def sigmoid(value):
    return 1.0 / (1.0 + jnp.exp(-value))


class Kernel:
    def __init__(self, refs, shapes):
        self.__dict__.update(refs)
        self.taps, self.frames, self.chans, self.width = shapes
        self.span = self.frames // SEG
        self.halo = (self.taps // 2) * SEG
        self.w = lax.axis_index(WIDE)
        self.n = lax.axis_index(NARROW)
        self.z, self.x = self.w // 2, self.w % 2
        self.y, self.core = self.n // 2, self.n % 2
        self.sems = 0
        self.sent = []


    def remote(self, src, dst, wide=None, narrow=None):
        index = self.sems
        self.sems += 1
        copy = pltpu.make_async_remote_copy(
            src_ref=src,
            dst_ref=dst,
            send_sem=self.send_sems.at[index],
            recv_sem=self.recv_sems.at[index],
            device_id=(
                self.w if wide is None else wide,
                self.n if narrow is None else narrow,
            ),
            device_id_type=MESH,
        )
        copy.start()
        return copy

    def narrow_peer(self, step):
        return (self.n + step) % 4

    def wide_peer(self, step):
        return (self.w + step) % 8

    def z_peer(self, step):
        return ((self.z + step) % 4) * 2 + self.x

    def x_peer(self):
        return self.z * 2 + (1 - self.x)

    def y_peer(self):
        return (1 - self.y) * 2 + self.core

    def core_peer(self):
        return self.y * 2 + (1 - self.core)

    def barrier(self):
        barrier = pltpu.get_barrier_semaphore()
        for step in range(1, 4):
            pl.semaphore_signal(
                barrier, inc=1, device_id=(self.w, self.narrow_peer(step)), device_id_type=MESH
            )
        for step in range(1, 8):
            pl.semaphore_signal(
                barrier, inc=1, device_id=(self.wide_peer(step), self.n), device_id_type=MESH
            )
        pl.semaphore_wait(barrier, 10)


    def sums_start(self, rows):
        place = self.turn % 2
        self.turn += 1
        self.copies = [
            self.slot_copy(
                self.mine.at[place, 0, pl.ds(0, rows)],
                self.from_narrow.at[place, step - 1, pl.ds(0, rows)],
                place * 10 + step - 1,
                (self.w, self.narrow_peer(step)),
            )
            for step in range(1, 4)
        ]
        return place

    def slot_copy(self, src, dst, index, device):
        copy = pltpu.make_async_remote_copy(
            src_ref=src,
            dst_ref=dst,
            send_sem=self.sum_send.at[index],
            recv_sem=self.sum_recv.at[index],
            device_id=device,
            device_id_type=MESH,
        )
        copy.start()
        return copy

    def sums_finish(self, rows, place, join):
        for copy in self.copies:
            copy.wait_recv()
        parts = [self.mine[place, 0, pl.ds(0, rows)]]
        for step in range(3):
            parts.append(self.from_narrow[place, step, pl.ds(0, rows)])
        self.mine[place, 1, pl.ds(0, rows)] = join(parts)
        second = [
            self.slot_copy(
                self.mine.at[place, 1, pl.ds(0, rows)],
                self.from_wide.at[place, step - 1, pl.ds(0, rows)],
                place * 10 + 2 + step,
                (self.wide_peer(step), self.n),
            )
            for step in range(1, 8)
        ]
        for copy in second:
            copy.wait_recv()
        parts = [self.mine[place, 1, pl.ds(0, rows)]]
        for step in range(7):
            parts.append(self.from_wide[place, step, pl.ds(0, rows)])
        result = join(parts)
        for copy in self.copies + second:
            copy.wait_send()
        return result

    @staticmethod
    def join_moments(fields):
        def join(parts):
            counts = [part[2 * fields : 2 * fields + 1] for part in parts]
            count = functools.reduce(jnp.add, counts)
            mean = (
                functools.reduce(
                    jnp.add, [part[0:fields] * own for part, own in zip(parts, counts)]
                )
                / count
            )
            spread = functools.reduce(
                jnp.add,
                [
                    part[fields : 2 * fields] + own * jnp.square(part[0:fields] - mean)
                    for part, own in zip(parts, counts)
                ],
            )
            rows = parts[0].shape[0] - 2 * fields - 1
            return jnp.concatenate(
                [mean, spread, count, jnp.zeros((rows, count.shape[1]), F32)], axis=0
            )

        return join

    @staticmethod
    def join_sums(parts):
        return functools.reduce(jnp.add, parts)


    def pick(self, owner):
        row = lax.broadcasted_iota(jnp.int32, (128, self.chans), 0)
        lane = lax.broadcasted_iota(jnp.int32, (128, self.chans), 1)
        hit = jnp.logical_and(row < self.width, lane == owner * self.width + row)
        return jnp.where(hit, 1.0, 0.0).astype(BF)

    def quarter(self, group, narrow):
        return al(self.depth[group] * narrow)

    def load_local(self, group):
        local = self.local[group]
        local[...] = jnp.zeros(local.shape, local.dtype)
        at = 0
        for ref in self.pieces[group]:
            rows = ref.shape[1]
            for tap in range(ref.shape[0]):
                local[at : at + rows, 0 : self.width] = ref[tap]
                at += rows

    def gather_steps(self, group):
        full, local, landing = self.full[group], self.local[group], self.landing[group]
        depth = self.depth[group]
        half = depth // 2
        z, x, n = self.z, self.x, self.n
        state = {}

        def rows(narrow, part):
            return pl.ds(al(depth * narrow + part * half), half)

        def exchange():
            state["a2a"] = [
                self.remote(
                    local.at[pl.ds(self.quarter(group, self.narrow_peer(step)), depth)],
                    landing.at[step - 1],
                    narrow=self.narrow_peer(step),
                )
                for step in range(1, 4)
            ]

        def along_z():
            for copy in state["a2a"]:
                copy.wait_recv()
            total = jnp.dot(
                local[pl.ds(self.quarter(group, n), depth), :],
                self.pick(n),
                preferred_element_type=F32,
            )
            for step in range(1, 4):
                total = total + jnp.dot(
                    landing[step - 1], self.pick((n - step) % 4), preferred_element_type=F32
                )
            piece = pl.ds(self.quarter(group, n), depth)
            full[z, x, piece, :] = total.astype(BF)
            state["z"] = [
                self.remote(full.at[z, x, piece], full.at[z, x, piece], wide=self.z_peer(step))
                for step in (1, 3, 2)
            ]

        def hop_one():
            for copy in state["z"]:
                copy.wait_recv()
            first, second = full.at[:, x, rows(n, 0)], full.at[:, x, rows(n, 1)]
            state["one"] = [
                self.remote(first, first, wide=self.x_peer()),
                self.remote(second, second, narrow=self.y_peer()),
            ]

        def hop_two():
            for copy in state["one"]:
                copy.wait_recv()
            first = full.at[:, :, rows(n, 0)]
            own, other = full.at[:, x, rows(n, 1)], full.at[:, x, rows(self.y_peer(), 1)]
            state["two"] = [
                self.remote(first, first, narrow=self.y_peer()),
                self.remote(own, own, wide=self.x_peer()),
                self.remote(other, other, wide=self.x_peer()),
            ]

        def across_cores():
            for copy in state["two"]:
                copy.wait_recv()
            state["core"] = []
            for row in range(2):
                part = full.at[:, :, pl.ds(al(depth * (2 * row + self.core)), depth)]
                state["core"].append(self.remote(part, part, narrow=self.core_peer()))

        def arrived():
            for copy in state["core"]:
                copy.wait_recv()

        def settle():
            for key in ("a2a", "z", "one", "two", "core"):
                for copy in state[key]:
                    copy.wait_send()

        return [exchange, along_z, hop_one, hop_two, across_cores, arrived, settle]


    def add_into(self, target, index, landing, place, count, height):
        def step(item, carry):
            total = target[index(item)].astype(F32) + landing[place(item)].astype(F32)
            target[index(item)] = total.astype(BF)
            return carry

        lax.fori_loop(0, count, step, 0)

    def scatter_steps(self, group):
        full = self.full[group]
        depth = self.depth[group]
        half = depth // 2
        z, x, y, n, core = self.z, self.x, self.y, self.n, self.core
        other = self.y_peer()
        by_core = self.by_core[group % 2]
        two_a = self.two_a[group % 3].at[:, :, pl.ds(0, half)]
        two_b = self.two_b[group % 3].at[:, :, pl.ds(0, half)]
        one_a, one_b, by_z = self.one_a[group], self.one_b[group], self.by_z[group]
        landing, local = self.landing[group], self.local[group]
        state = {}

        def rows(narrow, part):
            return pl.ds(al(depth * narrow + part * half), half)

        def across_cores():
            state["core"] = []
            for row in range(2):
                part = full.at[:, :, pl.ds(al(depth * (2 * row + 1 - core)), depth)]
                state["core"].append(
                    self.remote(
                        part, by_core.at[row, :, :, pl.ds(0, depth)], narrow=self.core_peer()
                    )
                )

        def hop_two():
            for copy in state["core"]:
                copy.wait_recv()
            for row in range(2):
                for part in range(2):
                    self.add_into(
                        full,
                        lambda i: (i // 2, i % 2, rows(2 * row + core, part)),
                        by_core,
                        lambda i: (row, i // 2, i % 2, pl.ds(part * half, half)),
                        8,
                        half,
                    )
            state["two"] = [
                self.remote(full.at[:, :, rows(other, 0)], two_a, narrow=other),
                self.remote(full.at[:, 1 - x, rows(n, 1)], two_b.at[0], wide=self.x_peer()),
                self.remote(full.at[:, 1 - x, rows(other, 1)], two_b.at[1], wide=self.x_peer()),
            ]

        def hop_one():
            for copy in state["two"]:
                copy.wait_recv()
            self.add_into(
                full,
                lambda i: (i // 2, i % 2, rows(n, 0)),
                two_a,
                lambda i: (i // 2, i % 2),
                8,
                half,
            )
            for item, narrow in enumerate((n, other)):
                self.add_into(
                    full,
                    lambda i: (i, x, rows(narrow, 1)),
                    two_b,
                    lambda i: (item, i),
                    4,
                    half,
                )
            state["one"] = [
                self.remote(full.at[:, 1 - x, rows(n, 0)], one_a, wide=self.x_peer()),
                self.remote(full.at[:, x, rows(other, 1)], one_b, narrow=other),
            ]

        def along_z():
            for copy in state["one"]:
                copy.wait_recv()
            for part, landed in ((0, one_a), (1, one_b)):
                self.add_into(
                    full, lambda i: (i, x, rows(n, part)), landed, lambda i: i, 4, half
                )
            piece = pl.ds(self.quarter(group, n), depth)
            state["z"] = [
                self.remote(
                    full.at[(z + step) % 4, x, piece], by_z.at[step - 1], wide=self.z_peer(step)
                )
                for step in range(1, 4)
            ]

        def exchange():
            for copy in state["z"]:
                copy.wait_recv()
            piece = pl.ds(self.quarter(group, n), depth)
            total = full[z, x, piece, :].astype(F32)
            for step in range(3):
                total = total + by_z[step].astype(F32)
            total = total.astype(BF)
            state["a2a"] = []
            for step in range(4):
                peer = self.narrow_peer(step)
                part = lax.dot_general(
                    total, self.pick(peer), NT, preferred_element_type=F32
                ).astype(BF)
                if step == 0:
                    local[piece, :] = part
                else:
                    landing[step - 1] = part
                    state["a2a"].append(
                        self.remote(landing.at[step - 1], local.at[piece], narrow=peer)
                    )

        def deliver():
            for copy in state["a2a"]:
                copy.wait_recv()
            at = 0
            for ref in self.grad_outs[group]:
                height = ref.shape[1]
                for tap in range(ref.shape[0]):
                    ref[tap] = local[at : at + height, 0 : self.width].astype(F32)
                    at += height

        def settle():
            for key in ("core", "two", "one", "z", "a2a"):
                for copy in state[key]:
                    copy.wait_send()

        return [across_cores, hop_two, hop_one, along_z, exchange, deliver, settle]


    def weight(self, group, tap, low=0, high=None, lane_low=0, lane_high=None):
        piece = self.piece[group]
        high = piece * 8 if high is None else high
        lanes = slice(lane_low, self.chans if lane_high is None else lane_high)
        full = self.full[group]
        if low == 0 and high == piece * 8:
            return full[:, :, tap * piece : (tap + 1) * piece, lanes].reshape(
                piece * 8, lanes.stop - lanes.start
            )
        parts = []
        while low < high:
            part, begin = low // piece, low % piece
            end = min(piece, begin + high - low)
            parts.append(full[part // 2, part % 2, tap * piece + begin : tap * piece + end, lanes])
            low += end - begin
        return jnp.concatenate(parts, axis=0)

    def conv_forward(self, group, field, out):
        taps, main, pairs = self.taps, 256, self.taps // 2
        block = self.frames // 2

        def chunk(item, carry):
            base = al(item * block)

            def shifted(tap, height=block):
                return field[pl.ds(al(base + SEG * tap), height), :]

            left = jnp.concatenate([shifted(tap) for tap in range(taps)], axis=1)
            right = jnp.concatenate(
                [self.weight(group, tap, 0, None, 0, main) for tap in range(taps)], axis=0
            )
            out[pl.ds(base, block), 0:main] = jnp.dot(left, right, preferred_element_type=F32)
            left = jnp.concatenate([shifted(2 * pair) for pair in range(pairs)], axis=1)
            right = jnp.concatenate(
                [
                    jnp.concatenate(
                        [
                            self.weight(group, 2 * pair, 0, None, main),
                            self.weight(group, 2 * pair + 1, 0, None, main),
                        ],
                        axis=1,
                    )
                    for pair in range(pairs)
                ],
                axis=0,
            )
            self.paired[pl.ds(base, block), :] = jnp.dot(
                left, right, preferred_element_type=F32
            )
            out[pl.ds(base, block), main:] = jnp.dot(
                shifted(taps - 1),
                self.weight(group, taps - 1, 0, None, main),
                preferred_element_type=F32,
            )
            return carry

        lax.fori_loop(0, self.frames // block, chunk, 0)
        rows = self.frames
        left = jnp.concatenate(
            [field[rows + 2 * SEG * pair : rows + 2 * SEG * pair + SEG, :] for pair in range(pairs)],
            axis=1,
        )
        right = jnp.concatenate(
            [self.weight(group, 2 * pair + 1, 0, None, main) for pair in range(pairs)], axis=0
        )
        self.paired[rows : rows + SEG, 128:256] = jnp.dot(
            left, right, preferred_element_type=F32
        )

    def conv_backward(self, group, grad, out):
        taps, main, pairs = self.taps, 256, self.taps // 2
        chans = self.piece[group] * 8
        block = self.frames // 2
        last = taps - 1

        def chunk(item, carry):
            base = al(item * block)

            def shifted(tap):
                return grad[pl.ds(al(base + SEG * (last - tap)), block), :]

            left = jnp.concatenate([shifted(tap) for tap in range(taps)], axis=1)
            right = jnp.concatenate(
                [self.weight(group, tap, 0, main) for tap in range(taps)], axis=1
            )
            out[pl.ds(base, block), 0:main] = lax.dot_general(
                left, right, NT, preferred_element_type=F32
            )
            if chans > main:
                left = jnp.concatenate([shifted(2 * pair) for pair in range(pairs)], axis=1)
                right = jnp.concatenate(
                    [
                        jnp.concatenate(
                            [
                                self.weight(group, 2 * pair, main, chans),
                                self.weight(group, 2 * pair + 1, main, chans),
                            ],
                            axis=0,
                        )
                        for pair in range(pairs)
                    ],
                    axis=1,
                )
                self.paired[pl.ds(al(base + SEG), block), :] = lax.dot_general(
                    left, right, NT, preferred_element_type=F32
                )
                out[pl.ds(base, block), main:] = lax.dot_general(
                    shifted(last),
                    self.weight(group, last, main, chans),
                    NT,
                    preferred_element_type=F32,
                )
            return carry

        lax.fori_loop(0, self.frames // block, chunk, 0)
        if chans > main:
            left = jnp.concatenate(
                [
                    grad[SEG * (last - 2 * pair) - SEG : SEG * (last - 2 * pair), :]
                    for pair in range(pairs)
                ],
                axis=1,
            )
            right = jnp.concatenate(
                [self.weight(group, 2 * pair + 1, main, chans) for pair in range(pairs)], axis=1
            )
            self.paired[0:SEG, 128:256] = lax.dot_general(
                left, right, NT, preferred_element_type=F32
            )

    def weight_grad(self, group, field, grad):
        taps, piece, chans = self.taps, self.piece[group], self.chans
        full = self.full[group]
        middle = field[self.halo : self.halo + self.frames, :]
        tap = 0
        while tap < taps:
            count = min(2, taps - tap)
            right = jnp.concatenate(
                [
                    grad[
                        SEG * (taps - 1 - tap - k) : SEG * (taps - 1 - tap - k) + self.frames, :
                    ]
                    for k in range(count)
                ],
                axis=1,
            )
            got = lax.dot_general(middle, right, TN, preferred_element_type=F32).astype(BF)
            for k in range(count):
                full[:, :, (tap + k) * piece : (tap + k + 1) * piece, :] = got[
                    :, chans * k : chans * (k + 1)
                ].reshape(4, 2, piece, chans)
            tap += count

    def each(self, body, carry=None, height=64):
        def step(item, carry):
            return body(pl.ds(al(item * height, height), height), item, carry)

        return lax.fori_loop(0, self.frames // height, step, carry)

    def mask_of(self, rows, lanes):
        return wide_of(self.valid[rows, :], lanes)

    def fill_halo(self, field):
        span, around = self.span, self.halo // SEG
        lanes = field.shape[1]
        place = lax.broadcasted_iota(jnp.int32, (SEG, lanes), 0)
        for step in range(around):
            source = self.halo + SEG * (span - around + step)
            block = field[source : source + SEG, :].astype(F32)
            block = jnp.where(place == 0, 0.0, pltpu.roll(block, 1, 0))
            field[SEG * step : SEG * (step + 1), :] = block.astype(BF)
            source = self.halo + SEG * step
            block = field[source : source + SEG, :].astype(F32)
            block = jnp.where(place == SEG - 1, 0.0, pltpu.roll(block, SEG - 1, 0))
            target = self.halo + SEG * (span + step)
            field[target : target + SEG, :] = block.astype(BF)

    def permute_in(self, ref, target, offset, masked):
        lanes = ref.shape[2]
        scratch = self.block_output

        def widen(rows, item, carry):
            value = ref[0, rows, :].astype(F32)
            for k in range(lanes // 128):
                scratch[k, rows, :] = value[:, 128 * k : 128 * (k + 1)]
            return carry

        self.each(widen, 0)

        def move(item, carry):
            for k in range(4):
                at = item * 4 + k
                block = self.frames_in(at, scratch)[:, 0:lanes]
                if masked:
                    block = block * self.mask_of(pl.ds(al(at * SEG), SEG), lanes)
                target[pl.ds(al(offset + at * SEG), SEG), :] = block.astype(BF)
            return carry

        lax.fori_loop(0, self.span // 4, move, 0)

    def make_mask(self):
        length = (self.raw_lengths[0] * 10) // (9 + self.speed_index[0])

        def body(rows, item, carry):
            row = lax.broadcasted_iota(jnp.int32, (64, 128), 0) + item * 64
            frame = (row % SEG) * self.span + row // SEG
            self.valid[rows, :] = jnp.where(frame < length, 1.0, 0.0)
            return carry

        self.each(body, 0)
        self.own_count = length.astype(F32)

    def moments_of(self, out, join_pairs):
        chans = self.chans

        def first(rows, item, total):
            value = out[rows, :]
            if join_pairs:
                late = pl.ds(al(item * 64 + SEG), 64)
                tail = value[:, 256:] + self.paired[rows, 0:128] + self.paired[late, 128:256]
                out[rows, 256:] = tail
                value = jnp.concatenate([value[:, :256], tail], axis=1)
            return total + fold(value * self.mask_of(rows, chans))

        total = self.each(first, jnp.zeros((8, chans), F32))
        mean = jnp.sum(total, axis=0, keepdims=True) / self.own_count

        def second(rows, item, total):
            away = out[rows, :] - mean
            return total + fold(away * away * self.mask_of(rows, chans))

        total = self.each(second, jnp.zeros((8, chans), F32))
        return mean, jnp.sum(total, axis=0, keepdims=True)

    def moments_start(self, pairs):
        fields = len(pairs)
        rows = 8 if fields == 1 else 16
        place = self.turn % 2
        parts = [mean for mean, _ in pairs] + [spread for _, spread in pairs]
        parts.append(jnp.full((1, self.chans), 1.0, F32) * self.own_count)
        parts.append(jnp.zeros((rows - len(parts), self.chans), F32))
        self.mine[place, 0, pl.ds(0, rows)] = jnp.concatenate(parts, axis=0)
        return rows, self.sums_start(rows), fields

    def moments_finish(self, started):
        rows, place, fields = started
        joined = self.sums_finish(rows, place, self.join_moments(fields))
        count = joined[2 * fields : 2 * fields + 1]
        means = joined[0:fields]
        spread = joined[fields : 2 * fields] / count
        return means, lax.rsqrt(spread + EPS), count

    def row(self, ref, index):
        return ref[index : index + 1, :]

    def activate(self, layer, out, hidden):
        mean, inv = self.row(self.means, layer), self.row(self.invs, layer)
        gain = self.row(self.scales, layer) * inv
        shift = self.row(self.shifts, layer)

        def body(rows, item, carry):
            act = (out[rows, :] - mean) * gain + shift
            value = act * sigmoid(act) * self.mask_of(rows, self.chans)
            hidden[pl.ds(al(self.halo + item * 64), 64), :] = value.astype(BF)
            return carry

        self.each(body, 0)
        self.fill_halo(hidden)

    def act_grad(self, layer, out, grad, join_pairs):
        mean, inv = self.row(self.means, layer), self.row(self.invs, layer)
        scale, shift = self.row(self.scales, layer), self.row(self.shifts, layer)
        chans = self.chans

        def body(rows, item, sums):
            norm = (out[rows, :] - mean) * inv
            act = norm * scale + shift
            slope = sigmoid(act)
            slope = slope * (1.0 + act * (1.0 - slope))
            value = grad[rows, :]
            if join_pairs:
                late = pl.ds(al(item * 64 + SEG), 64)
                tail = value[:, 256:] + self.paired[late, 0:128] + self.paired[rows, 128:256]
                value = jnp.concatenate([value[:, :256], tail], axis=1)
            value = value * slope * self.mask_of(rows, chans)
            grad[rows, :] = value
            return sums[0] + fold(value), sums[1] + fold(value * norm)

        zero = jnp.zeros((8, chans), F32)
        sums = self.each(body, (zero, zero))
        return [jnp.sum(value, axis=0, keepdims=True) for value in sums]

    def totals_start(self, parts):
        place = self.turn % 2
        pad = jnp.zeros((8 - len(parts), self.chans), F32)
        self.mine[place, 0, pl.ds(0, 8)] = jnp.concatenate(parts + [pad], axis=0)
        return self.sums_start(8)

    def totals_finish(self, place):
        return self.sums_finish(8, place, self.join_sums)

    def norm_grad(self, layer, out, grad, shift_sum, scale_sum, target, offset):
        mean, inv = self.row(self.means, layer), self.row(self.invs, layer)
        gain = self.row(self.scales, layer) * inv
        count = self.count
        flat, tilt = shift_sum / count, scale_sum / count

        def body(rows, item, carry):
            norm = (out[rows, :].astype(F32) - mean) * inv
            mask = self.mask_of(rows, self.chans)
            value = gain * (grad[rows, :] - mask * (flat + norm * tilt))
            target[pl.ds(al(offset + item * 64), 64), :] = value.astype(BF)
            return carry

        self.each(body, 0)

    def frames_in(self, at, ref):
        return jnp.concatenate(
            [ref[part, pl.ds(at, SEG, stride=self.span), :] for part in range(ref.shape[0])],
            axis=1,
        )

    def frames_out(self, at, value, ref):
        for part in range(value.shape[1] // 128):
            ref[part, pl.ds(at, SEG, stride=self.span), :] = value[:, 128 * part : 128 * (part + 1)]

    def last_forward(self):
        chans = self.chans
        ins = (self.outs[4],) + tuple(self.dense_outs)
        means = [self.row(self.means, 4 + k) for k in range(4)]
        invs = [self.row(self.invs, 4 + k) for k in range(4)]
        scales = [self.row(self.scales, 4 + k) for k in range(4)]
        shift = sum(self.row(self.shifts, 4 + k) for k in range(4))

        def body(rows, item, sums):
            norms = [
                (ref[rows, :].astype(F32) - mean) * inv
                for ref, mean, inv in zip(ins, means, invs)
            ]
            total = shift
            for norm, scale in zip(norms, scales):
                total = total + norm * scale
            gate = sigmoid(total)
            mask = self.mask_of(rows, chans)
            value = total * gate * mask
            for k in range(32 // SEG):
                self.frames_out(
                    item * (32 // SEG) + k, value[SEG * k : SEG * (k + 1)], self.block_output
                )
            slope = gate * (1.0 + total * (1.0 - gate))
            value = self.top_grad[rows, :].astype(F32) * mask * slope
            self.grad[rows, :] = value
            return (sums[0] + fold(value),) + tuple(
                old + fold(value * norm) for old, norm in zip(sums[1:], norms)
            )

        sums = self.each(body, (jnp.zeros((8, chans), F32),) * 5, height=32)
        return [jnp.sum(value, axis=0, keepdims=True) for value in sums]

    def dense_weight(self, index):
        piece = self.piece[0]
        at = self.taps * piece + index * piece
        return self.full[0][:, :, at : at + piece, :].reshape(piece * 8, self.chans)

    def dense_forward(self, index, source):
        self.dense_outs[index][...] = jnp.dot(
            source, self.dense_weight(index), preferred_element_type=F32
        ).astype(self.dense_outs[index].dtype)

    def write_frames(self, source, target, add=False):
        lanes = source.shape[1]

        def move(item, carry):
            for k in range(4):
                at = item * 4 + k
                rows = pl.ds(al(at * SEG), SEG)
                value = source[rows, :] * self.mask_of(rows, lanes)
                if add:
                    value = value + self.frames_in(at, target)
                self.frames_out(at, value, target)
            return carry

        lax.fori_loop(0, self.span // 4, move, 0)

    def dense_backward(self, index, source, place, grad_index, totals):
        self.norm_grad(
            5 + index,
            self.dense_outs[index],
            self.grad,
            totals[0:1],
            totals[2 + index : 3 + index],
            self.dense_grad,
            0,
        )
        grad = self.dense_grad[...]
        got = lax.dot_general(grad, self.dense_weight(index), NT, preferred_element_type=F32)
        spare = self.outs[4]
        spare[:, 0 : got.shape[1]] = got
        self.write_frames(
            spare.at[:, pl.ds(0, got.shape[1])],
            (self.input_grad, self.first_grad, self.second_grad)[index],
        )
        piece = self.piece[0]
        at = self.taps * piece + index * piece
        got = lax.dot_general(source, grad, TN, preferred_element_type=F32).astype(BF)
        self.full[0][:, :, at : at + piece, :] = got.reshape(4, 2, piece, self.chans)

    def share_norms(self):
        rows = jnp.concatenate(
            [self.norm_scale[...].astype(F32), self.norm_shift[...].astype(F32)], axis=0
        )
        rows = jnp.concatenate(
            [rows, jnp.zeros((rows.shape[0], 128 - self.width), F32)], axis=1
        ).astype(BF)
        self.norms[0] = jnp.dot(rows, self.pick(self.n), preferred_element_type=F32)
        return [
            self.remote(
                self.norms.at[0], self.norms.at[step], narrow=self.narrow_peer(step)
            )
            for step in range(1, 4)
        ]

    def own_channels(self, rows):
        pick = self.pick(self.n)
        total = None
        for _ in range(3):
            high = rows.astype(BF)
            part = lax.dot_general(high, pick, NT, preferred_element_type=F32)
            total = part if total is None else total + part
            rows = rows - high.astype(F32)
        return total[:, : self.width]

    def run(self):
        self.turn = 0
        gathers = [self.gather_steps(group) for group in range(5)]
        self.barrier()
        norms = self.share_norms()
        for group in range(5):
            self.load_local(group)
            gathers[group][0]()
        self.make_mask()
        gathers[0][1]()
        gathers[1][1]()
        self.permute_in(self.block_input, self.hidden[0], self.halo, True)
        self.fill_halo(self.hidden[0])
        gathers[0][2]()
        gathers[2][1]()
        gathers[1][2]()
        gathers[0][3]()
        gathers[3][1]()
        gathers[4][1]()
        self.permute_in(self.prior_first, self.sources[0], 0, True)
        for copy in norms:
            copy.wait_recv()
        both = self.norms[0] + self.norms[1] + self.norms[2] + self.norms[3]
        self.scales[...] = both[0:8]
        self.shifts[...] = both[8:16]
        gathers[0][4]()
        gathers[2][2]()
        gathers[1][3]()
        self.permute_in(self.prior_second, self.sources[1], 0, True)
        self.permute_in(self.out_grad, self.top_grad, 0, False)
        gathers[0][5]()

        for layer in range(4):
            self.conv_forward(layer, self.hidden[layer], self.outs[layer])
            started = self.moments_start([self.moments_of(self.outs[layer], True)])
            if layer + 1 < 5:
                gathers[layer + 1][4]()
            if layer + 3 < 5:
                gathers[layer + 3][2]()
            if layer + 2 < 5:
                gathers[layer + 2][3]()
            means, inv, count = self.moments_finish(started)
            self.means[layer : layer + 1, :] = means
            self.invs[layer : layer + 1, :] = inv
            self.activate(layer, self.outs[layer], self.hidden[layer + 1])
            if layer == 0:
                self.dense_forward(
                    0, self.hidden[0][self.halo : self.halo + self.frames, :]
                )
                self.dense_forward(1, self.sources[0][...])
                self.dense_forward(2, self.sources[1][...])
                dense = [self.moments_of(ref, False) for ref in self.dense_outs]
            gathers[layer + 1][5]()

        self.conv_forward(4, self.hidden[4], self.outs[4])
        started = self.moments_start([self.moments_of(self.outs[4], True)] + dense)
        for group in range(5):
            gathers[group][6]()
        for copy in norms:
            copy.wait_send()
        means, inv, count = self.moments_finish(started)
        self.means[4:8, :] = means
        self.invs[4:8, :] = inv
        self.count = count

        place = self.totals_start(self.last_forward())
        totals = self.totals_finish(place)
        self.totals = [None] * 4
        self.norm_grad(
            4, self.outs[4], self.grad, totals[0:1], totals[1:2], self.conv_grad, self.halo
        )
        self.fill_halo(self.conv_grad)
        scatters = [self.scatter_steps(group) for group in range(5)]
        for index in range(3):
            source = (
                self.hidden[0][self.halo : self.halo + self.frames, :]
                if index == 0
                else self.sources[index - 1][...]
            )
            self.dense_backward(index, source, None, None, totals)
        sums = [None] * 4
        for layer in (3, 2, 1, 0):
            group = layer + 1
            self.conv_backward(group, self.conv_grad, self.grad)
            place = self.totals_start(
                self.act_grad(layer, self.outs[layer], self.grad, True)
            )
            self.weight_grad(group, self.hidden[group], self.conv_grad)
            scatters[group][0]()
            if group + 1 < 5:
                scatters[group + 1][2]()
            got = self.totals_finish(place)
            sums[layer] = got
            self.norm_grad(
                layer,
                self.outs[layer],
                self.grad,
                got[0:1],
                got[1:2],
                self.conv_grad,
                self.halo,
            )
            self.fill_halo(self.conv_grad)
            scatters[group][1]()
            if group + 1 < 5:
                scatters[group + 1][3]()
            if group + 2 < 5:
                scatters[group + 2][4]()
        self.weight_grad_first(scatters)
        self.scale_grad[...] = self.own_channels(
            jnp.concatenate([got[1:2] for got in sums] + [totals[1:5]], axis=0)
        )
        self.shift_grad[...] = self.own_channels(
            jnp.concatenate([got[0:1] for got in sums] + [totals[0:1]] * 4, axis=0)
        )
        for group in range(5):
            scatters[group][6]()

    def weight_grad_first(self, scatters):
        width = self.hidden[0].shape[1]
        out = self.outs[4].at[:, pl.ds(0, width)]
        self.conv_backward(0, self.conv_grad, out)
        self.weight_grad(0, self.hidden[0], self.conv_grad)
        scatters[0][0]()
        self.write_frames(out, self.input_grad, True)
        scatters[1][2]()
        scatters[0][1]()
        scatters[2][4]()
        scatters[1][3]()
        scatters[0][2]()
        scatters[1][4]()
        scatters[0][3]()
        for group in (4, 3, 2, 1):
            scatters[group][5]()
        scatters[0][4]()
        scatters[0][5]()


INS = (
    "block_input",
    "prior_first",
    "prior_second",
    "raw_lengths",
    "speed_index",
    "conv_one",
    "conv_two",
    "conv_three",
    "conv_four",
    "conv_five",
    "dense_input",
    "dense_first",
    "dense_second",
    "norm_scale",
    "norm_shift",
    "out_grad",
)
OUTS = (
    ("block_output", "input_grad", "first_grad", "second_grad")
    + tuple(name + GRAD for name in INS[5:13])
    + ("scale_grad", "shift_grad")
)
SEMS = 140


def device_program(*args):
    named = dict(zip(INS, args))
    frames, c_in = args[0].shape[1:]
    chans = named["out_grad"].shape[2]
    taps = named["conv_one"].shape[0]
    width = named["conv_one"].shape[2]
    piece = [c_in // 8] + [chans // 8] * 4
    height = [taps * piece[0] + 3 * piece[0]] + [taps * part for part in piece[1:]]
    depth = [-(-rows // (4 * 32)) * 32 for rows in height]
    halo = (taps // 2) * SEG
    tall = frames + 2 * halo

    shape = {
        "block_output": (chans // 128, frames, 128),
        "input_grad": (c_in // 128, frames, 128),
        "first_grad": (c_in // 128, frames, 128),
        "second_grad": (c_in // 128, frames, 128),
        "scale_grad": (8, width),
        "shift_grad": (8, width),
    }
    for name in OUTS:
        if name not in shape:
            shape[name] = named[name[:-5]].shape
    vmem = pltpu.VMEM
    groups = range(5)
    scratch = {
        "full": [vmem((4, 2, 4 * depth[g], chans), BF) for g in groups],
        "local": [vmem((4 * depth[g], 128), BF) for g in groups],
        "landing": [vmem((3, depth[g], 128), BF) for g in groups],
        "by_core": [vmem((2, 4, 2, max(depth), chans), BF) for _ in range(2)],
        "two_a": [vmem((4, 2, max(depth) // 2, chans), BF) for _ in range(3)],
        "two_b": [vmem((2, 4, max(depth) // 2, chans), BF) for _ in range(3)],
        "one_a": [vmem((4, depth[g] // 2, chans), BF) for g in groups],
        "one_b": [vmem((4, depth[g] // 2, chans), BF) for g in groups],
        "by_z": [vmem((3, depth[g], chans), BF) for g in groups],
        "hidden": [vmem((tall, c_in), BF)] + [vmem((tall, chans), BF)] * 4,
        "outs": [vmem((frames, chans), F32)] * 5,
        "dense_outs": [vmem((frames, chans), BF)] * 3,
        "sources": [vmem((frames, c_in), BF)] * 2,
        "top_grad": vmem((frames, chans), BF),
        "conv_grad": vmem((tall, chans), BF),
        "dense_grad": vmem((frames, chans), BF),
        "grad": vmem((frames, chans), F32),
        "paired": vmem((frames + SEG, 256), F32),
        "valid": vmem((frames, 128), F32),
        "mine": vmem((2, 2, 16, chans), F32),
        "from_narrow": vmem((2, 3, 16, chans), F32),
        "from_wide": vmem((2, 7, 16, chans), F32),
        "norms": vmem((4, 16, chans), F32),
        "scales": vmem((8, chans), F32),
        "shifts": vmem((8, chans), F32),
        "means": vmem((8, chans), F32),
        "invs": vmem((8, chans), F32),
        "send_sems": pltpu.SemaphoreType.DMA((SEMS,)),
        "recv_sems": pltpu.SemaphoreType.DMA((SEMS,)),
        "sum_send": pltpu.SemaphoreType.DMA((20,)),
        "sum_recv": pltpu.SemaphoreType.DMA((20,)),
    }
    flat, tree = jax.tree.flatten(scratch, is_leaf=lambda leaf: not isinstance(leaf, (dict, list)))

    def body(*refs):
        refs, rest = dict(zip(INS + OUTS, refs)), refs[len(INS) + len(OUTS) :]
        refs.update(jax.tree.unflatten(tree, rest))
        refs["pieces"] = [
            [refs[name] for name in INS[5:6] + INS[10:13]]
        ] + [[refs[name]] for name in INS[6:10]]
        refs["grad_outs"] = [
            [refs[name + GRAD] for name in INS[5:6] + INS[10:13]]
        ] + [[refs[name + GRAD]] for name in INS[6:10]]
        refs["depth"], refs["piece"] = depth, piece
        kernel = Kernel(refs, (taps, frames, chans, width))
        kernel.run()

    whole = pl.BlockSpec(memory_space=pltpu.VMEM)
    small = pl.BlockSpec(memory_space=pltpu.SMEM)
    outs = pl.pallas_call(
        body,
        out_shape=[jax.ShapeDtypeStruct(shape[name], F32) for name in OUTS],
        in_specs=[small if name in ("raw_lengths", "speed_index") else whole for name in INS],
        out_specs=[whole] * len(OUTS),
        scratch_shapes=flat,
        compiler_params=pltpu.CompilerParams(
            collective_id=0, has_side_effects=True, vmem_limit_bytes=63 * 2**20
        ),
    )(*args)
    outs = [
        out.transpose(1, 0, 2).reshape(1, frames, -1) if place < 4 else out
        for place, out in enumerate(outs)
    ]
    outs[0] = outs[0].astype(BF)
    return tuple(outs)


def silu_slope(value):
    sigmoid = jax.nn.sigmoid(value)
    return sigmoid * (1.0 + value * (1.0 - sigmoid))


def padded_time(field, extent):
    half = extent // 2
    return jnp.pad(field, ((0, 0), (half, half), (0, 0)))


def conv_apply(field, weight):
    extent = weight.shape[0]
    length = field.shape[1]
    padded = padded_time(field, extent)
    total = jnp.einsum(
        APPLY, padded[:, 0:length], weight[0], preferred_element_type=jnp.float32
    )
    for offset in range(1, extent):
        total = total + jnp.einsum(
            APPLY,
            padded[:, offset : offset + length],
            weight[offset],
            preferred_element_type=jnp.float32,
        )
    return total


def conv_grads(field, grad_out, weight):
    extent = weight.shape[0]
    length = field.shape[1]
    padded = padded_time(field, extent)
    padded_grad = padded_time(grad_out, extent)
    taps = []
    grad_in = None
    for offset in range(extent):
        taps.append(
            jnp.einsum(
                OUTER,
                padded[:, offset : offset + length],
                grad_out,
                preferred_element_type=jnp.float32,
            )
        )
        back = extent - 1 - offset
        term = jnp.einsum(
            BACK,
            padded_grad[:, back : back + length],
            weight[offset],
            preferred_element_type=jnp.float32,
        )
        grad_in = term if grad_in is None else grad_in + term
    return (jnp.stack(taps), grad_in)


def moments(fields, mask, local_count):
    firsts = jnp.stack([jnp.sum(field * mask, axis=(0, 1)) for field in fields])
    firsts, count = lax.psum((firsts, local_count), (WIDE, NARROW))
    means = firsts / count
    seconds = jnp.stack(
        [
            jnp.sum(mask * jnp.square(field - means[place]), axis=(0, 1))
            for place, field in enumerate(fields)
        ]
    )
    spread = lax.psum(seconds, (WIDE, NARROW)) / count
    return (means, lax.rsqrt(spread + EPS), count)


def norm_backward(grad_act, norms, scales, inv_std, mask, count):
    shift_part = jnp.sum(grad_act, axis=(0, 1))
    scale_parts = jnp.stack([jnp.sum(grad_act * norm, axis=(0, 1)) for norm in norms])
    shift_sum, scale_sum = lax.psum((shift_part, scale_parts), (WIDE, NARROW))
    grads = []
    for place in range(len(norms)):
        centered = grad_act - mask * (shift_sum + norms[place] * scale_sum[place]) / count
        grads.append((scales[place] * inv_std[place] * centered).astype(jnp.bfloat16))
    return (grads, shift_sum, scale_sum)


def collect(item):
    return lax.all_gather(
        lax.all_gather(item, WIDE, axis=1, tiled=True), NARROW, axis=2, tiled=True
    )


def spread(item):
    item = lax.psum_scatter(item.astype(BF), NARROW, scatter_dimension=2, tiled=True)
    return lax.psum_scatter(item.astype(F32), WIDE, scatter_dimension=1, tiled=True)


def shards(
    block_input,
    prior_first,
    prior_second,
    raw_lengths,
    speed_index,
    conv_one,
    conv_two,
    conv_three,
    conv_four,
    conv_five,
    dense_input,
    dense_first,
    dense_second,
    norm_scale,
    norm_shift,
    out_grad,
):
    utter, length = (block_input.shape[0], block_input.shape[1])
    lengths = raw_lengths * 10 // (9 + speed_index)
    frames = lax.broadcasted_iota(jnp.int32, (utter, length), 1)
    mask = (frames < lengths[:, None]).astype(jnp.float32)[:, :, None]
    mask_low = mask.astype(jnp.bfloat16)
    local_count = jnp.sum(lengths).astype(jnp.float32)
    weights = (
        conv_one,
        conv_two,
        conv_three,
        conv_four,
        conv_five,
        dense_input,
        dense_first,
        dense_second,
    )
    full_weights = [collect(weight) for weight in weights]
    scales = lax.all_gather(norm_scale, NARROW, axis=1, tiled=True).astype(F32)
    shifts = lax.all_gather(norm_shift, NARROW, axis=1, tiled=True).astype(F32)
    sources = (block_input * mask_low, prior_first * mask_low, prior_second * mask_low)
    hidden = sources[0]
    inputs_kept, norms_kept, acts_kept, inv_kept = ([], [], [], [])
    for index in range(4):
        conv_out = conv_apply(hidden, full_weights[index])
        means, inv_std, count = moments((conv_out,), mask, local_count)
        norm = (conv_out - means[0]) * inv_std[0]
        act = scales[index] * norm + shifts[index]
        inputs_kept.append(hidden)
        norms_kept.append(norm)
        acts_kept.append(act)
        inv_kept.append(inv_std[0])
        hidden = (jax.nn.silu(act) * mask).astype(jnp.bfloat16)
    last_out = conv_apply(hidden, full_weights[4])
    dense_outs = tuple(
        (
            jnp.einsum(
                APPLY,
                sources[place],
                full_weights[5 + place][0],
                preferred_element_type=jnp.float32,
            )
            for place in range(3)
        )
    )
    fields = (last_out,) + dense_outs
    means, inv_std, count = moments(fields, mask, local_count)
    last_norms = tuple(((fields[place] - means[place]) * inv_std[place] for place in range(4)))
    total = scales[4] * last_norms[0] + shifts[4]
    for place in range(1, 4):
        total = total + scales[4 + place] * last_norms[place] + shifts[4 + place]
    block_output = (jax.nn.silu(total) * mask).astype(jnp.bfloat16)
    grad_total = out_grad.astype(jnp.float32) * mask * silu_slope(total)
    field_grads, shift_sum, scale_sum = norm_backward(
        grad_total, last_norms, scales[4:8], inv_std, mask, count
    )
    weight_grads = [None] * 8
    scale_rows = [None] * 8
    shift_rows = [None] * 8
    for place in range(4):
        scale_rows[4 + place] = scale_sum[place]
        shift_rows[4 + place] = shift_sum
    weight_grads[4], grad_hidden = conv_grads(hidden, field_grads[0], full_weights[4])
    source_grads = []
    for place in range(3):
        weight_grads[5 + place] = jnp.einsum(
            OUTER,
            sources[place],
            field_grads[1 + place],
            preferred_element_type=jnp.float32,
        )[None]
        source_grads.append(
            jnp.einsum(
                BACK,
                field_grads[1 + place],
                full_weights[5 + place][0],
                preferred_element_type=jnp.float32,
            )
        )
    for index in (3, 2, 1, 0):
        grad_act = grad_hidden * mask * silu_slope(acts_kept[index])
        grads_one, shift_one, scale_one = norm_backward(
            grad_act,
            (norms_kept[index],),
            scales[index : index + 1],
            inv_kept[index][None],
            mask,
            count,
        )
        scale_rows[index] = scale_one[0]
        shift_rows[index] = shift_one
        weight_grads[index], grad_hidden = conv_grads(
            inputs_kept[index], grads_one[0], full_weights[index]
        )
    input_grad = mask * (grad_hidden + source_grads[0])
    first_grad = mask * source_grads[1]
    second_grad = mask * source_grads[2]
    owned = [spread(grad) for grad in weight_grads]
    portion = scales.shape[1] // lax.axis_size(NARROW)
    start = lax.axis_index(NARROW) * portion
    scale_grad = lax.dynamic_slice_in_dim(jnp.stack(scale_rows), start, portion, 1)
    shift_grad = lax.dynamic_slice_in_dim(jnp.stack(shift_rows), start, portion, 1)
    return (
        block_output,
        input_grad,
        first_grad,
        second_grad,
        owned[0],
        owned[1],
        owned[2],
        owned[3],
        owned[4],
        owned[5],
        owned[6],
        owned[7],
        scale_grad,
        shift_grad,
    )


def solution(mesh):
    by_utterance = P((WIDE, NARROW), None, None)
    lengths = P((WIDE, NARROW))
    weight = P(None, WIDE, NARROW)
    norm = P(None, NARROW)
    kernel_fits = (mesh.shape[WIDE], mesh.shape[NARROW]) == (8, 4)
    return jax.shard_map(
        device_program if kernel_fits else shards,
        mesh=mesh,
        in_specs=(by_utterance,) * 3
        + (lengths,) * 2
        + (weight,) * 8
        + (norm,) * 2
        + (by_utterance,),
        out_specs=(by_utterance,) * 4 + (weight,) * 8 + (norm,) * 2,
        check_vma=False,
    )
```

```python
import functools

import jax
import jax.numpy as jnp
from jax import lax
from jax.experimental import pallas as pl
from jax.experimental.pallas import tpu as pltpu
from jax.sharding import PartitionSpec as P

EPS = 1e-05
BF = jnp.bfloat16
F32 = jnp.float32
WIDE, NARROW = "wide", "narrow"
GRAD = "_grad"
APPLY, OUTER, BACK = "utc,cd->utd", "utc,utd->cd", "utd,cd->utc"
MESH = pl.DeviceIdType.MESH
X, Y, Z = "xyz"
SEG = 16
NT = (((1,), (1,)), ((), ()))
TN = (((0,), (0,)), ((), ()))


def al(value, to=16):
    return pl.multiple_of(value, to)


def fold(value):
    rows, lanes = value.shape
    return jnp.sum(value.reshape(rows // 8, 8, lanes), axis=0)


def wide_of(column, lanes):
    return jnp.concatenate([column] * (lanes // 128), axis=1)


def sigmoid(value):
    return 1.0 / (1.0 + jnp.exp(-value))


class Unit:
    def __init__(self, kernel, group, base, depth, parts):
        self.k, self.group, self.base, self.depth = kernel, group, base, depth
        at = 0
        self.parts = []
        for order, size in parts:
            if size:
                self.parts.append((order, at, size))
            at += size
        early = [part for part in self.parts if part[0][0] == Z]
        self.early, self.late = early, [part for part in self.parts if part[0][0] != Z]
        self.head = (early[0][0], 0, sum(part[2] for part in early))
        self.full = kernel.full[group]

    def rows(self, narrow, off, size):
        return pl.ds(al(self.base + self.depth * narrow + off), size)

    def peers(self, axis):
        k = self.k
        if axis == Z:
            return [(k.z_peer(step), k.n) for step in (1, 3, 2)]
        return [(k.x_peer(), k.n)] if axis == X else [(k.w, k.y_peer())]


    def pass_on(self, part, stage):
        k = self.k
        order, off, size = part
        have, axis = order[:stage], order[stage]
        z = slice(None) if Z in have else k.z
        x = slice(None) if X in have else k.x
        copies = []
        for narrow in (k.n, k.y_peer()) if Y in have else (k.n,):
            view = self.full.at[z, x, self.rows(narrow, off, size)]
            copies += [k.remote(view, view, *peer) for peer in self.peers(axis)]
        return copies

    def exchange(self):
        k, depth = self.k, self.depth
        local, self.landing = k.local[self.group], k.landing[k.units.index(self)]
        self.a2a = [
            k.remote(
                local.at[self.rows(k.narrow_peer(step), 0, depth)],
                self.landing.at[step - 1],
                k.w,
                k.narrow_peer(step),
            )
            for step in range(1, 4)
        ]

    def spread(self):
        k = self.k
        k.land(self.a2a)
        mine = self.rows(k.n, 0, self.depth)
        total = jnp.dot(k.local[self.group][mine, :], k.pick(k.n), preferred_element_type=F32)
        for step in range(1, 4):
            total = total + jnp.dot(
                self.landing[step - 1], k.pick((k.n - step) % 4), preferred_element_type=F32
            )
        self.full[k.z, k.x, mine] = total.astype(BF)
        self.first = self.pass_on(self.head, 0)
        self.side = [copy for part in self.late for copy in self.pass_on(part, 0)]

    def second(self):
        self.k.land(self.first)
        self.two = [copy for part in self.early for copy in self.pass_on(part, 1)]

    def third(self):
        self.k.land(self.two)
        self.three = [copy for part in self.early for copy in self.pass_on(part, 2)]

    def side_second(self):
        self.k.land(self.side)
        self.side_two = [copy for part in self.late for copy in self.pass_on(part, 1)]

    def side_third(self):
        self.k.land(self.side_two)
        self.side_three = [copy for part in self.late for copy in self.pass_on(part, 2)]

    def cores(self):
        k = self.k
        k.land(self.three)
        if self.late:
            k.land(self.side_three)
        self.cross = []
        for row in range(2):
            part = self.full.at[:, :, self.rows(2 * row + k.core, 0, self.depth)]
            self.cross.append(k.remote(part, part, k.w, k.core_peer()))

    def arrived(self):
        self.k.land(self.cross)


    def begin_scatter(self, full, base, by_core, buffers):
        self.full, self.base, self.by_core, self.buffers = full, base, by_core, buffers

    def give(self, part, stage):
        k = self.k
        order, off, size = part
        keep, axis = order[:stage], order[stage]
        buffer = self.buffers[order + str(stage)]
        copies = []
        for narrow in (k.n, k.y_peer()) if Y in keep else (k.n,):
            for wide, far in self.peers(axis):
                z = slice(None) if Z in keep else wide // 2
                x = slice(None) if X in keep else wide % 2
                row = far if axis == Y else narrow
                copies.append(
                    k.remote(
                        self.full.at[z, x, self.rows(row, off, size)],
                        buffer.at[len(copies)],
                        wide,
                        far,
                    )
                )
        return copies

    def take(self, part, stage):
        k = self.k
        order, off, size = part
        keep, axis = order[:stage], order[stage]
        buffer = self.buffers[order + str(stage)]
        each = len(self.peers(axis))
        for place, narrow in enumerate((k.n, k.y_peer()) if Y in keep else (k.n,)):
            k.add_into(
                self.full,
                self.rows(narrow, off, size),
                [buffer.at[place * each + index] for index in range(each)],
                None if Z in keep else k.z,
                None if X in keep else k.x,
            )

    def back_cores(self):
        k = self.k
        self.cross = []
        for row in range(2):
            part = self.full.at[:, :, self.rows(2 * row + 1 - k.core, 0, self.depth)]
            self.cross.append(
                k.remote(
                    part, self.by_core.at[row, :, :, pl.ds(0, self.depth)], k.w, k.core_peer()
                )
            )

    def back_third(self):
        k = self.k
        k.land(self.cross)
        for row in range(2):
            landing = self.by_core.at[row, :, :, pl.ds(0, self.depth)]
            k.add_into(
                self.full, self.rows(2 * row + k.core, 0, self.depth), [landing], None, None
            )
        self.three = [copy for part in self.early for copy in self.give(part, 2)]
        self.side_three = [copy for part in self.late for copy in self.give(part, 2)]

    def back_second(self):
        self.k.land(self.three)
        for part in self.early:
            self.take(part, 2)
        self.two = [copy for part in self.early for copy in self.give(part, 1)]

    def back_first(self):
        self.k.land(self.two)
        for part in self.early:
            self.take(part, 1)
        self.first = self.give(self.head, 0)

    def back_side_second(self):
        self.k.land(self.side_three)
        for part in self.late:
            self.take(part, 2)
        self.side_two = [copy for part in self.late for copy in self.give(part, 1)]

    def back_side_first(self):
        self.k.land(self.side_two)
        for part in self.late:
            self.take(part, 1)
        self.side = [copy for part in self.late for copy in self.give(part, 0)]

    def back_exchange(self):
        k = self.k
        k.land(self.first)
        if self.late:
            k.land(self.side)
        sums = []
        for part in [self.head] + self.late:
            order, off, size = part
            total = self.full[k.z, k.x, self.rows(k.n, off, size)].astype(F32)
            buffer = self.buffers[order + str(0)]
            for index in range(len(self.peers(order[0]))):
                total = total + buffer[index].astype(F32)
            sums.append(total.astype(BF))
        total = jnp.concatenate(sums, axis=0) if len(sums) > 1 else sums[0]
        self.a2a = []
        local = k.local[self.group]
        mine = pl.ds(al(self.local_base + self.depth * k.n), self.depth)
        for step in range(4):
            peer = k.narrow_peer(step)
            part = lax.dot_general(total, k.pick(peer), NT, preferred_element_type=F32)
            if step == 0:
                local[mine, :] = part.astype(BF)
            else:
                self.landing[step - 1] = part.astype(BF)
                self.a2a.append(k.remote(self.landing.at[step - 1], local.at[mine], k.w, peer))

    def back_deliver(self):
        k = self.k
        k.land(self.a2a)
        k.deliver(self.group, self.local_base, self.local_base + 4 * self.depth)

class Kernel:
    def __init__(self, refs, shapes):
        self.__dict__.update(refs)
        self.taps, self.frames, self.chans, self.width = shapes
        self.span = self.frames // SEG
        self.halo = (self.taps // 2) * SEG
        self.w = lax.axis_index(WIDE)
        self.n = lax.axis_index(NARROW)
        self.z, self.x = self.w // 2, self.w % 2
        self.y, self.core = self.n // 2, self.n % 2
        self.sems = 0
        self.turn = self.ended = 0
        self.flying, self.landed = {}, []


    def remote(self, src, dst, wide, narrow):
        index = self.semaphore()
        copy = pltpu.make_async_remote_copy(
            src_ref=src,
            dst_ref=dst,
            send_sem=self.send_sems.at[index],
            recv_sem=self.recv_sems.at[index],
            device_id=(wide, narrow),
            device_id_type=MESH,
        )
        copy.start()
        self.flying[id(copy)] = (index, copy)
        return copy

    def semaphore(self):
        for place, (turn, index, copy) in enumerate(self.landed):
            if turn <= self.ended:
                self.landed.pop(place)
                if copy is not None:
                    copy.wait_send()
                return index
        self.sems += 1
        return self.sems - 1

    def land(self, copies):
        for copy in copies:
            copy.wait_recv()
            if id(copy) in self.flying:
                index, copy = self.flying.pop(id(copy))
                self.landed.append([self.turn + 1, index, copy])

    def settle(self):
        for entry in self.landed:
            if entry[2] is not None:
                entry[2].wait_send()
                entry[2] = None

    def narrow_peer(self, step):
        return (self.n + step) % 4

    def wide_peer(self, step):
        return (self.w + step) % 8

    def z_peer(self, step):
        return ((self.z + step) % 4) * 2 + self.x

    def x_peer(self):
        return self.z * 2 + (1 - self.x)

    def y_peer(self):
        return (1 - self.y) * 2 + self.core

    def core_peer(self):
        return self.y * 2 + (1 - self.core)

    def chip_peers(self):
        return [
            ((self.w + step) % 8, (self.n + 2 * far) % 4)
            for step in range(8)
            for far in range(2)
            if step + far > 0
        ]

    def greet(self):
        barrier = pltpu.get_barrier_semaphore()
        greeted = self.chip_peers() + [(self.w, self.narrow_peer(step)) for step in (1, 3)]
        for peer in greeted:
            pl.semaphore_signal(barrier, inc=1, device_id=peer, device_id_type=MESH)
        return barrier, len(greeted)

    def met(self, greeted):
        pl.semaphore_wait(*greeted)


    def pack(self, rows):
        parts = [row[:, at : at + 128] for row in rows for at in range(0, row.shape[1], 128)]
        rest = -len(parts) % 8
        if rest:
            parts.append(jnp.zeros((rest, 128), F32))
        return jnp.concatenate(parts, axis=0)

    def unpack(self, packed, index):
        each = self.chans // 128
        return jnp.concatenate(
            [packed[each * index + k : each * index + k + 1] for k in range(each)], axis=1
        )

    def slot_copy(self, src, dst, index, device):
        copy = pltpu.make_async_remote_copy(
            src_ref=src,
            dst_ref=dst,
            send_sem=self.sum_send.at[index],
            recv_sem=self.sum_recv.at[index],
            device_id=device,
            device_id_type=MESH,
        )
        copy.start()
        return copy

    def sums_start(self, packed):
        place = self.turn % 2
        self.turn += 1
        rows = pl.ds(0, packed.shape[0])
        self.mine[place, 0, rows] = packed
        copy = self.slot_copy(
            self.mine.at[place, 0, rows],
            self.others.at[place, 15, rows],
            place * 16 + 15,
            (self.w, self.core_peer()),
        )
        return packed, place, rows, copy

    def sums_middle(self, started, join):
        packed, place, rows, copy = started
        self.land([copy])
        pair = join([packed, self.others[place, 15, rows]])
        self.mine[place, 1, rows] = pair
        copies = [
            self.slot_copy(
                self.mine.at[place, 1, rows],
                self.others.at[place, index, rows],
                place * 16 + index,
                peer,
            )
            for index, peer in enumerate(self.chip_peers())
        ]
        return pair, place, rows, [copy], copies

    def sums_end(self, started, join):
        pair, place, rows, first, copies = started
        self.land(copies)
        result = join([pair] + [self.others[place, index, rows] for index in range(15)])
        for sent in first + copies:
            sent.wait_send()
        self.ended += 1
        return result

    def join_moments(self, fields):
        each = fields * (self.chans // 128)

        def join(parts):
            counts = [part[2 * each : 2 * each + 1] for part in parts]
            count = functools.reduce(jnp.add, counts)
            mean = (
                functools.reduce(
                    jnp.add, [part[0:each] * own for part, own in zip(parts, counts)]
                )
                / count
            )
            spread = functools.reduce(
                jnp.add,
                [
                    part[each : 2 * each] + own * jnp.square(part[0:each] - mean)
                    for part, own in zip(parts, counts)
                ],
            )
            joined = [mean, spread, count]
            rest = parts[0].shape[0] - 2 * each - 1
            if rest:
                joined.append(jnp.zeros((rest, 128), F32))
            return jnp.concatenate(joined, axis=0)

        return join

    @staticmethod
    def join_sums(parts):
        return functools.reduce(jnp.add, parts)


    def pick(self, owner):
        row = lax.broadcasted_iota(jnp.int32, (128, self.chans), 0)
        lane = lax.broadcasted_iota(jnp.int32, (128, self.chans), 1)
        hit = jnp.logical_and(row < self.width, lane == owner * self.width + row)
        return jnp.where(hit, 1.0, 0.0).astype(BF)

    def load_local(self, group):
        local = self.local[group]
        local[...] = jnp.zeros(local.shape, local.dtype)
        at = 0
        for ref in self.pieces[group]:
            rows = ref.shape[1]
            for tap in range(ref.shape[0]):
                local[at : at + rows, 0 : self.width] = ref[tap]
                at += rows

    def add_into(self, target, rows, landings, zs, xs):
        whole = (zs is None, xs is None)
        count = (4 if whole[0] else 1) * (2 if whole[1] else 1)

        def step(item, carry):
            z = (item // 2 if whole[1] else item) if whole[0] else zs
            x = item % 2 if whole[1] else xs
            inner = ((z,) if whole[0] else ()) + ((x,) if whole[1] else ())
            total = target[z, x, rows].astype(F32)
            for landing in landings:
                total = total + landing[inner + (slice(None),)].astype(F32)
            target[z, x, rows] = total.astype(BF)
            return carry

        if count == 1:
            step(0, 0)
        else:
            lax.fori_loop(0, count, step, 0)

    def deliver(self, group, low, high):
        slot = group % 2 if 0 < group < 5 else 2 + group // 5
        for copy in self.stage_sent.pop((slot, group + 2), []):
            copy.wait()
        local, stage, at = self.local[group], self.grad_stage[slot], 0
        sent = self.stage_sent.setdefault((slot, group), [])
        for index, ref in enumerate(self.grad_outs[group]):
            height = ref.shape[1]
            done = []
            for tap in range(ref.shape[0]):
                if low < at + height <= high:
                    value = local[at : at + height, 0 : self.width]
                    stage[index + tap] = value.astype(F32)
                    done.append(tap)
                at += height
            if done:
                place = self.outgoing
                copy = self.out_copy(
                    stage.at[pl.ds(index + done[0], len(done))],
                    ref.at[pl.ds(done[0], len(done))],
                    8 + place,
                )
                self.outgoing += 1
                sent.append(copy)


    def weight(self, group, tap, low=0, high=None, lane_low=0, lane_high=None):
        piece = self.piece[group]
        high = piece * 8 if high is None else high
        lanes = slice(lane_low, self.chans if lane_high is None else lane_high)
        full = self.full[group]
        if low == 0 and high == piece * 8:
            return full[:, :, tap * piece : (tap + 1) * piece, lanes].reshape(
                piece * 8, lanes.stop - lanes.start
            )
        parts = []
        while low < high:
            part, begin = low // piece, low % piece
            end = min(piece, begin + high - low)
            parts.append(full[part // 2, part % 2, tap * piece + begin : tap * piece + end, lanes])
            low += end - begin
        return jnp.concatenate(parts, axis=0)

    def conv_forward(self, group, field, out):
        taps, main, pairs = self.taps, 256, self.taps // 2
        block = self.frames // 2

        def chunk(item, carry):
            base = al(item * block)

            def shifted(tap):
                return field[pl.ds(al(base + SEG * tap), block), :]

            left = jnp.concatenate([shifted(tap) for tap in range(taps)], axis=1)
            right = jnp.concatenate(
                [self.weight(group, tap, 0, None, 0, main) for tap in range(taps)], axis=0
            )
            out[pl.ds(base, block), 0:main] = jnp.dot(left, right, preferred_element_type=F32)
            left = jnp.concatenate([shifted(2 * pair) for pair in range(pairs)], axis=1)
            right = jnp.concatenate(
                [
                    jnp.concatenate(
                        [
                            self.weight(group, 2 * pair, 0, None, main),
                            self.weight(group, 2 * pair + 1, 0, None, main),
                        ],
                        axis=1,
                    )
                    for pair in range(pairs)
                ],
                axis=0,
            )
            self.paired[pl.ds(base, block), :] = jnp.dot(
                left, right, preferred_element_type=F32
            )
            out[pl.ds(base, block), main:] = jnp.dot(
                shifted(taps - 1),
                self.weight(group, taps - 1, 0, None, main),
                preferred_element_type=F32,
            )
            return carry

        lax.fori_loop(0, self.frames // block, chunk, 0)
        rows = self.frames
        left = jnp.concatenate(
            [field[rows + 2 * SEG * pair : rows + 2 * SEG * pair + SEG, :] for pair in range(pairs)],
            axis=1,
        )
        right = jnp.concatenate(
            [self.weight(group, 2 * pair + 1, 0, None, main) for pair in range(pairs)], axis=0
        )
        self.paired[rows : rows + SEG, 128:256] = jnp.dot(
            left, right, preferred_element_type=F32
        )

    def conv_backward(self, group, grad, out):
        taps, main, pairs = self.taps, 256, self.taps // 2
        chans = self.piece[group] * 8
        block = self.frames // 2
        last = taps - 1

        def chunk(item, carry):
            base = al(item * block)

            def shifted(tap):
                return grad[pl.ds(al(base + SEG * (last - tap)), block), :]

            left = jnp.concatenate([shifted(tap) for tap in range(taps)], axis=1)
            right = jnp.concatenate(
                [self.weight(group, tap, 0, main) for tap in range(taps)], axis=1
            )
            out[pl.ds(base, block), 0:main] = lax.dot_general(
                left, right, NT, preferred_element_type=F32
            )
            if chans > main:
                left = jnp.concatenate([shifted(2 * pair) for pair in range(pairs)], axis=1)
                right = jnp.concatenate(
                    [
                        jnp.concatenate(
                            [
                                self.weight(group, 2 * pair, main, chans),
                                self.weight(group, 2 * pair + 1, main, chans),
                            ],
                            axis=0,
                        )
                        for pair in range(pairs)
                    ],
                    axis=1,
                )
                self.paired[pl.ds(al(base + SEG), block), :] = lax.dot_general(
                    left, right, NT, preferred_element_type=F32
                )
                out[pl.ds(base, block), main:] = lax.dot_general(
                    shifted(last),
                    self.weight(group, last, main, chans),
                    NT,
                    preferred_element_type=F32,
                )
            return carry

        lax.fori_loop(0, self.frames // block, chunk, 0)
        if chans > main:
            left = jnp.concatenate(
                [
                    grad[SEG * (last - 2 * pair) - SEG : SEG * (last - 2 * pair), :]
                    for pair in range(pairs)
                ],
                axis=1,
            )
            right = jnp.concatenate(
                [self.weight(group, 2 * pair + 1, main, chans) for pair in range(pairs)], axis=1
            )
            self.paired[0:SEG, 128:256] = lax.dot_general(
                left, right, NT, preferred_element_type=F32
            )

    def weight_grad(self, group, field, grad, full, tap, taps_end):
        taps, piece, chans = self.taps, self.piece[group], self.chans
        middle = field[self.halo : self.halo + self.frames, :]
        while tap < taps_end:
            count = min(2, taps_end - tap)
            right = jnp.concatenate(
                [
                    grad[
                        SEG * (taps - 1 - tap - k) : SEG * (taps - 1 - tap - k) + self.frames, :
                    ]
                    for k in range(count)
                ],
                axis=1,
            )
            got = lax.dot_general(middle, right, TN, preferred_element_type=F32).astype(BF)
            for k in range(count):
                full[:, :, (tap + k) * piece : (tap + k + 1) * piece, :] = got[
                    :, chans * k : chans * (k + 1)
                ].reshape(4, 2, piece, chans)
            tap += count

    def each(self, body, carry=None, height=64):
        def step(item, carry):
            return body(pl.ds(al(item * height, height), height), item, carry)

        return lax.fori_loop(0, self.frames // height, step, carry)

    def mask_of(self, rows, lanes):
        return wide_of(self.valid[rows, :], lanes)

    def fill_halo(self, field):
        span, around = self.span, self.halo // SEG
        lanes = field.shape[1]
        place = lax.broadcasted_iota(jnp.int32, (SEG, lanes), 0)
        for step in range(around):
            source = self.halo + SEG * (span - around + step)
            block = field[source : source + SEG, :].astype(F32)
            block = jnp.where(place == 0, 0.0, pltpu.roll(block, 1, 0))
            field[SEG * step : SEG * (step + 1), :] = block.astype(BF)
            source = self.halo + SEG * step
            block = field[source : source + SEG, :].astype(F32)
            block = jnp.where(place == SEG - 1, 0.0, pltpu.roll(block, SEG - 1, 0))
            target = self.halo + SEG * (span + step)
            field[target : target + SEG, :] = block.astype(BF)

    def fetch(self):
        self.fetched = []
        homes = (self.dense_grad, self.conv_grad, self.hidden[4], self.hidden[3])
        inputs = (self.block_input, self.prior_first, self.prior_second, self.out_grad)
        for place, (source, home) in enumerate(zip(inputs, homes)):
            target = home.at[pl.ds(0, source.shape[1]), pl.ds(0, source.shape[2])]
            copy = pltpu.make_async_copy(source.at[0], target, self.fetch_sems.at[place])
            copy.start()
            self.fetched.append((target, copy))

    def permute_in(self, ref, target, offset, masked):
        ref, copy = self.fetched[ref]
        copy.wait()
        lanes = ref.shape[1]
        scratch = self.stage

        def widen(rows, item, carry):
            value = ref[rows, :].astype(F32)
            for k in range(lanes // 128):
                scratch[k, rows, :] = value[:, 128 * k : 128 * (k + 1)]
            return carry

        self.each(widen, 0)

        def move(item, carry):
            for k in range(4):
                at = item * 4 + k
                block = self.frames_in(at, scratch)[:, 0:lanes]
                if masked:
                    block = block * self.mask_of(pl.ds(al(at * SEG), SEG), lanes)
                target[pl.ds(al(offset + at * SEG), SEG), :] = block.astype(BF)
            return carry

        lax.fori_loop(0, self.span // 4, move, 0)

    def make_mask(self):
        length = (self.raw_lengths[0] * 10) // (9 + self.speed_index[0])

        def body(rows, item, carry):
            row = lax.broadcasted_iota(jnp.int32, (64, 128), 0) + item * 64
            frame = (row % SEG) * self.span + row // SEG
            self.valid[rows, :] = jnp.where(frame < length, 1.0, 0.0)
            return carry

        self.each(body, 0)
        self.own_count = length.astype(F32)

    def moments_of(self, out, join_pairs):
        chans = self.chans

        def first(rows, item, total):
            value = out[rows, :]
            if join_pairs:
                late = pl.ds(al(item * 64 + SEG), 64)
                tail = value[:, 256:] + self.paired[rows, 0:128] + self.paired[late, 128:256]
                out[rows, 256:] = tail
                value = jnp.concatenate([value[:, :256], tail], axis=1)
            return total + fold(value * self.mask_of(rows, chans))

        total = self.each(first, jnp.zeros((8, chans), F32))
        mean = jnp.sum(total, axis=0, keepdims=True) / self.own_count

        def second(rows, item, total):
            away = out[rows, :] - mean
            return total + fold(away * away * self.mask_of(rows, chans))

        total = self.each(second, jnp.zeros((8, chans), F32))
        return mean, jnp.sum(total, axis=0, keepdims=True)

    def moments_start(self, pairs):
        rows = [mean for mean, _ in pairs] + [spread for _, spread in pairs]
        rows.append(jnp.full((1, 128), 1.0, F32) * self.own_count)
        join = self.join_moments(len(pairs))
        return self.sums_start(self.pack(rows)), len(pairs), join

    def moments_finish(self, started, norms):
        started, fields, join = started
        joined = self.sums_end(started, join)
        each = fields * (self.chans // 128)
        self.count = joined[2 * each : 2 * each + 1, 0:1]
        inv = lax.rsqrt(joined[each : 2 * each] / self.count + EPS)
        for place, norm in enumerate(norms):
            self.means[norm : norm + 1, :] = self.unpack(joined, place)
            self.invs[norm : norm + 1, :] = self.unpack(inv, place)

    def row(self, ref, index):
        return ref[index : index + 1, :]

    def activate(self, layer):
        out, hidden = self.outs[layer], self.hidden[layer + 1]
        mean, inv = self.row(self.means, layer), self.row(self.invs, layer)
        gain = self.row(self.scales, layer) * inv
        shift = self.row(self.shifts, layer)

        def body(rows, item, carry):
            act = (out[rows, :] - mean) * gain + shift
            value = act * sigmoid(act) * self.mask_of(rows, self.chans)
            hidden[pl.ds(al(self.halo + item * 64), 64), :] = value.astype(BF)
            return carry

        self.each(body, 0)
        self.fill_halo(hidden)

    def act_grad(self, layer, out, grad, join_pairs):
        mean, inv = self.row(self.means, layer), self.row(self.invs, layer)
        scale, shift = self.row(self.scales, layer), self.row(self.shifts, layer)
        chans = self.chans

        def body(rows, item, sums):
            norm = (out[rows, :] - mean) * inv
            act = norm * scale + shift
            slope = sigmoid(act)
            slope = slope * (1.0 + act * (1.0 - slope))
            value = grad[rows, :]
            if join_pairs:
                late = pl.ds(al(item * 64 + SEG), 64)
                tail = value[:, 256:] + self.paired[late, 0:128] + self.paired[rows, 128:256]
                value = jnp.concatenate([value[:, :256], tail], axis=1)
            value = value * slope * self.mask_of(rows, chans)
            grad[rows, :] = value
            return sums[0] + fold(value), sums[1] + fold(value * norm)

        zero = jnp.zeros((8, chans), F32)
        sums = self.each(body, (zero, zero))
        return [jnp.sum(value, axis=0, keepdims=True) for value in sums]

    def totals_start(self, parts):
        return self.sums_start(self.pack(parts)), len(parts)

    def totals_middle(self, started):
        started, count = started
        return self.sums_middle(started, self.join_sums), count

    def totals_finish(self, started):
        started, count = started
        joined = self.sums_end(started, self.join_sums)
        return [self.unpack(joined, place) for place in range(count)]

    def norm_grad(self, layer, out, grad, shift_sum, scale_sum, target, offset):
        mean, inv = self.row(self.means, layer), self.row(self.invs, layer)
        gain = self.row(self.scales, layer) * inv
        count = self.count
        flat, tilt = shift_sum / count, scale_sum / count

        def body(rows, item, carry):
            norm = (out[rows, :].astype(F32) - mean) * inv
            mask = self.mask_of(rows, self.chans)
            value = gain * (grad[rows, :] - mask * (flat + norm * tilt))
            target[pl.ds(al(offset + item * 64), 64), :] = value.astype(BF)
            return carry

        self.each(body, 0)

    def frames_in(self, at, ref):
        return jnp.concatenate(
            [ref[part, pl.ds(at, SEG, stride=self.span), :] for part in range(ref.shape[0])],
            axis=1,
        )

    def frames_out(self, at, value, ref):
        for part in range(value.shape[1] // 128):
            ref[part, pl.ds(at, SEG, stride=self.span), :] = value[:, 128 * part : 128 * (part + 1)]

    def last_forward(self):
        chans = self.chans
        ins = (self.outs[4],) + tuple(self.dense_outs)
        means = [self.row(self.means, 4 + k) for k in range(4)]
        invs = [self.row(self.invs, 4 + k) for k in range(4)]
        scales = [self.row(self.scales, 4 + k) for k in range(4)]
        shift = sum(self.row(self.shifts, 4 + k) for k in range(4))

        def body(rows, item, sums):
            norms = [
                (ref[rows, :].astype(F32) - mean) * inv
                for ref, mean, inv in zip(ins, means, invs)
            ]
            total = shift
            for norm, scale in zip(norms, scales):
                total = total + norm * scale
            gate = sigmoid(total)
            mask = self.mask_of(rows, chans)
            value = total * gate * mask
            self.dense_grad[rows, :] = value.astype(BF)
            slope = gate * (1.0 + total * (1.0 - gate))
            value = self.top_grad[rows, :].astype(F32) * mask * slope
            self.grad[rows, :] = value
            return (sums[0] + fold(value),) + tuple(
                old + fold(value * norm) for old, norm in zip(sums[1:], norms)
            )

        sums = self.each(body, (jnp.zeros((8, chans), F32),) * 5, height=32)
        return [jnp.sum(value, axis=0, keepdims=True) for value in sums]

    def dense_weight(self, index):
        piece = self.piece[5]
        at = index * piece
        return self.full[5][:, :, at : at + piece, :].reshape(piece * 8, self.chans)

    def dense_forward(self, index):
        self.dense_outs[index][...] = jnp.dot(
            self.dense_source(index), self.dense_weight(index), preferred_element_type=F32
        ).astype(self.dense_outs[index].dtype)

    def write_frames(self, source, stage, target, place, extra=None):
        lanes = target.shape[1]

        def move(item, carry):
            for k in range(4):
                at = item * 4 + k
                rows = pl.ds(al(at * SEG), SEG)
                value = source[rows, 0:lanes]
                if extra is not None:
                    value = value + extra[rows, 0:lanes]
                self.frames_out(at, value * self.mask_of(rows, lanes), stage)
            return carry

        lax.fori_loop(0, self.span // 4, move, 0)
        sent = [
            self.out_copy(
                stage.at[part], target.at[:, pl.ds(128 * part, 128)], place + part
            )
            for part in range(lanes // 128)
        ]
        if extra is not None:
            self.input_sent = sent
        else:
            self.frames_sent += sent

    def out_copy(self, source, target, place):
        copy = pltpu.make_async_copy(source, target, self.out_sems.at[place])
        copy.start()
        return copy

    def write_output(self):
        def move(item, carry):
            for k in range(4):
                at = item * 4 + k
                value = self.dense_grad[pl.ds(al(at * SEG), SEG), :]
                self.frames_out(at, value.astype(F32), self.stage)
            return carry

        lax.fori_loop(0, self.span // 4, move, 0)

        def body(rows, item, carry):
            value = jnp.concatenate([self.stage[part, rows, :] for part in range(3)], axis=1)
            self.dense_grad[rows, :] = value.astype(BF)
            return carry

        self.each(body, 0)
        self.output_sent = self.out_copy(self.dense_grad, self.block_output, 0)

    def dense_field_grad(self, index):
        totals = self.totals[4]
        self.norm_grad(
            5 + index,
            self.dense_outs[index],
            self.grad,
            totals[0],
            totals[2 + index],
            self.dense_grad,
            0,
        )
        return self.dense_grad[...]

    def dense_source(self, index):
        if index == 0:
            return self.hidden[0][self.halo : self.halo + self.frames, :]
        return self.sources[index - 1][...]

    def dense_weight_grad(self, index):
        if self.output_sent is not None:
            self.output_sent.wait()
            self.output_sent = None
        grad = self.dense_field_grad(index)
        piece = self.piece[5]
        at = 4 * (self.units[0].depth + self.units[1].depth) + index * piece
        got = lax.dot_general(
            self.dense_source(index), grad, TN, preferred_element_type=F32
        ).astype(BF)
        self.homes[0][:, :, at : at + piece, :] = got.reshape(4, 2, piece, self.chans)

    def dense_source_grad(self, index):
        grad = self.dense_field_grad(index)
        got = lax.dot_general(grad, self.dense_weight(index), NT, preferred_element_type=F32)
        spare = self.outs[3]
        spare[:, 0 : got.shape[1]] = got
        if index == 1:
            self.write_frames(spare, self.second_stage, self.first_grad, 3)
        if index == 2:
            for copy in self.input_sent:
                copy.wait()
            self.write_frames(spare, self.stage, self.second_grad, 34)

    def share_norms(self):
        rows = jnp.concatenate(
            [self.norm_scale[...].astype(F32), self.norm_shift[...].astype(F32)], axis=0
        )
        rows = jnp.concatenate(
            [rows, jnp.zeros((rows.shape[0], 128 - self.width), F32)], axis=1
        ).astype(BF)
        self.norms[0] = jnp.dot(rows, self.pick(self.n), preferred_element_type=F32)

    def send_norms(self):
        return [
            self.remote(
                self.norms.at[0], self.norms.at[step], self.w, self.narrow_peer(step)
            )
            for step in range(1, 4)
        ]

    def own_channels(self, rows):
        pick = self.pick(self.n)
        total = None
        for _ in range(3):
            high = rows.astype(BF)
            part = lax.dot_general(high, pick, NT, preferred_element_type=F32)
            total = part if total is None else total + part
            rows = rows - high.astype(F32)
        return total[:, : self.width]

    def take_norms(self):
        self.land(self.norm_copies)
        both = self.norms[0] + self.norms[1] + self.norms[2] + self.norms[3]
        self.scales[...] = both[0:8]
        self.shifts[...] = both[8:16]

    def conv(self, layer):
        self.conv_forward(layer, self.hidden[layer], self.outs[layer])

    def moments_begin(self, layer):
        pairs, self.joined = [self.moments_of(self.outs[layer], True)], [layer]
        for index in {2: (0, 1), 3: (2,)}.get(layer, ()):
            pairs.append(self.moments_of(self.dense_outs[index], False))
            self.joined.append(5 + index)
        self.started = self.moments_start(pairs)

    def moments_pass(self, layer):
        started, fields, join = self.started
        self.started = self.sums_middle(started, join), fields, join

    def moments_end(self, layer):
        self.moments_finish(self.started, self.joined)

    def dense_all(self):
        for index in range(3):
            self.dense_forward(index)

    def totals_begin(self, layer):
        if layer == 4:
            parts = self.last_forward()
        else:
            parts = self.act_grad(layer, self.outs[layer], self.outs[layer + 1], True)
        self.started = self.totals_start(parts)

    def totals_pass(self, layer):
        self.started = self.totals_middle(self.started)

    def totals_end(self, layer):
        self.totals[layer] = self.totals_finish(self.started)

    def gather_done(self):
        self.settle()
        for place, unit in enumerate(self.units):
            unit.local_base = unit.base
            group, half = unit.group, place % 2
            base = unit.base
            if group == 5:
                base = 4 * (self.units[0].depth + self.units[1].depth)
            core = 4 if group == 5 else 2 * (group % 2) + half
            first = 8 if group == 5 else 6 + half if group == 0 else 2 * (group % 3) + half
            buffers = dict(self.landings[place])
            buffers.update(self.first_landing[first])
            unit.begin_scatter(
                self.homes[group % 5], base, self.by_core[core], buffers
            )

    def field_grad(self, layer):
        got = self.totals[layer]
        grad = self.grad if layer == 4 else self.outs[layer + 1]
        self.norm_grad(
            layer, self.outs[layer], grad, got[0], got[1], self.conv_grad, self.halo
        )
        self.fill_halo(self.conv_grad)

    def taps_grad(self, layer, item):
        height = self.piece[layer]
        first = 4 * self.units[2 * layer].depth
        middle = -(-first // height)
        low, high = (0, middle) if item == 0 else (middle, self.taps)
        self.weight_grad(
            layer, self.hidden[layer], self.conv_grad, self.homes[layer], low, high
        )

    def conv_back(self, layer):
        out = self.outs[max(layer, 1)]
        lanes = self.hidden[layer].shape[1]
        self.conv_backward(layer, self.conv_grad, out.at[:, pl.ds(0, lanes)])

    def write_input_grad(self):
        self.write_frames(self.outs[1], self.stage, self.input_grad, 1, self.outs[3])

    def write_norm_grads(self):
        rows = [self.totals[layer][1] for layer in range(4)] + self.totals[4][1:5]
        self.norm_grads[0] = self.own_channels(jnp.concatenate(rows, axis=0))
        rows = [self.totals[layer][0] for layer in range(4)] + [self.totals[4][0]] * 4
        self.norm_grads[1] = self.own_channels(jnp.concatenate(rows, axis=0))
        self.frames_sent.append(self.out_copy(self.norm_grads.at[0], self.scale_grad, 6))
        self.frames_sent.append(self.out_copy(self.norm_grads.at[1], self.shift_grad, 7))

    def run(self):
        self.totals = [None] * 5
        self.frames_sent, self.stage_sent, self.outgoing = [], {}, 0
        unit = self.units = [Unit(self, *spec) for spec in self.specs]
        self.homes = [self.full[4]] + list(self.full[1:4]) + [self.first_sum]
        self.fetch()
        greeted = self.greet()
        for group in range(6):
            self.load_local(group)
        self.make_mask()
        self.share_norms()
        self.permute_in(0, self.hidden[0], self.halo, True)
        self.fill_halo(self.hidden[0])
        self.met(greeted)
        self.schedule(unit)
        self.settle()
        for copies in list(self.stage_sent.values()) + [self.frames_sent]:
            for copy in copies:
                copy.wait()
        if self.sems != SEMS:
            raise ValueError(self.sems)

    def schedule(self, unit):
        unit[0].exchange()
        self.norm_copies = self.send_norms()
        unit[1].exchange()
        unit[6].exchange()
        unit[3].exchange()
        unit[7].exchange()
        unit[2].exchange()
        unit[4].exchange()
        unit[1].spread()
        self.permute_in(1, self.sources[0], 0, True)
        self.take_norms()
        unit[10].exchange()
        unit[0].spread()
        self.permute_in(3, self.top_grad, 0, False)
        unit[6].spread()
        unit[2].spread()
        unit[3].spread()
        unit[10].spread()
        unit[5].exchange()
        unit[8].exchange()
        unit[2].side_second()
        unit[9].exchange()
        unit[1].second()
        unit[3].side_second()
        unit[5].spread()
        unit[4].spread()
        unit[0].second()
        unit[1].third()
        unit[6].second()
        unit[2].second()
        unit[0].third()
        unit[3].second()
        unit[5].side_second()
        unit[1].cores()
        unit[10].second()
        unit[1].arrived()
        unit[0].cores()
        unit[2].third()
        unit[0].arrived()
        unit[3].third()
        self.conv(0)
        unit[2].side_third()
        self.moments_begin(0)
        self.moments_pass(0)
        unit[4].side_second()
        unit[3].side_third()
        unit[4].second()
        unit[5].second()
        unit[10].third()
        unit[2].cores()
        unit[7].spread()
        unit[5].side_third()
        unit[2].arrived()
        unit[6].side_second()
        self.moments_end(0)
        unit[8].spread()
        unit[3].cores()
        unit[4].third()
        self.activate(0)
        unit[4].side_third()
        unit[5].third()
        unit[3].arrived()
        unit[10].cores()
        self.conv(1)
        unit[10].arrived()
        self.moments_begin(1)
        self.permute_in(2, self.sources[1], 0, True)
        self.moments_pass(1)
        unit[7].second()
        unit[7].side_second()
        self.dense_all()
        unit[9].spread()
        unit[4].cores()
        unit[6].side_third()
        unit[6].third()
        unit[5].cores()
        unit[4].arrived()
        unit[8].second()
        self.moments_end(1)
        self.activate(1)
        unit[9].side_second()
        unit[5].arrived()
        unit[7].third()
        self.conv(2)
        unit[7].side_third()
        self.moments_begin(2)
        unit[6].cores()
        self.moments_pass(2)
        unit[8].side_second()
        unit[9].second()
        unit[8].third()
        unit[7].cores()
        unit[9].side_third()
        unit[6].arrived()
        self.moments_end(2)
        self.activate(2)
        unit[9].third()
        unit[7].arrived()
        self.conv(3)
        unit[8].side_third()
        self.moments_begin(3)
        self.moments_pass(3)
        unit[9].cores()
        unit[8].cores()
        unit[9].arrived()
        self.moments_end(3)
        self.activate(3)
        unit[8].arrived()
        self.conv(4)
        self.moments_begin(4)
        self.moments_pass(4)
        self.moments_end(4)
        self.totals_begin(4)
        self.totals_pass(4)
        self.write_output()
        self.gather_done()
        self.totals_end(4)
        self.field_grad(4)
        self.conv_back(4)
        self.totals_begin(3)
        self.taps_grad(4, 0)
        self.totals_pass(3)
        unit[8].back_cores()
        self.taps_grad(4, 1)
        unit[9].back_cores()
        self.dense_weight_grad(2)
        unit[8].back_third()
        self.dense_weight_grad(0)
        self.totals_end(3)
        self.field_grad(3)
        unit[9].back_third()
        self.conv_back(3)
        self.totals_begin(2)
        self.taps_grad(3, 0)
        unit[6].back_cores()
        self.totals_pass(2)
        unit[9].back_second()
        unit[8].back_side_second()
        unit[8].back_second()
        self.taps_grad(3, 1)
        unit[7].back_cores()
        unit[6].back_third()
        unit[9].back_side_second()
        self.dense_weight_grad(1)
        self.totals_end(2)
        unit[10].back_cores()
        unit[9].back_first()
        self.field_grad(2)
        unit[7].back_third()
        self.conv_back(2)
        unit[8].back_first()
        self.totals_begin(1)
        unit[10].back_third()
        self.taps_grad(2, 0)
        self.totals_pass(1)
        unit[6].back_second()
        unit[4].back_cores()
        unit[6].back_side_second()
        self.taps_grad(2, 1)
        unit[5].back_cores()
        unit[7].back_second()
        unit[7].back_side_second()
        unit[10].back_second()
        self.totals_end(1)
        self.field_grad(1)
        unit[5].back_third()
        unit[4].back_third()
        unit[6].back_first()
        self.conv_back(1)
        unit[10].back_first()
        unit[7].back_first()
        self.totals_begin(0)
        self.taps_grad(1, 0)
        self.totals_pass(0)
        unit[5].back_second()
        unit[2].back_cores()
        unit[5].back_side_second()
        unit[4].back_second()
        self.taps_grad(1, 1)
        unit[2].back_third()
        unit[3].back_cores()
        unit[4].back_side_second()
        unit[5].back_first()
        unit[3].back_third()
        self.totals_end(0)
        self.field_grad(0)
        self.taps_grad(0, 0)
        unit[0].back_cores()
        unit[4].back_first()
        self.taps_grad(0, 1)
        unit[0].back_third()
        unit[2].back_second()
        unit[3].back_second()
        unit[2].back_side_second()
        self.conv_back(0)
        unit[3].back_side_second()
        unit[1].back_cores()
        unit[1].back_third()
        unit[2].back_first()
        unit[0].back_second()
        unit[7].back_side_first()
        unit[4].back_side_first()
        unit[8].back_side_first()
        unit[2].back_side_first()
        unit[5].back_side_first()
        unit[3].back_first()
        self.dense_source_grad(0)
        unit[1].back_second()
        unit[0].back_first()
        unit[2].back_exchange()
        unit[6].back_side_first()
        unit[4].back_exchange()
        unit[8].back_exchange()
        unit[1].back_first()
        unit[10].back_exchange()
        unit[5].back_exchange()
        self.write_input_grad()
        unit[9].back_side_first()
        unit[6].back_exchange()
        unit[3].back_side_first()
        unit[7].back_exchange()
        self.dense_source_grad(1)
        unit[0].back_exchange()
        unit[9].back_exchange()
        unit[3].back_exchange()
        unit[8].back_deliver()
        unit[6].back_deliver()
        unit[1].back_exchange()
        unit[7].back_deliver()
        self.dense_source_grad(2)
        self.write_norm_grads()
        unit[2].back_deliver()
        unit[9].back_deliver()
        unit[3].back_deliver()
        unit[4].back_deliver()
        unit[0].back_deliver()
        unit[10].back_deliver()
        unit[5].back_deliver()
        unit[1].back_deliver()


INS = (
    "block_input",
    "prior_first",
    "prior_second",
    "raw_lengths",
    "speed_index",
    "conv_one",
    "conv_two",
    "conv_three",
    "conv_four",
    "conv_five",
    "dense_input",
    "dense_first",
    "dense_second",
    "norm_scale",
    "norm_shift",
    "out_grad",
)
OUTS = (
    ("block_output", "input_grad", "first_grad", "second_grad")
    + tuple(name + GRAD for name in INS[5:13])
    + ("scale_grad", "shift_grad")
)
FIRST_X, FIRST_Y, SIDE_X, SIDE_Y = Z + X + Y, Z + Y + X, X + Z + Y, Y + Z + X
SEMS = 204


PARTS = (
    ((32, 32, 0, 0), (32, 16, 0, 0)),
    ((32, 16, 16, 16), (16, 32, 16, 16)),
    ((32, 16, 16, 16), (16, 32, 16, 16)),
    ((32, 16, 16, 16), (16, 32, 16, 16)),
    ((32, 16, 16, 16), (16, 32, 16, 16)),
    ((16, 16, 0, 0),),
)


def hop_buffers(spec, stages, vmem, chans):
    _, _, _, parts = spec
    found = {}
    early = sum(size for order, size in parts if order[0] == Z)
    for order, size in parts:
        for stage in stages:
            if not size or (stage == 0 and order == FIRST_Y):
                continue
            keep, axis = order[:stage], order[stage]
            count = (3 if axis == Z else 1) * (2 if Y in keep else 1)
            inner = ((4,) if Z in keep else ()) + ((2,) if X in keep else ())
            rows = early if order == FIRST_X and stage == 0 else size
            found[order + str(stage)] = vmem((count,) + inner + (rows, chans), BF)
    return found


def device_program(*args):
    named = dict(zip(INS, args))
    frames, c_in = args[0].shape[1:]
    chans = named["out_grad"].shape[2]
    taps = named["conv_one"].shape[0]
    width = named["conv_one"].shape[2]
    piece = [c_in // 8] + [chans // 8] * 4
    height = [taps * part for part in piece] + [3 * piece[0]]
    piece.append(piece[0])
    specs = []
    for group, rows in enumerate(height):
        quarter = -(-rows // 64) * 16
        base = 0
        for parts in PARTS[group]:
            parts = tuple(zip((FIRST_X, FIRST_Y, SIDE_X, SIDE_Y), parts))
            depth = sum(size for _, size in parts)
            specs.append((group, base, depth, parts))
            base += 4 * depth
        if base != 4 * quarter:
            raise ValueError((group, base, quarter))
    tops = [max(base + 4 * depth for at, base, depth, _ in specs if at == g) for g in range(6)]
    halo = (taps // 2) * SEG
    tall = frames + 2 * halo

    shape = [args[spot].shape for spot in (15, 0, 1, 2)]
    shape = [(frames, one[2]) for one in shape]
    shape += [args[spot].shape for spot in range(5, 13)] + [(8, width)] * 2
    kinds = [BF] + [F32] * 13
    vmem = pltpu.VMEM
    groups = range(6)
    scratch = {
        "full": [vmem((4, 2, tops[g], chans), BF) for g in groups],
        "local": [vmem((tops[g], 128), BF) for g in groups],
        "landing": [vmem((3, spec[2], 128), BF) for spec in specs],
        "by_core": [vmem((2, 4, 2, spec[2], chans), BF) for spec in specs[2:6]]
        + [vmem((2, 4, 2, specs[10][2], chans), BF)],
        "first_landing": [hop_buffers(specs[at], (2,), vmem, chans) for at in (2, 3, 4, 5, 6, 7, 0, 1, 10)],
        "landings": [hop_buffers(spec, (0, 1), vmem, chans) for spec in specs],
        "first_sum": vmem((4, 2, tops[4], chans), BF),
        "stage": vmem((chans // 128, frames, 128), F32),
        "second_stage": vmem((c_in // 128, frames, 128), F32),
        "grad_stage": [vmem(args[5 + g].shape, F32) for g in (1, 2, 0)]
        + [vmem((3, c_in // 8, width), F32)],
        "norm_grads": vmem((2, 8, width), F32),
        "out_sems": pltpu.SemaphoreType.DMA((40,)),
        "hidden": [vmem((tall, c_in), BF)] + [vmem((tall, chans), BF)] * 4,
        "outs": [vmem((frames, chans), F32)] * 5,
        "dense_outs": [vmem((frames, chans), BF)] * 3,
        "sources": [vmem((frames, c_in), BF)] * 2,
        "top_grad": vmem((frames, chans), BF),
        "conv_grad": vmem((tall, chans), BF),
        "dense_grad": vmem((frames, chans), BF),
        "grad": vmem((frames, chans), F32),
        "paired": vmem((frames + SEG, 256), F32),
        "valid": vmem((frames, 128), F32),
        "mine": vmem((2, 2, 24, 128), F32),
        "others": vmem((2, 16, 24, 128), F32),
        "norms": vmem((4, 16, chans), F32),
        "scales": vmem((8, chans), F32),
        "shifts": vmem((8, chans), F32),
        "means": vmem((8, chans), F32),
        "invs": vmem((8, chans), F32),
        "send_sems": pltpu.SemaphoreType.DMA((SEMS,)),
        "recv_sems": pltpu.SemaphoreType.DMA((SEMS,)),
        "fetch_sems": pltpu.SemaphoreType.DMA((4,)),
        "sum_send": pltpu.SemaphoreType.DMA((32,)),
        "sum_recv": pltpu.SemaphoreType.DMA((32,)),
    }
    flat, tree = jax.tree.flatten(scratch, is_leaf=lambda leaf: not isinstance(leaf, (dict, list)))

    def body(*refs):
        refs, rest = dict(zip(INS + OUTS, refs)), refs[len(INS) + len(OUTS) :]
        refs.update(jax.tree.unflatten(tree, rest))
        refs["pieces"] = [[refs[name]] for name in INS[5:10]] + [
            [refs[name] for name in INS[10:13]]
        ]
        refs["grad_outs"] = [[refs[name + GRAD]] for name in INS[5:10]] + [
            [refs[name + GRAD] for name in INS[10:13]]
        ]
        refs["piece"], refs["specs"] = piece, specs
        kernel = Kernel(refs, (taps, frames, chans, width))
        kernel.run()

    whole = pl.BlockSpec(memory_space=pltpu.VMEM)
    outside = pl.BlockSpec(memory_space=pl.ANY)
    small = pl.BlockSpec(memory_space=pltpu.SMEM)
    outs = pl.pallas_call(
        body,
        out_shape=[jax.ShapeDtypeStruct(dims, kind) for dims, kind in zip(shape, kinds)],
        in_specs=[
            outside if spot in (0, 1, 2, 15) else small if spot in (3, 4) else whole
            for spot in range(16)
        ],
        out_specs=[outside] * 14,
        scratch_shapes=flat,
        compiler_params=pltpu.CompilerParams(
            collective_id=0, has_side_effects=True, vmem_limit_bytes=63 * 2**20
        ),
    )(*args)
    outs = hand_over(outs)
    return tuple(out[None] if place < 4 else out for place, out in enumerate(outs))


def hand_over(arrays):
    count = len(arrays)

    def body(*refs):
        ins, outs, held = refs[:count], refs[count : 2 * count], refs[2 * count : 3 * count]
        sems = refs[-1]
        first = [
            pltpu.make_async_copy(ins[place], held[place], sems.at[place])
            for place in range(count)
        ]
        for copy in first:
            copy.start()
        second = [
            pltpu.make_async_copy(held[place], outs[place], sems.at[count + place])
            for place in range(count)
        ]
        for came, copy in zip(first, second):
            came.wait()
            copy.start()
        for copy in second:
            copy.wait()

    return pl.pallas_call(
        body,
        out_shape=[jax.ShapeDtypeStruct(one.shape, one.dtype) for one in arrays],
        in_specs=[pl.BlockSpec(memory_space=pl.ANY)] * count,
        out_specs=[pl.BlockSpec(memory_space=pl.ANY)] * count,
        scratch_shapes=[pltpu.VMEM(one.shape, one.dtype) for one in arrays]
        + [pltpu.SemaphoreType.DMA((2 * count,))],
        compiler_params=pltpu.CompilerParams(vmem_limit_bytes=62 * 2**20),
    )(*arrays)


def silu_slope(value):
    sigmoid = jax.nn.sigmoid(value)
    return sigmoid * (1.0 + value * (1.0 - sigmoid))


def padded_time(field, extent):
    half = extent // 2
    return jnp.pad(field, ((0, 0), (half, half), (0, 0)))


def conv_apply(field, weight):
    extent = weight.shape[0]
    length = field.shape[1]
    padded = padded_time(field, extent)
    total = jnp.einsum(
        APPLY, padded[:, 0:length], weight[0], preferred_element_type=jnp.float32
    )
    for offset in range(1, extent):
        total = total + jnp.einsum(
            APPLY,
            padded[:, offset : offset + length],
            weight[offset],
            preferred_element_type=jnp.float32,
        )
    return total


def conv_grads(field, grad_out, weight):
    extent = weight.shape[0]
    length = field.shape[1]
    padded = padded_time(field, extent)
    padded_grad = padded_time(grad_out, extent)
    taps = []
    grad_in = None
    for offset in range(extent):
        taps.append(
            jnp.einsum(
                OUTER,
                padded[:, offset : offset + length],
                grad_out,
                preferred_element_type=jnp.float32,
            )
        )
        back = extent - 1 - offset
        term = jnp.einsum(
            BACK,
            padded_grad[:, back : back + length],
            weight[offset],
            preferred_element_type=jnp.float32,
        )
        grad_in = term if grad_in is None else grad_in + term
    return (jnp.stack(taps), grad_in)


def moments(fields, mask, local_count):
    firsts = jnp.stack([jnp.sum(field * mask, axis=(0, 1)) for field in fields])
    firsts, count = lax.psum((firsts, local_count), (WIDE, NARROW))
    means = firsts / count
    seconds = jnp.stack(
        [
            jnp.sum(mask * jnp.square(field - means[place]), axis=(0, 1))
            for place, field in enumerate(fields)
        ]
    )
    spread = lax.psum(seconds, (WIDE, NARROW)) / count
    return (means, lax.rsqrt(spread + EPS), count)


def norm_backward(grad_act, norms, scales, inv_std, mask, count):
    shift_part = jnp.sum(grad_act, axis=(0, 1))
    scale_parts = jnp.stack([jnp.sum(grad_act * norm, axis=(0, 1)) for norm in norms])
    shift_sum, scale_sum = lax.psum((shift_part, scale_parts), (WIDE, NARROW))
    grads = []
    for place in range(len(norms)):
        centered = grad_act - mask * (shift_sum + norms[place] * scale_sum[place]) / count
        grads.append((scales[place] * inv_std[place] * centered).astype(jnp.bfloat16))
    return (grads, shift_sum, scale_sum)


def collect(item):
    return lax.all_gather(
        lax.all_gather(item, WIDE, axis=1, tiled=True), NARROW, axis=2, tiled=True
    )


def spread(item):
    item = lax.psum_scatter(item.astype(BF), NARROW, scatter_dimension=2, tiled=True)
    return lax.psum_scatter(item.astype(F32), WIDE, scatter_dimension=1, tiled=True)


def shards(
    block_input,
    prior_first,
    prior_second,
    raw_lengths,
    speed_index,
    conv_one,
    conv_two,
    conv_three,
    conv_four,
    conv_five,
    dense_input,
    dense_first,
    dense_second,
    norm_scale,
    norm_shift,
    out_grad,
):
    utter, length = (block_input.shape[0], block_input.shape[1])
    lengths = raw_lengths * 10 // (9 + speed_index)
    frames = lax.broadcasted_iota(jnp.int32, (utter, length), 1)
    mask = (frames < lengths[:, None]).astype(jnp.float32)[:, :, None]
    mask_low = mask.astype(jnp.bfloat16)
    local_count = jnp.sum(lengths).astype(jnp.float32)
    weights = (
        conv_one,
        conv_two,
        conv_three,
        conv_four,
        conv_five,
        dense_input,
        dense_first,
        dense_second,
    )
    full_weights = [collect(weight) for weight in weights]
    scales = lax.all_gather(norm_scale, NARROW, axis=1, tiled=True).astype(F32)
    shifts = lax.all_gather(norm_shift, NARROW, axis=1, tiled=True).astype(F32)
    sources = (block_input * mask_low, prior_first * mask_low, prior_second * mask_low)
    hidden = sources[0]
    inputs_kept, norms_kept, acts_kept, inv_kept = ([], [], [], [])
    for index in range(4):
        conv_out = conv_apply(hidden, full_weights[index])
        means, inv_std, count = moments((conv_out,), mask, local_count)
        norm = (conv_out - means[0]) * inv_std[0]
        act = scales[index] * norm + shifts[index]
        inputs_kept.append(hidden)
        norms_kept.append(norm)
        acts_kept.append(act)
        inv_kept.append(inv_std[0])
        hidden = (jax.nn.silu(act) * mask).astype(jnp.bfloat16)
    last_out = conv_apply(hidden, full_weights[4])
    dense_outs = tuple(
        (
            jnp.einsum(
                APPLY,
                sources[place],
                full_weights[5 + place][0],
                preferred_element_type=jnp.float32,
            )
            for place in range(3)
        )
    )
    fields = (last_out,) + dense_outs
    means, inv_std, count = moments(fields, mask, local_count)
    last_norms = tuple(((fields[place] - means[place]) * inv_std[place] for place in range(4)))
    total = scales[4] * last_norms[0] + shifts[4]
    for place in range(1, 4):
        total = total + scales[4 + place] * last_norms[place] + shifts[4 + place]
    block_output = (jax.nn.silu(total) * mask).astype(jnp.bfloat16)
    grad_total = out_grad.astype(jnp.float32) * mask * silu_slope(total)
    field_grads, shift_sum, scale_sum = norm_backward(
        grad_total, last_norms, scales[4:8], inv_std, mask, count
    )
    weight_grads = [None] * 8
    scale_rows = [None] * 8
    shift_rows = [None] * 8
    for place in range(4):
        scale_rows[4 + place] = scale_sum[place]
        shift_rows[4 + place] = shift_sum
    weight_grads[4], grad_hidden = conv_grads(hidden, field_grads[0], full_weights[4])
    source_grads = []
    for place in range(3):
        weight_grads[5 + place] = jnp.einsum(
            OUTER,
            sources[place],
            field_grads[1 + place],
            preferred_element_type=jnp.float32,
        )[None]
        source_grads.append(
            jnp.einsum(
                BACK,
                field_grads[1 + place],
                full_weights[5 + place][0],
                preferred_element_type=jnp.float32,
            )
        )
    for index in (3, 2, 1, 0):
        grad_act = grad_hidden * mask * silu_slope(acts_kept[index])
        grads_one, shift_one, scale_one = norm_backward(
            grad_act,
            (norms_kept[index],),
            scales[index : index + 1],
            inv_kept[index][None],
            mask,
            count,
        )
        scale_rows[index] = scale_one[0]
        shift_rows[index] = shift_one
        weight_grads[index], grad_hidden = conv_grads(
            inputs_kept[index], grads_one[0], full_weights[index]
        )
    input_grad = mask * (grad_hidden + source_grads[0])
    first_grad = mask * source_grads[1]
    second_grad = mask * source_grads[2]
    owned = [spread(grad) for grad in weight_grads]
    portion = scales.shape[1] // lax.axis_size(NARROW)
    start = lax.axis_index(NARROW) * portion
    scale_grad = lax.dynamic_slice_in_dim(jnp.stack(scale_rows), start, portion, 1)
    shift_grad = lax.dynamic_slice_in_dim(jnp.stack(shift_rows), start, portion, 1)
    return (
        block_output,
        input_grad,
        first_grad,
        second_grad,
        owned[0],
        owned[1],
        owned[2],
        owned[3],
        owned[4],
        owned[5],
        owned[6],
        owned[7],
        scale_grad,
        shift_grad,
    )


def solution(mesh):
    by_utterance = P((WIDE, NARROW), None, None)
    lengths = P((WIDE, NARROW))
    weight = P(None, WIDE, NARROW)
    norm = P(None, NARROW)
    kernel_fits = (mesh.shape[WIDE], mesh.shape[NARROW]) == (8, 4)
    return jax.shard_map(
        device_program if kernel_fits else shards,
        mesh=mesh,
        in_specs=(by_utterance,) * 3
        + (lengths,) * 2
        + (weight,) * 8
        + (norm,) * 2
        + (by_utterance,),
        out_specs=(by_utterance,) * 4 + (weight,) * 8 + (norm,) * 2,
        check_vma=False,
    )
```

```python
import functools

import jax
import jax.numpy as jnp
from jax import lax
from jax.experimental import pallas as pl
from jax.experimental.pallas import tpu as pltpu
from jax.sharding import PartitionSpec as P

EPS = 1e-05
BF = jnp.bfloat16
F32 = jnp.float32
WIDE, NARROW = "wide", "narrow"
GRAD = "_grad"
APPLY, OUTER, BACK = "utc,cd->utd", "utc,utd->cd", "utd,cd->utc"
MESH = pl.DeviceIdType.MESH
X, Y, Z = "xyz"
SEG = 16
NT = (((1,), (1,)), ((), ()))
TN = (((0,), (0,)), ((), ()))


def al(value, to=16):
    return pl.multiple_of(value, to)


def fold(value):
    rows, lanes = value.shape
    return jnp.sum(value.reshape(rows // 8, 8, lanes), axis=0)


def wide_of(column, lanes):
    return jnp.concatenate([column] * (lanes // 128), axis=1)


def sigmoid(value):
    return 0.5 * jnp.tanh(0.5 * value) + 0.5


class Unit:
    def __init__(self, kernel, group, base, depth, parts):
        self.k, self.group, self.base, self.depth = kernel, group, base, depth
        at = 0
        self.parts = []
        for order, size in parts:
            if size:
                self.parts.append((order, at, size))
            at += size
        early = [part for part in self.parts if part[0][0] == Z]
        self.early, self.late = early, [part for part in self.parts if part[0][0] != Z]
        self.head = (early[0][0], 0, sum(part[2] for part in early))
        self.full = kernel.full[group]

    def rows(self, narrow, off, size):
        return pl.ds(al(self.base + self.depth * narrow + off), size)

    def peers(self, axis):
        k = self.k
        if axis == Z:
            return [(k.z_peer(step), k.n) for step in (1, 3, 2)]
        return [(k.x_peer(), k.n)] if axis == X else [(k.w, k.y_peer())]


    def pass_on(self, part, stage):
        k = self.k
        order, off, size = part
        have, axis = order[:stage], order[stage]
        z = slice(None) if Z in have else k.z
        x = slice(None) if X in have else k.x
        copies = []
        for narrow in (k.n, k.y_peer()) if Y in have else (k.n,):
            view = self.full.at[z, x, self.rows(narrow, off, size)]
            copies += [k.remote(view, view, *peer) for peer in self.peers(axis)]
        return copies

    def exchange(self):
        k, depth = self.k, self.depth
        local, self.landing = k.local[self.group], k.landing[k.units.index(self)]
        self.a2a = [
            k.remote(
                local.at[self.rows(k.narrow_peer(step), 0, depth)],
                self.landing.at[step - 1],
                k.w,
                k.narrow_peer(step),
            )
            for step in range(1, 4)
        ]

    def spread(self):
        k = self.k
        k.land(self.a2a)
        mine = self.rows(k.n, 0, self.depth)
        total = jnp.dot(k.local[self.group][mine, :], k.pick(k.n), preferred_element_type=F32)
        for step in range(1, 4):
            total = total + jnp.dot(
                self.landing[step - 1], k.pick((k.n - step) % 4), preferred_element_type=F32
            )
        self.full[k.z, k.x, mine] = total.astype(BF)
        self.first = self.pass_on(self.head, 0)
        self.side = [copy for part in self.late for copy in self.pass_on(part, 0)]

    def second(self):
        self.k.land(self.first)
        self.two = [copy for part in self.early for copy in self.pass_on(part, 1)]

    def third(self):
        self.k.land(self.two)
        self.three = [copy for part in self.early for copy in self.pass_on(part, 2)]

    def side_second(self):
        self.k.land(self.side)
        self.side_two = [copy for part in self.late for copy in self.pass_on(part, 1)]

    def side_third(self):
        self.k.land(self.side_two)
        self.side_three = [copy for part in self.late for copy in self.pass_on(part, 2)]

    def cores(self):
        k = self.k
        k.land(self.three)
        if self.late:
            k.land(self.side_three)
        self.cross = []
        for row in range(2):
            part = self.full.at[:, :, self.rows(2 * row + k.core, 0, self.depth)]
            self.cross.append(k.remote(part, part, k.w, k.core_peer()))

    def arrived(self):
        self.k.land(self.cross)


    def begin_scatter(self, full, base, by_core, buffers):
        self.full, self.base, self.by_core, self.buffers = full, base, by_core, buffers

    def give(self, part, stage):
        k = self.k
        order, off, size = part
        keep, axis = order[:stage], order[stage]
        buffer = self.buffers[order + str(stage)]
        copies = []
        for narrow in (k.n, k.y_peer()) if Y in keep else (k.n,):
            for wide, far in self.peers(axis):
                z = slice(None) if Z in keep else wide // 2
                x = slice(None) if X in keep else wide % 2
                row = far if axis == Y else narrow
                copies.append(
                    k.remote(
                        self.full.at[z, x, self.rows(row, off, size)],
                        buffer.at[len(copies)],
                        wide,
                        far,
                    )
                )
        return copies

    def take(self, part, stage):
        k = self.k
        order, off, size = part
        keep, axis = order[:stage], order[stage]
        buffer = self.buffers[order + str(stage)]
        each = len(self.peers(axis))
        for place, narrow in enumerate((k.n, k.y_peer()) if Y in keep else (k.n,)):
            k.add_into(
                self.full,
                self.rows(narrow, off, size),
                [buffer.at[place * each + index] for index in range(each)],
                None if Z in keep else k.z,
                None if X in keep else k.x,
            )

    def back_cores(self):
        k = self.k
        self.cross = []
        for row in range(2):
            part = self.full.at[:, :, self.rows(2 * row + 1 - k.core, 0, self.depth)]
            self.cross.append(
                k.remote(
                    part, self.by_core.at[row, :, :, pl.ds(0, self.depth)], k.w, k.core_peer()
                )
            )

    def back_third(self):
        k = self.k
        k.land(self.cross)
        for row in range(2):
            landing = self.by_core.at[row, :, :, pl.ds(0, self.depth)]
            k.add_into(
                self.full, self.rows(2 * row + k.core, 0, self.depth), [landing], None, None
            )
        self.three = [copy for part in self.early for copy in self.give(part, 2)]
        self.side_three = [copy for part in self.late for copy in self.give(part, 2)]

    def back_second(self):
        self.k.land(self.three)
        for part in self.early:
            self.take(part, 2)
        self.two = [copy for part in self.early for copy in self.give(part, 1)]

    def back_first(self):
        self.k.land(self.two)
        for part in self.early:
            self.take(part, 1)
        self.first = self.give(self.head, 0)

    def back_side_second(self):
        self.k.land(self.side_three)
        for part in self.late:
            self.take(part, 2)
        self.side_two = [copy for part in self.late for copy in self.give(part, 1)]

    def back_side_first(self):
        self.k.land(self.side_two)
        for part in self.late:
            self.take(part, 1)
        self.side = [copy for part in self.late for copy in self.give(part, 0)]

    def back_exchange(self):
        k = self.k
        k.land(self.first)
        if self.late:
            k.land(self.side)
        sums = []
        for part in [self.head] + self.late:
            order, off, size = part
            total = self.full[k.z, k.x, self.rows(k.n, off, size)].astype(F32)
            buffer = self.buffers[order + str(0)]
            for index in range(len(self.peers(order[0]))):
                total = total + buffer[index].astype(F32)
            sums.append(total.astype(BF))
        total = jnp.concatenate(sums, axis=0) if len(sums) > 1 else sums[0]
        self.a2a = []
        local = k.local[self.group]
        mine = pl.ds(al(self.local_base + self.depth * k.n), self.depth)
        for step in range(4):
            peer = k.narrow_peer(step)
            part = lax.dot_general(total, k.pick(peer), NT, preferred_element_type=F32)
            if step == 0:
                local[mine, :] = part.astype(BF)
            else:
                self.landing[step - 1] = part.astype(BF)
                self.a2a.append(k.remote(self.landing.at[step - 1], local.at[mine], k.w, peer))

    def back_deliver(self):
        k = self.k
        k.land(self.a2a)
        k.deliver(self.group, self.local_base, self.local_base + 4 * self.depth)

class Kernel:
    def __init__(self, refs, shapes):
        self.__dict__.update(refs)
        self.taps, self.frames, self.chans, self.width = shapes
        self.span = self.frames // SEG
        self.halo = (self.taps // 2) * SEG
        self.w = lax.axis_index(WIDE)
        self.n = lax.axis_index(NARROW)
        self.z, self.x = self.w // 2, self.w % 2
        self.y, self.core = self.n // 2, self.n % 2
        self.sems = 0
        self.turn = self.ended = 0
        self.flying, self.landed = {}, []


    def remote(self, src, dst, wide, narrow):
        index = self.semaphore()
        copy = pltpu.make_async_remote_copy(
            src_ref=src,
            dst_ref=dst,
            send_sem=self.send_sems.at[index],
            recv_sem=self.recv_sems.at[index],
            device_id=(wide, narrow),
            device_id_type=MESH,
        )
        copy.start()
        self.flying[id(copy)] = (index, copy)
        return copy

    def semaphore(self):
        for place, (turn, index, copy) in enumerate(self.landed):
            if turn <= self.ended:
                self.landed.pop(place)
                if copy is not None:
                    copy.wait_send()
                return index
        self.sems += 1
        return self.sems - 1

    def land(self, copies):
        for copy in copies:
            copy.wait_recv()
            if id(copy) in self.flying:
                index, copy = self.flying.pop(id(copy))
                self.landed.append([self.turn + 1, index, copy])

    def settle(self):
        for entry in self.landed:
            if entry[2] is not None:
                entry[2].wait_send()
                entry[2] = None

    def narrow_peer(self, step):
        return (self.n + step) % 4

    def wide_peer(self, step):
        return (self.w + step) % 8

    def z_peer(self, step):
        return ((self.z + step) % 4) * 2 + self.x

    def x_peer(self):
        return self.z * 2 + (1 - self.x)

    def y_peer(self):
        return (1 - self.y) * 2 + self.core

    def core_peer(self):
        return self.y * 2 + (1 - self.core)

    def chip_peers(self):
        return [
            ((self.w + step) % 8, (self.n + 2 * far) % 4)
            for step in range(8)
            for far in range(2)
            if step + far > 0
        ]

    def greet(self):
        barrier = pltpu.get_barrier_semaphore()
        greeted = self.chip_peers() + [(self.w, self.narrow_peer(step)) for step in (1, 3)]
        for peer in greeted:
            pl.semaphore_signal(barrier, inc=1, device_id=peer, device_id_type=MESH)
        return barrier, len(greeted)

    def met(self, greeted):
        pl.semaphore_wait(*greeted)


    def pack(self, rows):
        parts = [row[:, at : at + 128] for row in rows for at in range(0, row.shape[1], 128)]
        rest = -len(parts) % 8
        if rest:
            parts.append(jnp.zeros((rest, 128), F32))
        return jnp.concatenate(parts, axis=0)

    def unpack(self, packed, index):
        each = self.chans // 128
        return jnp.concatenate(
            [packed[each * index + k : each * index + k + 1] for k in range(each)], axis=1
        )

    def slot_copy(self, src, dst, index, device):
        copy = pltpu.make_async_remote_copy(
            src_ref=src,
            dst_ref=dst,
            send_sem=self.sum_send.at[index],
            recv_sem=self.sum_recv.at[index],
            device_id=device,
            device_id_type=MESH,
        )
        copy.start()
        return copy

    def sums_start(self, packed):
        place = self.turn % 2
        self.turn += 1
        rows = pl.ds(0, packed.shape[0])
        self.mine[place, 0, rows] = packed
        copy = self.slot_copy(
            self.mine.at[place, 0, rows],
            self.others.at[place, 15, rows],
            2 * place,
            (self.w, self.core_peer()),
        )
        return packed, place, rows, copy

    def sums_middle(self, started, join):
        packed, place, rows, copy = started
        self.land([copy])
        pair = join([packed, self.others[place, 15, rows]])
        self.mine[place, 1, rows] = pair
        for index, peer in enumerate(self.chip_peers()):
            self.slot_copy(
                self.mine.at[place, 1, rows],
                self.others.at[place, index, rows],
                2 * place + 1,
                peer,
            )
        return pair, place, rows, copy

    def sums_end(self, started, join):
        pair, place, rows, first = started
        landed = self.others.at[place, pl.ds(0, 15), rows]
        index = 2 * place + 1
        pltpu.make_async_copy(landed, landed, self.sum_recv.at[index]).wait()
        result = join([pair] + [self.others[place, at, rows] for at in range(15)])
        first.wait_send()
        pltpu.make_async_copy(landed, landed, self.sum_send.at[index]).wait()
        self.ended += 1
        return result

    def join_moments(self, fields):
        each = fields * (self.chans // 128)

        def join(parts):
            counts = [part[2 * each : 2 * each + 1] for part in parts]
            count = functools.reduce(jnp.add, counts)
            mean = (
                functools.reduce(
                    jnp.add, [part[0:each] * own for part, own in zip(parts, counts)]
                )
                / count
            )
            spread = functools.reduce(
                jnp.add,
                [
                    part[each : 2 * each] + own * jnp.square(part[0:each] - mean)
                    for part, own in zip(parts, counts)
                ],
            )
            joined = [mean, spread, count]
            rest = parts[0].shape[0] - 2 * each - 1
            if rest:
                joined.append(jnp.zeros((rest, 128), F32))
            return jnp.concatenate(joined, axis=0)

        return join

    @staticmethod
    def join_sums(parts):
        return functools.reduce(jnp.add, parts)


    def pick(self, owner):
        row = lax.broadcasted_iota(jnp.int32, (128, self.chans), 0)
        lane = lax.broadcasted_iota(jnp.int32, (128, self.chans), 1)
        hit = jnp.logical_and(row < self.width, lane == owner * self.width + row)
        return jnp.where(hit, 1.0, 0.0).astype(BF)

    def load_local(self, group):
        local = self.local[group]
        local[...] = jnp.zeros(local.shape, local.dtype)
        at = 0
        for ref in self.pieces[group]:
            rows = ref.shape[1]
            for tap in range(ref.shape[0]):
                local[at : at + rows, 0 : self.width] = ref[tap]
                at += rows

    def add_into(self, target, rows, landings, zs, xs):
        whole = (zs is None, xs is None)
        count = (4 if whole[0] else 1) * (2 if whole[1] else 1)

        def step(item, carry):
            z = (item // 2 if whole[1] else item) if whole[0] else zs
            x = item % 2 if whole[1] else xs
            inner = ((z,) if whole[0] else ()) + ((x,) if whole[1] else ())
            if len(landings) == 1:
                target[z, x, rows] = target[z, x, rows] + landings[0][inner + (slice(None),)]
                return carry
            total = target[z, x, rows].astype(F32)
            for landing in landings:
                total = total + landing[inner + (slice(None),)].astype(F32)
            target[z, x, rows] = total.astype(BF)
            return carry

        if count == 1:
            step(0, 0)
        else:
            lax.fori_loop(0, count, step, 0)

    def deliver(self, group, low, high):
        slot = group % 2 if 0 < group < 5 else 2 + group // 5
        for user in (group - 2, group + 2):
            for copy in self.stage_sent.pop((slot, user), []):
                copy.wait()
        local, stage, at = self.local[group], self.grad_stage[slot], 0
        sent = self.stage_sent.setdefault((slot, group), [])
        for index, ref in enumerate(self.grad_outs[group]):
            height = ref.shape[1]
            done = []
            for tap in range(ref.shape[0]):
                if low < at + height <= high:
                    value = local[at : at + height, 0 : self.width]
                    stage[index + tap] = value.astype(F32)
                    done.append(tap)
                at += height
            if done:
                place = self.outgoing
                copy = self.out_copy(
                    stage.at[pl.ds(index + done[0], len(done))],
                    ref.at[pl.ds(done[0], len(done))],
                    8 + place,
                )
                self.outgoing += 1
                sent.append(copy)


    def weight(self, group, tap, low=0, high=None, lane_low=0, lane_high=None):
        piece = self.piece[group]
        high = piece * 8 if high is None else high
        lanes = slice(lane_low, self.chans if lane_high is None else lane_high)
        full = self.full[group]
        if low == 0 and high == piece * 8:
            return full[:, :, tap * piece : (tap + 1) * piece, lanes].reshape(
                piece * 8, lanes.stop - lanes.start
            )
        parts = []
        while low < high:
            part, begin = low // piece, low % piece
            end = min(piece, begin + high - low)
            parts.append(full[part // 2, part % 2, tap * piece + begin : tap * piece + end, lanes])
            low += end - begin
        return jnp.concatenate(parts, axis=0)

    def conv_forward(self, group, field, out):
        taps, main, pairs = self.taps, 256, self.taps // 2
        block = self.frames // 2
        for base in (0, block):
            tall = block + SEG if base else block

            def shifted(tap, height):
                return field[base + SEG * tap : base + SEG * tap + height, :]

            left = jnp.concatenate([shifted(tap, block) for tap in range(taps)], axis=1)
            right = jnp.concatenate(
                [self.weight(group, tap, 0, None, 0, main) for tap in range(taps)], axis=0
            )
            out[base : base + block, 0:main] = jnp.dot(left, right, preferred_element_type=F32)
            left = jnp.concatenate([shifted(2 * pair, tall) for pair in range(pairs)], axis=1)
            right = jnp.concatenate(
                [
                    jnp.concatenate(
                        [
                            self.weight(group, 2 * pair, 0, None, main),
                            self.weight(group, 2 * pair + 1, 0, None, main),
                        ],
                        axis=1,
                    )
                    for pair in range(pairs)
                ],
                axis=0,
            )
            self.paired[base : base + tall, :] = jnp.dot(
                left, right, preferred_element_type=F32
            )
            out[base : base + block, main:] = jnp.dot(
                shifted(taps - 1, block),
                self.weight(group, taps - 1, 0, None, main),
                preferred_element_type=F32,
            )

    def conv_backward(self, group, grad, out):
        taps, main, pairs = self.taps, 256, self.taps // 2
        chans = self.piece[group] * 8
        block = self.frames // 2
        last = taps - 1
        for base in (0, block):
            early = 0 if base else SEG

            def shifted(tap, early=0):
                at = base + SEG * (last - tap)
                return grad[at - early : at + block, :]

            left = jnp.concatenate([shifted(tap) for tap in range(taps)], axis=1)
            right = jnp.concatenate(
                [self.weight(group, tap, 0, main) for tap in range(taps)], axis=1
            )
            out[base : base + block, 0:main] = lax.dot_general(
                left, right, NT, preferred_element_type=F32
            )
            if chans > main:
                left = jnp.concatenate([shifted(2 * pair, early) for pair in range(pairs)], axis=1)
                right = jnp.concatenate(
                    [
                        jnp.concatenate(
                            [
                                self.weight(group, 2 * pair, main, chans),
                                self.weight(group, 2 * pair + 1, main, chans),
                            ],
                            axis=0,
                        )
                        for pair in range(pairs)
                    ],
                    axis=1,
                )
                self.paired[base + SEG - early : base + SEG + block, :] = lax.dot_general(
                    left, right, NT, preferred_element_type=F32
                )
                out[base : base + block, main:] = lax.dot_general(
                    shifted(last),
                    self.weight(group, last, main, chans),
                    NT,
                    preferred_element_type=F32,
                )

    def weight_grad(self, group, field, grad, full, tap, taps_end):
        taps, piece, chans = self.taps, self.piece[group], self.chans
        middle = field[self.halo : self.halo + self.frames, :]
        while tap < taps_end:
            count = min(2, taps_end - tap)
            right = jnp.concatenate(
                [
                    grad[
                        SEG * (taps - 1 - tap - k) : SEG * (taps - 1 - tap - k) + self.frames, :
                    ]
                    for k in range(count)
                ],
                axis=1,
            )
            got = lax.dot_general(middle, right, TN, preferred_element_type=F32).astype(BF)
            for k in range(count):
                full[:, :, (tap + k) * piece : (tap + k + 1) * piece, :] = got[
                    :, chans * k : chans * (k + 1)
                ].reshape(4, 2, piece, chans)
            tap += count

    def each(self, body, carry=None, height=64):
        def step(item, carry):
            return body(pl.ds(al(item * height, height), height), item, carry)

        return lax.fori_loop(0, self.frames // height, step, carry)

    def mask_of(self, rows, lanes):
        return wide_of(self.valid[rows, :], lanes)

    def fill_halo(self, field):
        span, around = self.span, self.halo // SEG
        lanes = field.shape[1]
        place = lax.broadcasted_iota(jnp.int32, (SEG, lanes), 0)
        for step in range(around):
            source = self.halo + SEG * (span - around + step)
            block = field[source : source + SEG, :].astype(F32)
            block = jnp.where(place == 0, 0.0, pltpu.roll(block, 1, 0))
            field[SEG * step : SEG * (step + 1), :] = block.astype(BF)
            source = self.halo + SEG * step
            block = field[source : source + SEG, :].astype(F32)
            block = jnp.where(place == SEG - 1, 0.0, pltpu.roll(block, SEG - 1, 0))
            target = self.halo + SEG * (span + step)
            field[target : target + SEG, :] = block.astype(BF)

    def fetch(self):
        self.held_copies = [
            pltpu.make_async_copy(source, home, self.fetch_sems.at[4 + place])
            for place, (source, home) in enumerate(zip(self.given, self.held))
        ]
        for copy in self.held_copies:
            copy.start()
        self.fetched = []
        homes = (self.dense_grad, self.conv_grad, self.hidden[4], self.hidden[3])
        inputs = (self.block_input, self.prior_first, self.prior_second, self.out_grad)
        for place, (source, home) in enumerate(zip(inputs, homes)):
            target = home.at[pl.ds(0, source.shape[1]), pl.ds(0, source.shape[2])]
            copy = pltpu.make_async_copy(source.at[0], target, self.fetch_sems.at[place])
            copy.start()
            self.fetched.append((target, copy))

    def permute_in(self, ref, target, offset, masked):
        ref, copy = self.fetched[ref]
        copy.wait()
        lanes = ref.shape[1]
        scratch = self.stage

        def widen(rows, item, carry):
            value = ref[rows, :].astype(F32)
            for k in range(lanes // 128):
                scratch[k, rows, :] = value[:, 128 * k : 128 * (k + 1)]
            return carry

        self.each(widen, 0)

        def move(item, carry):
            for k in range(4):
                at = item * 4 + k
                block = self.frames_in(at, scratch)[:, 0:lanes]
                if masked:
                    block = block * self.mask_of(pl.ds(al(at * SEG), SEG), lanes)
                target[pl.ds(al(offset + at * SEG), SEG), :] = block.astype(BF)
            return carry

        lax.fori_loop(0, self.span // 4, move, 0)

    def make_mask(self):
        length = (self.raw_lengths[0] * 10) // (9 + self.speed_index[0])

        def body(rows, item, carry):
            row = lax.broadcasted_iota(jnp.int32, (64, 128), 0) + item * 64
            frame = (row % SEG) * self.span + row // SEG
            self.valid[rows, :] = jnp.where(frame < length, 1.0, 0.0)
            return carry

        self.each(body, 0)
        self.own_count = length.astype(F32)

    def moments_of(self, out, join_pairs):
        chans = self.chans

        def first(rows, item, total):
            value = out[rows, :]
            if join_pairs:
                late = pl.ds(al(item * 64 + SEG), 64)
                tail = value[:, 256:] + self.paired[rows, 0:128] + self.paired[late, 128:256]
                out[rows, 256:] = tail
                value = jnp.concatenate([value[:, :256], tail], axis=1)
            return total + fold(value * self.mask_of(rows, chans))

        total = self.each(first, jnp.zeros((8, chans), F32))
        mean = jnp.sum(total, axis=0, keepdims=True) / self.own_count

        def second(rows, item, total):
            away = out[rows, :] - mean
            return total + fold(away * away * self.mask_of(rows, chans))

        total = self.each(second, jnp.zeros((8, chans), F32))
        return mean, jnp.sum(total, axis=0, keepdims=True)

    def moments_start(self, pairs):
        rows = [mean for mean, _ in pairs] + [spread for _, spread in pairs]
        rows.append(jnp.full((1, 128), 1.0, F32) * self.own_count)
        join = self.join_moments(len(pairs))
        return self.sums_start(self.pack(rows)), len(pairs), join

    def moments_finish(self, started, norms):
        started, fields, join = started
        joined = self.sums_end(started, join)
        each = fields * (self.chans // 128)
        self.count = joined[2 * each : 2 * each + 1, 0:1]
        inv = lax.rsqrt(joined[each : 2 * each] / self.count + EPS)
        for place, norm in enumerate(norms):
            self.means[norm : norm + 1, :] = self.unpack(joined, place)
            self.invs[norm : norm + 1, :] = self.unpack(inv, place)

    def row(self, ref, index):
        return ref[index : index + 1, :]

    def activate(self, layer):
        out, hidden = self.outs[layer], self.hidden[layer + 1]
        mean, inv = self.row(self.means, layer), self.row(self.invs, layer)
        gain = self.row(self.scales, layer) * inv
        shift = self.row(self.shifts, layer)

        def body(rows, item, carry):
            act = (out[rows, :] - mean) * gain + shift
            value = act * sigmoid(act) * self.mask_of(rows, self.chans)
            hidden[pl.ds(al(self.halo + item * 64), 64), :] = value.astype(BF)
            return carry

        self.each(body, 0)
        self.fill_halo(hidden)

    def act_grad(self, layer, out, grad, join_pairs):
        mean, inv = self.row(self.means, layer), self.row(self.invs, layer)
        scale, shift = self.row(self.scales, layer), self.row(self.shifts, layer)
        chans = self.chans

        def body(rows, item, sums):
            norm = (out[rows, :] - mean) * inv
            act = norm * scale + shift
            slope = sigmoid(act)
            slope = slope * (1.0 + act * (1.0 - slope))
            value = grad[rows, :]
            if join_pairs:
                late = pl.ds(al(item * 64 + SEG), 64)
                tail = value[:, 256:] + self.paired[late, 0:128] + self.paired[rows, 128:256]
                value = jnp.concatenate([value[:, :256], tail], axis=1)
            value = value * slope * self.mask_of(rows, chans)
            grad[rows, :] = value
            return sums[0] + fold(value), sums[1] + fold(value * norm)

        zero = jnp.zeros((8, chans), F32)
        sums = self.each(body, (zero, zero))
        return [jnp.sum(value, axis=0, keepdims=True) for value in sums]

    def totals_start(self, parts):
        return self.sums_start(self.pack(parts)), len(parts)

    def totals_middle(self, started):
        started, count = started
        return self.sums_middle(started, self.join_sums), count

    def totals_finish(self, started):
        started, count = started
        joined = self.sums_end(started, self.join_sums)
        return [self.unpack(joined, place) for place in range(count)]

    def norm_grad(self, layer, out, grad, shift_sum, scale_sum, target, offset):
        mean, inv = self.row(self.means, layer), self.row(self.invs, layer)
        gain = self.row(self.scales, layer) * inv
        count = self.count
        flat, tilt = shift_sum / count, scale_sum / count

        def body(rows, item, carry):
            norm = (out[rows, :].astype(F32) - mean) * inv
            mask = self.mask_of(rows, self.chans)
            value = gain * (grad[rows, :] - mask * (flat + norm * tilt))
            target[pl.ds(al(offset + item * 64), 64), :] = value.astype(BF)
            return carry

        self.each(body, 0)

    def frames_in(self, at, ref):
        return jnp.concatenate(
            [ref[part, pl.ds(at, SEG, stride=self.span), :] for part in range(ref.shape[0])],
            axis=1,
        )

    def frames_out(self, at, value, ref):
        for part in range(value.shape[1] // 128):
            ref[part, pl.ds(at, SEG, stride=self.span), :] = value[:, 128 * part : 128 * (part + 1)]

    def last_forward(self):
        chans = self.chans
        ins = (self.outs[4],) + tuple(self.dense_outs)
        means = [self.row(self.means, 4 + k) for k in range(4)]
        invs = [self.row(self.invs, 4 + k) for k in range(4)]
        scales = [self.row(self.scales, 4 + k) for k in range(4)]
        shift = sum(self.row(self.shifts, 4 + k) for k in range(4))

        def body(rows, item, sums):
            norms = [
                (ref[rows, :].astype(F32) - mean) * inv
                for ref, mean, inv in zip(ins, means, invs)
            ]
            total = shift
            for norm, scale in zip(norms, scales):
                total = total + norm * scale
            gate = sigmoid(total)
            mask = self.mask_of(rows, chans)
            value = total * gate * mask
            self.dense_grad[rows, :] = value.astype(BF)
            slope = gate * (1.0 + total * (1.0 - gate))
            value = self.top_grad[rows, :].astype(F32) * mask * slope
            self.grad[rows, :] = value
            return (sums[0] + fold(value),) + tuple(
                old + fold(value * norm) for old, norm in zip(sums[1:], norms)
            )

        sums = self.each(body, (jnp.zeros((8, chans), F32),) * 5, height=32)
        return [jnp.sum(value, axis=0, keepdims=True) for value in sums]

    def dense_weight(self, index):
        piece = self.piece[5]
        at = index * piece
        return self.full[5][:, :, at : at + piece, :].reshape(piece * 8, self.chans)

    def dense_forward(self, index):
        self.dense_outs[index][...] = jnp.dot(
            self.dense_source(index), self.dense_weight(index), preferred_element_type=F32
        ).astype(self.dense_outs[index].dtype)

    def write_frames(self, source, stage, target, place, extra=None):
        lanes = target.shape[1]

        def move(item, carry):
            for k in range(4):
                at = item * 4 + k
                rows = pl.ds(al(at * SEG), SEG)
                value = source[rows, 0:lanes]
                if extra is not None:
                    value = value + extra[rows, 0:lanes]
                self.frames_out(at, value * self.mask_of(rows, lanes), stage)
            return carry

        lax.fori_loop(0, self.span // 4, move, 0)
        sent = [
            self.out_copy(
                stage.at[part], target.at[:, pl.ds(128 * part, 128)], place + part
            )
            for part in range(lanes // 128)
        ]
        if extra is not None:
            self.input_sent = sent
        else:
            self.frames_sent += sent

    def out_copy(self, source, target, place):
        copy = pltpu.make_async_copy(source, target, self.out_sems.at[place])
        copy.start()
        return copy

    def write_output(self):
        def move(item, carry):
            for k in range(4):
                at = item * 4 + k
                value = self.dense_grad[pl.ds(al(at * SEG), SEG), :]
                self.frames_out(at, value.astype(F32), self.stage)
            return carry

        lax.fori_loop(0, self.span // 4, move, 0)

        def body(rows, item, carry):
            value = jnp.concatenate([self.stage[part, rows, :] for part in range(3)], axis=1)
            self.dense_grad[rows, :] = value.astype(BF)
            return carry

        self.each(body, 0)
        self.output_sent = self.out_copy(self.dense_grad, self.block_output, 0)

    def dense_field_grad(self, index):
        totals = self.totals[4]
        self.norm_grad(
            5 + index,
            self.dense_outs[index],
            self.grad,
            totals[0],
            totals[2 + index],
            self.dense_grad,
            0,
        )
        return self.dense_grad[...]

    def dense_source(self, index):
        if index == 0:
            return self.hidden[0][self.halo : self.halo + self.frames, :]
        return self.sources[index - 1][...]

    def dense_weight_grad(self, index):
        if self.output_sent is not None:
            self.output_sent.wait()
            self.output_sent = None
        grad = self.dense_field_grad(index)
        piece = self.piece[5]
        at = 4 * (self.units[0].depth + self.units[1].depth) + index * piece
        got = lax.dot_general(
            self.dense_source(index), grad, TN, preferred_element_type=F32
        ).astype(BF)
        self.homes[0][:, :, at : at + piece, :] = got.reshape(4, 2, piece, self.chans)

    def dense_source_grad(self, index):
        grad = self.dense_field_grad(index)
        got = lax.dot_general(grad, self.dense_weight(index), NT, preferred_element_type=F32)
        spare = self.outs[3]
        spare[:, 0 : got.shape[1]] = got
        if index == 1:
            self.write_frames(spare, self.second_stage, self.first_grad, 3)
        if index == 2:
            for copy in self.input_sent:
                copy.wait()
            self.write_frames(spare, self.stage, self.second_grad, 26)

    def share_norms(self):
        rows = jnp.concatenate(
            [self.held[8][...].astype(F32), self.held[9][...].astype(F32)], axis=0
        )
        rows = jnp.concatenate(
            [rows, jnp.zeros((rows.shape[0], 128 - self.width), F32)], axis=1
        ).astype(BF)
        self.norms[0] = jnp.dot(rows, self.pick(self.n), preferred_element_type=F32)

    def send_norms(self):
        return [
            self.remote(
                self.norms.at[0], self.norms.at[step], self.w, self.narrow_peer(step)
            )
            for step in range(1, 4)
        ]

    def own_channels(self, rows):
        pick = self.pick(self.n)
        total = None
        for _ in range(3):
            high = rows.astype(BF)
            part = lax.dot_general(high, pick, NT, preferred_element_type=F32)
            total = part if total is None else total + part
            rows = rows - high.astype(F32)
        return total[:, : self.width]

    def take_norms(self):
        self.land(self.norm_copies)
        both = self.norms[0] + self.norms[1] + self.norms[2] + self.norms[3]
        self.scales[...] = both[0:8]
        self.shifts[...] = both[8:16]

    def conv(self, layer):
        self.conv_forward(layer, self.hidden[layer], self.outs[layer])

    def moments_begin(self, layer):
        pairs, self.joined = [self.moments_of(self.outs[layer], True)], [layer]
        for index in {2: (0, 1), 3: (2,)}.get(layer, ()):
            pairs.append(self.moments_of(self.dense_outs[index], False))
            self.joined.append(5 + index)
        self.started = self.moments_start(pairs)

    def moments_pass(self, layer):
        started, fields, join = self.started
        self.started = self.sums_middle(started, join), fields, join

    def moments_end(self, layer):
        self.moments_finish(self.started, self.joined)

    def dense_all(self):
        for index in range(3):
            self.dense_forward(index)

    def totals_begin(self, layer):
        if layer == 4:
            parts = self.last_forward()
        else:
            parts = self.act_grad(layer, self.outs[layer], self.outs[layer + 1], True)
        self.started = self.totals_start(parts)

    def totals_pass(self, layer):
        self.started = self.totals_middle(self.started)

    def totals_end(self, layer):
        self.totals[layer] = self.totals_finish(self.started)

    def gather_done(self):
        self.settle()
        for place, unit in enumerate(self.units):
            unit.local_base = unit.base
            group, half = unit.group, place % 2
            base = unit.base
            if group == 5:
                base = 4 * (self.units[0].depth + self.units[1].depth)
            core = 4 if group == 5 else 2 * (group % 2) + half
            first = 8 if group == 5 else 6 + half if group == 0 else 2 * (group % 3) + half
            buffers = dict(self.landings[place])
            buffers.update(self.first_landing[first])
            unit.begin_scatter(
                self.homes[group % 5], base, self.by_core[core], buffers
            )

    def field_grad(self, layer):
        got = self.totals[layer]
        grad = self.grad if layer == 4 else self.outs[layer + 1]
        self.norm_grad(
            layer, self.outs[layer], grad, got[0], got[1], self.conv_grad, self.halo
        )
        self.fill_halo(self.conv_grad)

    def taps_grad(self, layer, item):
        height = self.piece[layer]
        first = 4 * self.units[2 * layer].depth
        middle = -(-first // height)
        low, high = (0, middle) if item == 0 else (middle, self.taps)
        self.weight_grad(
            layer, self.hidden[layer], self.conv_grad, self.homes[layer], low, high
        )

    def conv_back(self, layer):
        out = self.outs[max(layer, 1)]
        lanes = self.hidden[layer].shape[1]
        self.conv_backward(layer, self.conv_grad, out.at[:, pl.ds(0, lanes)])

    def write_input_grad(self):
        self.write_frames(self.outs[1], self.stage, self.input_grad, 1, self.outs[3])

    def write_norm_grads(self):
        rows = [self.totals[layer][1] for layer in range(4)] + self.totals[4][1:5]
        self.norm_grads[0] = self.own_channels(jnp.concatenate(rows, axis=0))
        rows = [self.totals[layer][0] for layer in range(4)] + [self.totals[4][0]] * 4
        self.norm_grads[1] = self.own_channels(jnp.concatenate(rows, axis=0))
        self.frames_sent.append(self.out_copy(self.norm_grads.at[0], self.scale_grad, 6))
        self.frames_sent.append(self.out_copy(self.norm_grads.at[1], self.shift_grad, 7))

    def run(self):
        self.totals = [None] * 5
        self.frames_sent, self.stage_sent, self.outgoing = [], {}, 0
        unit = self.units = [Unit(self, *spec) for spec in self.specs]
        self.homes = [self.full[4]] + list(self.full[1:4]) + [self.first_sum]
        greeted = self.greet()
        self.fetch()
        for copy in self.held_copies:
            copy.wait()
        for group in range(6):
            self.load_local(group)
        self.met(greeted)
        self.schedule(unit)
        self.settle()
        for copies in list(self.stage_sent.values()) + [self.frames_sent]:
            for copy in copies:
                copy.wait()
        if self.sems != SEMS:
            raise ValueError(self.sems)

    def own_part(self):
        self.share_norms()
        self.norm_copies = self.send_norms()
        self.make_mask()
        self.permute_in(0, self.hidden[0], self.halo, True)
        self.fill_halo(self.hidden[0])

    def schedule(self, unit):
        unit[0].exchange()
        unit[1].exchange()
        unit[6].exchange()
        unit[3].exchange()
        unit[7].exchange()
        unit[2].exchange()
        unit[4].exchange()
        self.own_part()
        unit[1].spread()
        self.permute_in(1, self.sources[0], 0, True)
        self.take_norms()
        unit[10].exchange()
        unit[0].spread()
        self.permute_in(3, self.top_grad, 0, False)
        unit[6].spread()
        unit[2].spread()
        unit[3].spread()
        unit[10].spread()
        unit[5].exchange()
        unit[8].exchange()
        unit[2].side_second()
        unit[9].exchange()
        unit[1].second()
        unit[3].side_second()
        unit[5].spread()
        unit[4].spread()
        unit[0].second()
        unit[1].third()
        unit[6].second()
        unit[2].second()
        unit[0].third()
        unit[3].second()
        unit[5].side_second()
        unit[1].cores()
        unit[10].second()
        unit[1].arrived()
        unit[0].cores()
        unit[2].third()
        unit[0].arrived()
        unit[3].third()
        self.conv(0)
        unit[2].side_third()
        self.moments_begin(0)
        self.moments_pass(0)
        unit[4].side_second()
        unit[3].side_third()
        unit[4].second()
        unit[5].second()
        unit[10].third()
        unit[2].cores()
        unit[7].spread()
        unit[5].side_third()
        unit[2].arrived()
        unit[6].side_second()
        self.moments_end(0)
        unit[8].spread()
        unit[3].cores()
        unit[4].third()
        self.activate(0)
        unit[4].side_third()
        unit[5].third()
        unit[3].arrived()
        unit[10].cores()
        self.conv(1)
        unit[10].arrived()
        self.moments_begin(1)
        self.permute_in(2, self.sources[1], 0, True)
        self.moments_pass(1)
        unit[7].second()
        unit[7].side_second()
        self.dense_all()
        unit[9].spread()
        unit[4].cores()
        unit[6].side_third()
        unit[6].third()
        unit[5].cores()
        unit[4].arrived()
        unit[8].second()
        self.moments_end(1)
        self.activate(1)
        unit[9].side_second()
        unit[5].arrived()
        unit[7].third()
        self.conv(2)
        unit[7].side_third()
        self.moments_begin(2)
        unit[6].cores()
        self.moments_pass(2)
        unit[8].side_second()
        unit[9].second()
        unit[8].third()
        unit[7].cores()
        unit[9].side_third()
        unit[6].arrived()
        self.moments_end(2)
        self.activate(2)
        unit[9].third()
        unit[7].arrived()
        self.conv(3)
        unit[8].side_third()
        self.moments_begin(3)
        self.moments_pass(3)
        unit[9].cores()
        unit[8].cores()
        unit[9].arrived()
        self.moments_end(3)
        self.activate(3)
        unit[8].arrived()
        self.conv(4)
        self.moments_begin(4)
        self.moments_pass(4)
        self.moments_end(4)
        self.totals_begin(4)
        self.totals_pass(4)
        self.write_output()
        self.gather_done()
        self.totals_end(4)
        self.field_grad(4)
        self.conv_back(4)
        self.totals_begin(3)
        self.taps_grad(4, 0)
        self.totals_pass(3)
        unit[8].back_cores()
        self.taps_grad(4, 1)
        unit[9].back_cores()
        self.dense_weight_grad(2)
        unit[8].back_third()
        self.dense_weight_grad(0)
        self.totals_end(3)
        self.field_grad(3)
        unit[9].back_third()
        self.conv_back(3)
        self.totals_begin(2)
        self.taps_grad(3, 0)
        unit[6].back_cores()
        self.totals_pass(2)
        unit[9].back_second()
        unit[8].back_side_second()
        unit[8].back_second()
        self.taps_grad(3, 1)
        unit[7].back_cores()
        unit[6].back_third()
        unit[9].back_side_second()
        self.dense_weight_grad(1)
        self.totals_end(2)
        unit[10].back_cores()
        unit[9].back_first()
        self.field_grad(2)
        unit[7].back_third()
        self.conv_back(2)
        unit[8].back_first()
        self.totals_begin(1)
        unit[10].back_third()
        self.taps_grad(2, 0)
        self.totals_pass(1)
        unit[6].back_second()
        unit[4].back_cores()
        unit[6].back_side_second()
        self.taps_grad(2, 1)
        unit[5].back_cores()
        unit[7].back_second()
        unit[7].back_side_second()
        unit[10].back_second()
        self.totals_end(1)
        self.field_grad(1)
        unit[5].back_third()
        unit[4].back_third()
        unit[6].back_first()
        self.conv_back(1)
        unit[10].back_first()
        unit[7].back_first()
        self.totals_begin(0)
        self.taps_grad(1, 0)
        self.totals_pass(0)
        unit[5].back_second()
        unit[2].back_cores()
        unit[5].back_side_second()
        unit[4].back_second()
        self.taps_grad(1, 1)
        unit[2].back_third()
        unit[3].back_cores()
        unit[4].back_side_second()
        unit[5].back_first()
        unit[3].back_third()
        self.totals_end(0)
        self.field_grad(0)
        self.taps_grad(0, 0)
        unit[0].back_cores()
        unit[4].back_first()
        self.taps_grad(0, 1)
        unit[0].back_third()
        unit[2].back_second()
        unit[3].back_second()
        unit[2].back_side_second()
        self.conv_back(0)
        unit[3].back_side_second()
        unit[1].back_cores()
        unit[1].back_third()
        unit[2].back_first()
        unit[0].back_second()
        unit[7].back_side_first()
        unit[4].back_side_first()
        unit[8].back_side_first()
        unit[2].back_side_first()
        unit[5].back_side_first()
        unit[3].back_first()
        self.dense_source_grad(0)
        unit[1].back_second()
        unit[0].back_first()
        unit[2].back_exchange()
        unit[6].back_side_first()
        unit[4].back_exchange()
        unit[8].back_exchange()
        unit[1].back_first()
        unit[10].back_exchange()
        unit[5].back_exchange()
        self.write_input_grad()
        unit[9].back_side_first()
        unit[6].back_exchange()
        unit[3].back_side_first()
        unit[7].back_exchange()
        self.dense_source_grad(1)
        unit[0].back_exchange()
        unit[9].back_exchange()
        unit[3].back_exchange()
        unit[8].back_deliver()
        unit[6].back_deliver()
        unit[1].back_exchange()
        unit[7].back_deliver()
        self.dense_source_grad(2)
        self.write_norm_grads()
        unit[2].back_deliver()
        unit[9].back_deliver()
        unit[3].back_deliver()
        unit[4].back_deliver()
        unit[0].back_deliver()
        unit[10].back_deliver()
        unit[5].back_deliver()
        unit[1].back_deliver()


INS = (
    "block_input",
    "prior_first",
    "prior_second",
    "raw_lengths",
    "speed_index",
    "conv_one",
    "conv_two",
    "conv_three",
    "conv_four",
    "conv_five",
    "dense_input",
    "dense_first",
    "dense_second",
    "norm_scale",
    "norm_shift",
    "out_grad",
)
OUTS = (
    ("block_output", "input_grad", "first_grad", "second_grad")
    + tuple(name + GRAD for name in INS[5:13])
    + ("scale_grad", "shift_grad")
)
FIRST_X, FIRST_Y, SIDE_X, SIDE_Y = Z + X + Y, Z + Y + X, X + Z + Y, Y + Z + X
SEMS = 204


PARTS = (
    ((32, 32, 0, 0), (32, 16, 0, 0)),
    ((32, 16, 16, 16), (16, 32, 16, 16)),
    ((32, 16, 16, 16), (16, 32, 16, 16)),
    ((32, 16, 16, 16), (16, 32, 16, 16)),
    ((32, 16, 16, 16), (16, 32, 16, 16)),
    ((16, 16, 0, 0),),
)


def hop_buffers(spec, stages, vmem, chans):
    _, _, _, parts = spec
    found = {}
    early = sum(size for order, size in parts if order[0] == Z)
    for order, size in parts:
        for stage in stages:
            if not size or (stage == 0 and order == FIRST_Y):
                continue
            keep, axis = order[:stage], order[stage]
            count = (3 if axis == Z else 1) * (2 if Y in keep else 1)
            inner = ((4,) if Z in keep else ()) + ((2,) if X in keep else ())
            rows = early if order == FIRST_X and stage == 0 else size
            found[order + str(stage)] = vmem((count,) + inner + (rows, chans), BF)
    return found


def device_program(*args):
    named = dict(zip(INS, args))
    frames, c_in = args[0].shape[1:]
    chans = named["out_grad"].shape[2]
    taps = named["conv_one"].shape[0]
    width = named["conv_one"].shape[2]
    piece = [c_in // 8] + [chans // 8] * 4
    height = [taps * part for part in piece] + [3 * piece[0]]
    piece.append(piece[0])
    specs = []
    for group, rows in enumerate(height):
        quarter = -(-rows // 64) * 16
        base = 0
        for parts in PARTS[group]:
            parts = tuple(zip((FIRST_X, FIRST_Y, SIDE_X, SIDE_Y), parts))
            depth = sum(size for _, size in parts)
            specs.append((group, base, depth, parts))
            base += 4 * depth
        if base != 4 * quarter:
            raise ValueError((group, base, quarter))
    tops = [max(base + 4 * depth for at, base, depth, _ in specs if at == g) for g in range(6)]
    halo = (taps // 2) * SEG
    tall = frames + 2 * halo

    shape = [args[spot].shape for spot in (15, 0, 1, 2)]
    shape = [(frames, one[2]) for one in shape]
    shape += [args[spot].shape for spot in range(5, 13)] + [(8, width)] * 2
    kinds = [BF] + [F32] * 13
    vmem = pltpu.VMEM
    groups = range(6)
    scratch = {
        "full": [vmem((4, 2, tops[g], chans), BF) for g in groups],
        "local": [vmem((tops[g], 128), BF) for g in groups],
        "landing": [vmem((3, spec[2], 128), BF) for spec in specs],
        "by_core": [vmem((2, 4, 2, spec[2], chans), BF) for spec in specs[2:6]]
        + [vmem((2, 4, 2, specs[10][2], chans), BF)],
        "first_landing": [hop_buffers(specs[at], (2,), vmem, chans) for at in (2, 3, 4, 5, 6, 7, 0, 1, 10)],
        "landings": [hop_buffers(spec, (0, 1), vmem, chans) for spec in specs],
        "first_sum": vmem((4, 2, tops[4], chans), BF),
        "stage": vmem((chans // 128, frames, 128), F32),
        "second_stage": vmem((c_in // 128, frames, 128), F32),
        "grad_stage": [vmem(args[5 + g].shape, F32) for g in (1, 2, 0)]
        + [vmem((3, c_in // 8, width), F32)],
        "held": [vmem(args[5 + at].shape, BF) for at in range(10)],
        "norm_grads": vmem((2, 8, width), F32),
        "out_sems": pltpu.SemaphoreType.DMA((28,)),
        "hidden": [vmem((tall, c_in), BF)] + [vmem((tall, chans), BF)] * 4,
        "outs": [vmem((frames, chans), F32)] * 5,
        "dense_outs": [vmem((frames, chans), BF)] * 3,
        "sources": [vmem((frames, c_in), BF)] * 2,
        "top_grad": vmem((frames, chans), BF),
        "conv_grad": vmem((tall, chans), BF),
        "dense_grad": vmem((frames, chans), BF),
        "grad": vmem((frames, chans), F32),
        "paired": vmem((frames + SEG, 256), F32),
        "valid": vmem((frames, 128), F32),
        "mine": vmem((2, 2, 24, 128), F32),
        "others": vmem((2, 16, 24, 128), F32),
        "norms": vmem((4, 16, chans), F32),
        "scales": vmem((8, chans), F32),
        "shifts": vmem((8, chans), F32),
        "means": vmem((8, chans), F32),
        "invs": vmem((8, chans), F32),
        "send_sems": pltpu.SemaphoreType.DMA((SEMS,)),
        "recv_sems": pltpu.SemaphoreType.DMA((SEMS,)),
        "fetch_sems": pltpu.SemaphoreType.DMA((14,)),
        "sum_send": pltpu.SemaphoreType.DMA((4,)),
        "sum_recv": pltpu.SemaphoreType.DMA((4,)),
    }
    flat, tree = jax.tree.flatten(scratch, is_leaf=lambda leaf: not isinstance(leaf, (dict, list)))

    def body(*refs):
        refs, rest = dict(zip(INS + OUTS, refs)), refs[len(INS) + len(OUTS) :]
        refs.update(jax.tree.unflatten(tree, rest))
        refs["given"] = [refs[name] for name in INS[5:15]]
        refs["pieces"] = [refs["held"][at : at + 1] for at in range(5)] + [refs["held"][5:8]]
        refs["grad_outs"] = [[refs[name + GRAD]] for name in INS[5:10]] + [
            [refs[name + GRAD] for name in INS[10:13]]
        ]
        refs["piece"], refs["specs"] = piece, specs
        kernel = Kernel(refs, (taps, frames, chans, width))
        kernel.run()

    outside = pl.BlockSpec(memory_space=pl.ANY)
    small = pl.BlockSpec(memory_space=pltpu.SMEM)
    outs = pl.pallas_call(
        body,
        out_shape=[jax.ShapeDtypeStruct(dims, kind) for dims, kind in zip(shape, kinds)],
        in_specs=[small if spot in (3, 4) else outside for spot in range(16)],
        out_specs=[outside] * 14,
        scratch_shapes=flat,
        compiler_params=pltpu.CompilerParams(
            collective_id=0, has_side_effects=True, vmem_limit_bytes=63 * 2**20
        ),
    )(*args)
    outs = hand_over(outs)
    return tuple(out[None] if place < 4 else out for place, out in enumerate(outs))


def hand_over(arrays):
    count = len(arrays)

    def body(*refs):
        ins, outs, held = refs[:count], refs[count : 2 * count], refs[2 * count : 3 * count]
        sems = refs[-1]
        first = [
            pltpu.make_async_copy(ins[place], held[place], sems.at[place])
            for place in range(count)
        ]
        for copy in first:
            copy.start()
        second = [
            pltpu.make_async_copy(held[place], outs[place], sems.at[count + place])
            for place in range(count)
        ]
        for came, copy in zip(first, second):
            came.wait()
            copy.start()
        for copy in second:
            copy.wait()

    return pl.pallas_call(
        body,
        out_shape=[jax.ShapeDtypeStruct(one.shape, one.dtype) for one in arrays],
        in_specs=[pl.BlockSpec(memory_space=pl.ANY)] * count,
        out_specs=[pl.BlockSpec(memory_space=pl.ANY)] * count,
        scratch_shapes=[pltpu.VMEM(one.shape, one.dtype) for one in arrays]
        + [pltpu.SemaphoreType.DMA((2 * count,))],
        compiler_params=pltpu.CompilerParams(vmem_limit_bytes=62 * 2**20),
    )(*arrays)


def silu_slope(value):
    sigmoid = jax.nn.sigmoid(value)
    return sigmoid * (1.0 + value * (1.0 - sigmoid))


def padded_time(field, extent):
    half = extent // 2
    return jnp.pad(field, ((0, 0), (half, half), (0, 0)))


def conv_apply(field, weight):
    extent = weight.shape[0]
    length = field.shape[1]
    padded = padded_time(field, extent)
    total = jnp.einsum(
        APPLY, padded[:, 0:length], weight[0], preferred_element_type=jnp.float32
    )
    for offset in range(1, extent):
        total = total + jnp.einsum(
            APPLY,
            padded[:, offset : offset + length],
            weight[offset],
            preferred_element_type=jnp.float32,
        )
    return total


def conv_grads(field, grad_out, weight):
    extent = weight.shape[0]
    length = field.shape[1]
    padded = padded_time(field, extent)
    padded_grad = padded_time(grad_out, extent)
    taps = []
    grad_in = None
    for offset in range(extent):
        taps.append(
            jnp.einsum(
                OUTER,
                padded[:, offset : offset + length],
                grad_out,
                preferred_element_type=jnp.float32,
            )
        )
        back = extent - 1 - offset
        term = jnp.einsum(
            BACK,
            padded_grad[:, back : back + length],
            weight[offset],
            preferred_element_type=jnp.float32,
        )
        grad_in = term if grad_in is None else grad_in + term
    return (jnp.stack(taps), grad_in)


def moments(fields, mask, local_count):
    firsts = jnp.stack([jnp.sum(field * mask, axis=(0, 1)) for field in fields])
    firsts, count = lax.psum((firsts, local_count), (WIDE, NARROW))
    means = firsts / count
    seconds = jnp.stack(
        [
            jnp.sum(mask * jnp.square(field - means[place]), axis=(0, 1))
            for place, field in enumerate(fields)
        ]
    )
    spread = lax.psum(seconds, (WIDE, NARROW)) / count
    return (means, lax.rsqrt(spread + EPS), count)


def norm_backward(grad_act, norms, scales, inv_std, mask, count):
    shift_part = jnp.sum(grad_act, axis=(0, 1))
    scale_parts = jnp.stack([jnp.sum(grad_act * norm, axis=(0, 1)) for norm in norms])
    shift_sum, scale_sum = lax.psum((shift_part, scale_parts), (WIDE, NARROW))
    grads = []
    for place in range(len(norms)):
        centered = grad_act - mask * (shift_sum + norms[place] * scale_sum[place]) / count
        grads.append((scales[place] * inv_std[place] * centered).astype(jnp.bfloat16))
    return (grads, shift_sum, scale_sum)


def collect(item):
    return lax.all_gather(
        lax.all_gather(item, WIDE, axis=1, tiled=True), NARROW, axis=2, tiled=True
    )


def spread(item):
    item = lax.psum_scatter(item.astype(BF), NARROW, scatter_dimension=2, tiled=True)
    return lax.psum_scatter(item.astype(F32), WIDE, scatter_dimension=1, tiled=True)


def shards(
    block_input,
    prior_first,
    prior_second,
    raw_lengths,
    speed_index,
    conv_one,
    conv_two,
    conv_three,
    conv_four,
    conv_five,
    dense_input,
    dense_first,
    dense_second,
    norm_scale,
    norm_shift,
    out_grad,
):
    utter, length = (block_input.shape[0], block_input.shape[1])
    lengths = raw_lengths * 10 // (9 + speed_index)
    frames = lax.broadcasted_iota(jnp.int32, (utter, length), 1)
    mask = (frames < lengths[:, None]).astype(jnp.float32)[:, :, None]
    mask_low = mask.astype(jnp.bfloat16)
    local_count = jnp.sum(lengths).astype(jnp.float32)
    weights = (
        conv_one,
        conv_two,
        conv_three,
        conv_four,
        conv_five,
        dense_input,
        dense_first,
        dense_second,
    )
    full_weights = [collect(weight) for weight in weights]
    scales = lax.all_gather(norm_scale, NARROW, axis=1, tiled=True).astype(F32)
    shifts = lax.all_gather(norm_shift, NARROW, axis=1, tiled=True).astype(F32)
    sources = (block_input * mask_low, prior_first * mask_low, prior_second * mask_low)
    hidden = sources[0]
    inputs_kept, norms_kept, acts_kept, inv_kept = ([], [], [], [])
    for index in range(4):
        conv_out = conv_apply(hidden, full_weights[index])
        means, inv_std, count = moments((conv_out,), mask, local_count)
        norm = (conv_out - means[0]) * inv_std[0]
        act = scales[index] * norm + shifts[index]
        inputs_kept.append(hidden)
        norms_kept.append(norm)
        acts_kept.append(act)
        inv_kept.append(inv_std[0])
        hidden = (jax.nn.silu(act) * mask).astype(jnp.bfloat16)
    last_out = conv_apply(hidden, full_weights[4])
    dense_outs = tuple(
        (
            jnp.einsum(
                APPLY,
                sources[place],
                full_weights[5 + place][0],
                preferred_element_type=jnp.float32,
            )
            for place in range(3)
        )
    )
    fields = (last_out,) + dense_outs
    means, inv_std, count = moments(fields, mask, local_count)
    last_norms = tuple(((fields[place] - means[place]) * inv_std[place] for place in range(4)))
    total = scales[4] * last_norms[0] + shifts[4]
    for place in range(1, 4):
        total = total + scales[4 + place] * last_norms[place] + shifts[4 + place]
    block_output = (jax.nn.silu(total) * mask).astype(jnp.bfloat16)
    grad_total = out_grad.astype(jnp.float32) * mask * silu_slope(total)
    field_grads, shift_sum, scale_sum = norm_backward(
        grad_total, last_norms, scales[4:8], inv_std, mask, count
    )
    weight_grads = [None] * 8
    scale_rows = [None] * 8
    shift_rows = [None] * 8
    for place in range(4):
        scale_rows[4 + place] = scale_sum[place]
        shift_rows[4 + place] = shift_sum
    weight_grads[4], grad_hidden = conv_grads(hidden, field_grads[0], full_weights[4])
    source_grads = []
    for place in range(3):
        weight_grads[5 + place] = jnp.einsum(
            OUTER,
            sources[place],
            field_grads[1 + place],
            preferred_element_type=jnp.float32,
        )[None]
        source_grads.append(
            jnp.einsum(
                BACK,
                field_grads[1 + place],
                full_weights[5 + place][0],
                preferred_element_type=jnp.float32,
            )
        )
    for index in (3, 2, 1, 0):
        grad_act = grad_hidden * mask * silu_slope(acts_kept[index])
        grads_one, shift_one, scale_one = norm_backward(
            grad_act,
            (norms_kept[index],),
            scales[index : index + 1],
            inv_kept[index][None],
            mask,
            count,
        )
        scale_rows[index] = scale_one[0]
        shift_rows[index] = shift_one
        weight_grads[index], grad_hidden = conv_grads(
            inputs_kept[index], grads_one[0], full_weights[index]
        )
    input_grad = mask * (grad_hidden + source_grads[0])
    first_grad = mask * source_grads[1]
    second_grad = mask * source_grads[2]
    owned = [spread(grad) for grad in weight_grads]
    portion = scales.shape[1] // lax.axis_size(NARROW)
    start = lax.axis_index(NARROW) * portion
    scale_grad = lax.dynamic_slice_in_dim(jnp.stack(scale_rows), start, portion, 1)
    shift_grad = lax.dynamic_slice_in_dim(jnp.stack(shift_rows), start, portion, 1)
    return (
        block_output,
        input_grad,
        first_grad,
        second_grad,
        owned[0],
        owned[1],
        owned[2],
        owned[3],
        owned[4],
        owned[5],
        owned[6],
        owned[7],
        scale_grad,
        shift_grad,
    )


def solution(mesh):
    by_utterance = P((WIDE, NARROW), None, None)
    lengths = P((WIDE, NARROW))
    weight = P(None, WIDE, NARROW)
    norm = P(None, NARROW)
    kernel_fits = (mesh.shape[WIDE], mesh.shape[NARROW]) == (8, 4)
    return jax.shard_map(
        device_program if kernel_fits else shards,
        mesh=mesh,
        in_specs=(by_utterance,) * 3
        + (lengths,) * 2
        + (weight,) * 8
        + (norm,) * 2
        + (by_utterance,),
        out_specs=(by_utterance,) * 4 + (weight,) * 8 + (norm,) * 2,
        check_vma=False,
    )
```

```python
import functools

import jax
import jax.numpy as jnp
from jax import lax
from jax.experimental import pallas as pl
from jax.experimental.pallas import tpu as pltpu
from jax.sharding import PartitionSpec as P

EPS = 1e-05
BF = jnp.bfloat16
F32 = jnp.float32
WIDE, NARROW = "wide", "narrow"
GRAD = "_grad"
APPLY, OUTER, BACK = "utc,cd->utd", "utc,utd->cd", "utd,cd->utc"
MESH = pl.DeviceIdType.MESH
X, Y, Z = "xyz"
SEG = 16
NT = (((1,), (1,)), ((), ()))
TN = (((0,), (0,)), ((), ()))


def al(value, to=16):
    return pl.multiple_of(value, to)


def fold(value):
    rows, lanes = value.shape
    return jnp.sum(value.reshape(rows // 8, 8, lanes), axis=0)


def wide_of(column, lanes):
    return jnp.concatenate([column] * (lanes // 128), axis=1)


def sigmoid(value):
    return 0.5 * jnp.tanh(0.5 * value) + 0.5


class Unit:
    def __init__(self, kernel, group, base, depth, parts):
        self.k, self.group, self.base, self.depth = kernel, group, base, depth
        at = 0
        self.parts = []
        for order, size in parts:
            if size:
                self.parts.append((order, at, size))
            at += size
        early = [part for part in self.parts if part[0][0] == Z]
        self.early, self.late = early, [part for part in self.parts if part[0][0] != Z]
        self.head = (early[0][0], 0, sum(part[2] for part in early))
        self.full = kernel.full[group]

    def rows(self, narrow, off, size):
        return pl.ds(al(self.base + self.depth * narrow + off), size)

    def peers(self, axis):
        k = self.k
        if axis == Z:
            return [(k.z_peer(step), k.n) for step in (1, 3, 2)]
        return [(k.x_peer(), k.n)] if axis == X else [(k.w, k.y_peer())]


    def pass_on(self, part, stage):
        k = self.k
        order, off, size = part
        have, axis = order[:stage], order[stage]
        z = slice(None) if Z in have else k.z
        x = slice(None) if X in have else k.x
        copies = []
        for narrow in (k.n, k.y_peer()) if Y in have else (k.n,):
            view = self.full.at[z, x, self.rows(narrow, off, size)]
            copies += [k.remote(view, view, *peer) for peer in self.peers(axis)]
        return copies

    def exchange(self):
        k, depth = self.k, self.depth
        local, self.landing = k.local[self.group], k.landing[k.units.index(self)]
        self.a2a = [
            k.remote(
                local.at[self.rows(k.narrow_peer(step), 0, depth)],
                self.landing.at[step - 1],
                k.w,
                k.narrow_peer(step),
            )
            for step in range(1, 4)
        ]

    def spread(self):
        k = self.k
        k.land(self.a2a)
        mine = self.rows(k.n, 0, self.depth)
        total = jnp.dot(k.local[self.group][mine, :], k.pick(k.n), preferred_element_type=F32)
        for step in range(1, 4):
            total = total + jnp.dot(
                self.landing[step - 1], k.pick((k.n - step) % 4), preferred_element_type=F32
            )
        self.full[k.z, k.x, mine] = total.astype(BF)
        self.first = self.pass_on(self.head, 0)
        self.side = [copy for part in self.late for copy in self.pass_on(part, 0)]

    def second(self):
        self.k.land(self.first)
        self.two = [copy for part in self.early for copy in self.pass_on(part, 1)]

    def third(self):
        self.k.land(self.two)
        self.three = [copy for part in self.early for copy in self.pass_on(part, 2)]

    def side_second(self):
        self.k.land(self.side)
        self.side_two = [copy for part in self.late for copy in self.pass_on(part, 1)]

    def side_third(self):
        self.k.land(self.side_two)
        self.side_three = [copy for part in self.late for copy in self.pass_on(part, 2)]

    def cores(self):
        k = self.k
        k.land(self.three)
        if self.late:
            k.land(self.side_three)
        self.cross = []
        for row in range(2):
            part = self.full.at[:, :, self.rows(2 * row + k.core, 0, self.depth)]
            self.cross.append(k.remote(part, part, k.w, k.core_peer()))

    def arrived(self):
        self.k.land(self.cross)


    def begin_scatter(self, full, base, by_core, buffers):
        self.full, self.base, self.by_core, self.buffers = full, base, by_core, buffers

    def give(self, part, stage):
        k = self.k
        order, off, size = part
        keep, axis = order[:stage], order[stage]
        buffer = self.buffers[order + str(stage)]
        copies = []
        for narrow in (k.n, k.y_peer()) if Y in keep else (k.n,):
            for wide, far in self.peers(axis):
                z = slice(None) if Z in keep else wide // 2
                x = slice(None) if X in keep else wide % 2
                row = far if axis == Y else narrow
                copies.append(
                    k.remote(
                        self.full.at[z, x, self.rows(row, off, size)],
                        buffer.at[len(copies)],
                        wide,
                        far,
                    )
                )
        return copies

    def take(self, part, stage):
        k = self.k
        order, off, size = part
        keep, axis = order[:stage], order[stage]
        buffer = self.buffers[order + str(stage)]
        each = len(self.peers(axis))
        for place, narrow in enumerate((k.n, k.y_peer()) if Y in keep else (k.n,)):
            k.add_into(
                self.full,
                self.rows(narrow, off, size),
                [buffer.at[place * each + index] for index in range(each)],
                None if Z in keep else k.z,
                None if X in keep else k.x,
            )

    def back_cores(self):
        k = self.k
        self.cross = []
        for row in range(2):
            part = self.full.at[:, :, self.rows(2 * row + 1 - k.core, 0, self.depth)]
            self.cross.append(
                k.remote(
                    part, self.by_core.at[row, :, :, pl.ds(0, self.depth)], k.w, k.core_peer()
                )
            )

    def back_third(self):
        k = self.k
        k.land(self.cross)
        for row in range(2):
            landing = self.by_core.at[row, :, :, pl.ds(0, self.depth)]
            k.add_into(
                self.full, self.rows(2 * row + k.core, 0, self.depth), [landing], None, None
            )
        self.three = [copy for part in self.early for copy in self.give(part, 2)]
        self.side_three = [copy for part in self.late for copy in self.give(part, 2)]

    def back_second(self):
        self.k.land(self.three)
        for part in self.early:
            self.take(part, 2)
        self.two = [copy for part in self.early for copy in self.give(part, 1)]

    def back_first(self):
        self.k.land(self.two)
        for part in self.early:
            self.take(part, 1)
        self.first = self.give(self.head, 0)

    def back_side_second(self):
        self.k.land(self.side_three)
        for part in self.late:
            self.take(part, 2)
        self.side_two = [copy for part in self.late for copy in self.give(part, 1)]

    def back_side_first(self):
        self.k.land(self.side_two)
        for part in self.late:
            self.take(part, 1)
        self.side = [copy for part in self.late for copy in self.give(part, 0)]

    def back_exchange(self):
        k = self.k
        k.land(self.first)
        if self.late:
            k.land(self.side)
        sums = []
        for part in [self.head] + self.late:
            order, off, size = part
            total = self.full[k.z, k.x, self.rows(k.n, off, size)].astype(F32)
            buffer = self.buffers[order + str(0)]
            for index in range(len(self.peers(order[0]))):
                total = total + buffer[index].astype(F32)
            sums.append(total.astype(BF))
        total = jnp.concatenate(sums, axis=0) if len(sums) > 1 else sums[0]
        self.a2a = []
        local = k.local[self.group]
        mine = pl.ds(al(self.local_base + self.depth * k.n), self.depth)
        for step in range(4):
            peer = k.narrow_peer(step)
            part = lax.dot_general(total, k.pick(peer), NT, preferred_element_type=F32)
            if step == 0:
                local[mine, :] = part.astype(BF)
            else:
                self.landing[step - 1] = part.astype(BF)
                self.a2a.append(k.remote(self.landing.at[step - 1], local.at[mine], k.w, peer))

    def back_deliver(self):
        k = self.k
        k.land(self.a2a)
        k.deliver(self.group, self.local_base, self.local_base + 4 * self.depth)

class Kernel:
    def __init__(self, refs, shapes):
        self.__dict__.update(refs)
        self.taps, self.frames, self.chans, self.width = shapes
        self.span = self.frames // SEG
        self.halo = (self.taps // 2) * SEG
        self.w = lax.axis_index(WIDE)
        self.n = lax.axis_index(NARROW)
        self.z, self.x = self.w // 2, self.w % 2
        self.y, self.core = self.n // 2, self.n % 2
        self.sems = 0
        self.turn = self.ended = 0
        self.flying, self.landed = {}, []


    def remote(self, src, dst, wide, narrow):
        index = self.semaphore()
        copy = pltpu.make_async_remote_copy(
            src_ref=src,
            dst_ref=dst,
            send_sem=self.send_sems.at[index],
            recv_sem=self.recv_sems.at[index],
            device_id=(wide, narrow),
            device_id_type=MESH,
        )
        copy.start()
        self.flying[id(copy)] = (index, copy)
        return copy

    def semaphore(self):
        for place, (turn, index, copy) in enumerate(self.landed):
            if turn <= self.ended:
                self.landed.pop(place)
                if copy is not None:
                    copy.wait_send()
                return index
        self.sems += 1
        return self.sems - 1

    def land(self, copies):
        for copy in copies:
            copy.wait_recv()
            if id(copy) in self.flying:
                index, copy = self.flying.pop(id(copy))
                self.landed.append([self.turn + 1, index, copy])

    def settle(self):
        for entry in self.landed:
            if entry[2] is not None:
                entry[2].wait_send()
                entry[2] = None

    def narrow_peer(self, step):
        return (self.n + step) % 4

    def wide_peer(self, step):
        return (self.w + step) % 8

    def z_peer(self, step):
        return ((self.z + step) % 4) * 2 + self.x

    def x_peer(self):
        return self.z * 2 + (1 - self.x)

    def y_peer(self):
        return (1 - self.y) * 2 + self.core

    def core_peer(self):
        return self.y * 2 + (1 - self.core)

    def chip_peers(self):
        return [
            ((self.w + step) % 8, (self.n + 2 * far) % 4)
            for step in range(8)
            for far in range(2)
            if step + far > 0
        ]

    def greet(self):
        barrier = pltpu.get_barrier_semaphore()
        greeted = self.chip_peers() + [(self.w, self.narrow_peer(step)) for step in (1, 3)]
        for peer in greeted:
            pl.semaphore_signal(barrier, inc=1, device_id=peer, device_id_type=MESH)
        return barrier, len(greeted)

    def met(self, greeted):
        pl.semaphore_wait(*greeted)


    def pack(self, rows):
        parts = [row[:, at : at + 128] for row in rows for at in range(0, row.shape[1], 128)]
        rest = -len(parts) % 8
        if rest:
            parts.append(jnp.zeros((rest, 128), F32))
        return jnp.concatenate(parts, axis=0)

    def unpack(self, packed, index):
        each = self.chans // 128
        return jnp.concatenate(
            [packed[each * index + k : each * index + k + 1] for k in range(each)], axis=1
        )

    def slot_copy(self, src, dst, index, device):
        copy = pltpu.make_async_remote_copy(
            src_ref=src,
            dst_ref=dst,
            send_sem=self.sum_send.at[index],
            recv_sem=self.sum_recv.at[index],
            device_id=device,
            device_id_type=MESH,
        )
        copy.start()
        return copy

    def sums_start(self, packed):
        place = self.turn % 2
        self.turn += 1
        rows = pl.ds(0, packed.shape[0])
        self.mine[place, 0, rows] = packed
        copy = self.slot_copy(
            self.mine.at[place, 0, rows],
            self.others.at[place, 15, rows],
            2 * place,
            (self.w, self.core_peer()),
        )
        return packed, place, rows, copy

    def sums_middle(self, started, join):
        packed, place, rows, copy = started
        self.land([copy])
        pair = join([packed, self.others[place, 15, rows]])
        self.mine[place, 1, rows] = pair
        for index, peer in enumerate(self.chip_peers()):
            self.slot_copy(
                self.mine.at[place, 1, rows],
                self.others.at[place, index, rows],
                2 * place + 1,
                peer,
            )
        return pair, place, rows, copy

    def sums_end(self, started, join):
        pair, place, rows, first = started
        landed = self.others.at[place, pl.ds(0, 15), rows]
        index = 2 * place + 1
        pltpu.make_async_copy(landed, landed, self.sum_recv.at[index]).wait()
        result = join([pair] + [self.others[place, at, rows] for at in range(15)])
        first.wait_send()
        pltpu.make_async_copy(landed, landed, self.sum_send.at[index]).wait()
        self.ended += 1
        return result

    def join_moments(self, fields):
        each = fields * (self.chans // 128)

        def join(parts):
            counts = [part[2 * each : 2 * each + 1] for part in parts]
            count = functools.reduce(jnp.add, counts)
            mean = (
                functools.reduce(
                    jnp.add, [part[0:each] * own for part, own in zip(parts, counts)]
                )
                / count
            )
            spread = functools.reduce(
                jnp.add,
                [
                    part[each : 2 * each] + own * jnp.square(part[0:each] - mean)
                    for part, own in zip(parts, counts)
                ],
            )
            joined = [mean, spread, count]
            rest = parts[0].shape[0] - 2 * each - 1
            if rest:
                joined.append(jnp.zeros((rest, 128), F32))
            return jnp.concatenate(joined, axis=0)

        return join

    @staticmethod
    def join_sums(parts):
        return functools.reduce(jnp.add, parts)


    def pick(self, owner):
        row = lax.broadcasted_iota(jnp.int32, (128, self.chans), 0)
        lane = lax.broadcasted_iota(jnp.int32, (128, self.chans), 1)
        hit = jnp.logical_and(row < self.width, lane == owner * self.width + row)
        return jnp.where(hit, 1.0, 0.0).astype(BF)

    def load_local(self, group):
        local = self.local[group]
        local[...] = jnp.zeros(local.shape, local.dtype)
        at = 0
        for ref in self.pieces[group]:
            rows = ref.shape[1]
            for tap in range(ref.shape[0]):
                local[at : at + rows, 0 : self.width] = ref[tap]
                at += rows

    def add_into(self, target, rows, landings, zs, xs):
        whole = (zs is None, xs is None)
        count = (4 if whole[0] else 1) * (2 if whole[1] else 1)

        def step(item, carry):
            z = (item // 2 if whole[1] else item) if whole[0] else zs
            x = item % 2 if whole[1] else xs
            inner = ((z,) if whole[0] else ()) + ((x,) if whole[1] else ())
            if len(landings) == 1:
                target[z, x, rows] = target[z, x, rows] + landings[0][inner + (slice(None),)]
                return carry
            total = target[z, x, rows].astype(F32)
            for landing in landings:
                total = total + landing[inner + (slice(None),)].astype(F32)
            target[z, x, rows] = total.astype(BF)
            return carry

        if count == 1:
            step(0, 0)
        else:
            lax.fori_loop(0, count, step, 0)

    def deliver(self, group, low, high):
        slot = group % 2 if 0 < group < 5 else 2 + group // 5
        for user in (group - 2, group + 2):
            for copy in self.stage_sent.pop((slot, user), []):
                copy.wait()
        local, stage, at = self.local[group], self.grad_stage[slot], 0
        sent = self.stage_sent.setdefault((slot, group), [])
        for index, ref in enumerate(self.grad_outs[group]):
            height = ref.shape[1]
            done = []
            for tap in range(ref.shape[0]):
                if low < at + height <= high:
                    value = local[at : at + height, 0 : self.width]
                    stage[index + tap] = value.astype(F32)
                    done.append(tap)
                at += height
            if done:
                place = self.outgoing
                copy = self.out_copy(
                    stage.at[pl.ds(index + done[0], len(done))],
                    ref.at[pl.ds(done[0], len(done))],
                    8 + place,
                )
                self.outgoing += 1
                sent.append(copy)


    def weight(self, group, tap, low=0, high=None, lane_low=0, lane_high=None):
        piece = self.piece[group]
        high = piece * 8 if high is None else high
        lanes = slice(lane_low, self.chans if lane_high is None else lane_high)
        full = self.full[group]
        if low == 0 and high == piece * 8:
            return full[:, :, tap * piece : (tap + 1) * piece, lanes].reshape(
                piece * 8, lanes.stop - lanes.start
            )
        parts = []
        while low < high:
            part, begin = low // piece, low % piece
            end = min(piece, begin + high - low)
            parts.append(full[part // 2, part % 2, tap * piece + begin : tap * piece + end, lanes])
            low += end - begin
        return jnp.concatenate(parts, axis=0)

    def conv_forward(self, group, field, out):
        taps, main, pairs = self.taps, 256, self.taps // 2
        block = self.frames // 2
        for base in (0, block):
            tall = block + SEG if base else block

            def shifted(tap, height):
                return field[base + SEG * tap : base + SEG * tap + height, :]

            left = jnp.concatenate([shifted(tap, block) for tap in range(taps)], axis=1)
            right = jnp.concatenate(
                [self.weight(group, tap, 0, None, 0, main) for tap in range(taps)], axis=0
            )
            out[base : base + block, 0:main] = jnp.dot(left, right, preferred_element_type=F32)
            left = jnp.concatenate([shifted(2 * pair, tall) for pair in range(pairs)], axis=1)
            right = jnp.concatenate(
                [
                    jnp.concatenate(
                        [
                            self.weight(group, 2 * pair, 0, None, main),
                            self.weight(group, 2 * pair + 1, 0, None, main),
                        ],
                        axis=1,
                    )
                    for pair in range(pairs)
                ],
                axis=0,
            )
            self.paired[base : base + tall, :] = jnp.dot(
                left, right, preferred_element_type=F32
            )
            out[base : base + block, main:] = jnp.dot(
                shifted(taps - 1, block),
                self.weight(group, taps - 1, 0, None, main),
                preferred_element_type=F32,
            )

    def conv_backward(self, group, grad, out):
        taps, main, pairs = self.taps, 256, self.taps // 2
        chans = self.piece[group] * 8
        block = self.frames // 2
        last = taps - 1
        for base in (0, block):
            early = 0 if base else SEG

            def shifted(tap, early=0):
                at = base + SEG * (last - tap)
                return grad[at - early : at + block, :]

            left = jnp.concatenate([shifted(tap) for tap in range(taps)], axis=1)
            right = jnp.concatenate(
                [self.weight(group, tap, 0, main) for tap in range(taps)], axis=1
            )
            out[base : base + block, 0:main] = lax.dot_general(
                left, right, NT, preferred_element_type=F32
            )
            if chans > main:
                left = jnp.concatenate([shifted(2 * pair, early) for pair in range(pairs)], axis=1)
                right = jnp.concatenate(
                    [
                        jnp.concatenate(
                            [
                                self.weight(group, 2 * pair, main, chans),
                                self.weight(group, 2 * pair + 1, main, chans),
                            ],
                            axis=0,
                        )
                        for pair in range(pairs)
                    ],
                    axis=1,
                )
                self.paired[base + SEG - early : base + SEG + block, :] = lax.dot_general(
                    left, right, NT, preferred_element_type=F32
                )
                out[base : base + block, main:] = lax.dot_general(
                    shifted(last),
                    self.weight(group, last, main, chans),
                    NT,
                    preferred_element_type=F32,
                )

    def weight_grad(self, group, field, grad, full, tap, taps_end):
        taps, piece, chans = self.taps, self.piece[group], self.chans
        middle = field[self.halo : self.halo + self.frames, :]
        while tap < taps_end:
            count = min(2, taps_end - tap)
            right = jnp.concatenate(
                [
                    grad[
                        SEG * (taps - 1 - tap - k) : SEG * (taps - 1 - tap - k) + self.frames, :
                    ]
                    for k in range(count)
                ],
                axis=1,
            )
            got = lax.dot_general(middle, right, TN, preferred_element_type=F32).astype(BF)
            for k in range(count):
                full[:, :, (tap + k) * piece : (tap + k + 1) * piece, :] = got[
                    :, chans * k : chans * (k + 1)
                ].reshape(4, 2, piece, chans)
            tap += count

    def each(self, body, carry=None, height=64):
        def step(item, carry):
            return body(pl.ds(al(item * height, height), height), item, carry)

        return lax.fori_loop(0, self.frames // height, step, carry)

    def mask_of(self, rows, lanes):
        return wide_of(self.valid[rows, :], lanes)

    def fill_halo(self, field):
        span, around = self.span, self.halo // SEG
        lanes = field.shape[1]
        place = lax.broadcasted_iota(jnp.int32, (SEG, lanes), 0)
        for step in range(around):
            source = self.halo + SEG * (span - around + step)
            block = field[source : source + SEG, :].astype(F32)
            block = jnp.where(place == 0, 0.0, pltpu.roll(block, 1, 0))
            field[SEG * step : SEG * (step + 1), :] = block.astype(BF)
            source = self.halo + SEG * step
            block = field[source : source + SEG, :].astype(F32)
            block = jnp.where(place == SEG - 1, 0.0, pltpu.roll(block, SEG - 1, 0))
            target = self.halo + SEG * (span + step)
            field[target : target + SEG, :] = block.astype(BF)

    def fetch(self):
        self.held_copies = [
            pltpu.make_async_copy(source, home, self.fetch_sems.at[4 + place])
            for place, (source, home) in enumerate(zip(self.given, self.held))
        ]
        for copy in self.held_copies:
            copy.start()
        self.fetched = []
        homes = (self.dense_grad, self.conv_grad, self.hidden[4], self.hidden[3])
        inputs = (self.block_input, self.prior_first, self.prior_second, self.out_grad)
        for place, (source, home) in enumerate(zip(inputs, homes)):
            target = home.at[pl.ds(0, source.shape[1]), pl.ds(0, source.shape[2])]
            copy = pltpu.make_async_copy(source.at[0], target, self.fetch_sems.at[place])
            copy.start()
            self.fetched.append((target, copy))

    def permute_in(self, ref, target, offset, masked):
        ref, copy = self.fetched[ref]
        copy.wait()
        lanes = ref.shape[1]
        scratch = self.stage

        def widen(rows, item, carry):
            value = ref[rows, :].astype(F32)
            for k in range(lanes // 128):
                scratch[k, rows, :] = value[:, 128 * k : 128 * (k + 1)]
            return carry

        self.each(widen, 0)

        def move(item, carry):
            for k in range(4):
                at = item * 4 + k
                block = self.frames_in(at, scratch)[:, 0:lanes]
                if masked:
                    block = block * self.mask_of(pl.ds(al(at * SEG), SEG), lanes)
                target[pl.ds(al(offset + at * SEG), SEG), :] = block.astype(BF)
            return carry

        lax.fori_loop(0, self.span // 4, move, 0)

    def make_mask(self):
        length = (self.raw_lengths[0] * 10) // (9 + self.speed_index[0])

        def body(rows, item, carry):
            row = lax.broadcasted_iota(jnp.int32, (64, 128), 0) + item * 64
            frame = (row % SEG) * self.span + row // SEG
            self.valid[rows, :] = jnp.where(frame < length, 1.0, 0.0)
            return carry

        self.each(body, 0)
        self.own_count = length.astype(F32)

    def moments_of(self, out, join_pairs):
        chans = self.chans

        def first(rows, item, total):
            value = out[rows, :]
            if join_pairs:
                late = pl.ds(al(item * 64 + SEG), 64)
                tail = value[:, 256:] + self.paired[rows, 0:128] + self.paired[late, 128:256]
                out[rows, 256:] = tail
                value = jnp.concatenate([value[:, :256], tail], axis=1)
            return total + fold(value * self.mask_of(rows, chans))

        total = self.each(first, jnp.zeros((8, chans), F32))
        mean = jnp.sum(total, axis=0, keepdims=True) / self.own_count

        def second(rows, item, total):
            away = out[rows, :] - mean
            return total + fold(away * away * self.mask_of(rows, chans))

        total = self.each(second, jnp.zeros((8, chans), F32))
        return mean, jnp.sum(total, axis=0, keepdims=True)

    def moments_start(self, pairs):
        rows = [mean for mean, _ in pairs] + [spread for _, spread in pairs]
        rows.append(jnp.full((1, 128), 1.0, F32) * self.own_count)
        join = self.join_moments(len(pairs))
        return self.sums_start(self.pack(rows)), len(pairs), join

    def moments_finish(self, started, norms):
        started, fields, join = started
        joined = self.sums_end(started, join)
        each = fields * (self.chans // 128)
        self.count = joined[2 * each : 2 * each + 1, 0:1]
        inv = lax.rsqrt(joined[each : 2 * each] / self.count + EPS)
        for place, norm in enumerate(norms):
            self.means[norm : norm + 1, :] = self.unpack(joined, place)
            self.invs[norm : norm + 1, :] = self.unpack(inv, place)

    def row(self, ref, index):
        return ref[index : index + 1, :]

    def activate(self, layer):
        out, hidden = self.outs[layer], self.hidden[layer + 1]
        mean, inv = self.row(self.means, layer), self.row(self.invs, layer)
        gain = self.row(self.scales, layer) * inv
        shift = self.row(self.shifts, layer)

        def body(rows, item, carry):
            act = (out[rows, :] - mean) * gain + shift
            value = act * sigmoid(act) * self.mask_of(rows, self.chans)
            hidden[pl.ds(al(self.halo + item * 64), 64), :] = value.astype(BF)
            return carry

        self.each(body, 0)
        self.fill_halo(hidden)

    def act_grad(self, layer, out, grad, join_pairs):
        mean, inv = self.row(self.means, layer), self.row(self.invs, layer)
        scale, shift = self.row(self.scales, layer), self.row(self.shifts, layer)
        chans = self.chans

        def body(rows, item, sums):
            norm = (out[rows, :] - mean) * inv
            act = norm * scale + shift
            slope = sigmoid(act)
            slope = slope * (1.0 + act * (1.0 - slope))
            value = grad[rows, :]
            if join_pairs:
                late = pl.ds(al(item * 64 + SEG), 64)
                tail = value[:, 256:] + self.paired[late, 0:128] + self.paired[rows, 128:256]
                value = jnp.concatenate([value[:, :256], tail], axis=1)
            value = value * slope * self.mask_of(rows, chans)
            grad[rows, :] = value
            return sums[0] + fold(value), sums[1] + fold(value * norm)

        zero = jnp.zeros((8, chans), F32)
        sums = self.each(body, (zero, zero))
        return [jnp.sum(value, axis=0, keepdims=True) for value in sums]

    def totals_start(self, parts):
        return self.sums_start(self.pack(parts)), len(parts)

    def totals_middle(self, started):
        started, count = started
        return self.sums_middle(started, self.join_sums), count

    def totals_finish(self, started):
        started, count = started
        joined = self.sums_end(started, self.join_sums)
        return [self.unpack(joined, place) for place in range(count)]

    def norm_grad(self, layer, out, grad, shift_sum, scale_sum, target, offset):
        mean, inv = self.row(self.means, layer), self.row(self.invs, layer)
        gain = self.row(self.scales, layer) * inv
        count = self.count
        flat, tilt = shift_sum / count, scale_sum / count

        def body(rows, item, carry):
            norm = (out[rows, :].astype(F32) - mean) * inv
            mask = self.mask_of(rows, self.chans)
            value = gain * (grad[rows, :] - mask * (flat + norm * tilt))
            target[pl.ds(al(offset + item * 64), 64), :] = value.astype(BF)
            return carry

        self.each(body, 0)

    def frames_in(self, at, ref):
        return jnp.concatenate(
            [ref[part, pl.ds(at, SEG, stride=self.span), :] for part in range(ref.shape[0])],
            axis=1,
        )

    def frames_out(self, at, value, ref):
        for part in range(value.shape[1] // 128):
            ref[part, pl.ds(at, SEG, stride=self.span), :] = value[:, 128 * part : 128 * (part + 1)]

    def last_forward(self):
        chans = self.chans
        ins = (self.outs[4],) + tuple(self.dense_outs)
        means = [self.row(self.means, 4 + k) for k in range(4)]
        invs = [self.row(self.invs, 4 + k) for k in range(4)]
        scales = [self.row(self.scales, 4 + k) for k in range(4)]
        shift = sum(self.row(self.shifts, 4 + k) for k in range(4))

        def body(rows, item, sums):
            norms = [
                (ref[rows, :].astype(F32) - mean) * inv
                for ref, mean, inv in zip(ins, means, invs)
            ]
            total = shift
            for norm, scale in zip(norms, scales):
                total = total + norm * scale
            gate = sigmoid(total)
            mask = self.mask_of(rows, chans)
            value = total * gate * mask
            self.dense_grad[rows, :] = value.astype(BF)
            slope = gate * (1.0 + total * (1.0 - gate))
            value = self.top_grad[rows, :].astype(F32) * mask * slope
            self.grad[rows, :] = value
            return (sums[0] + fold(value),) + tuple(
                old + fold(value * norm) for old, norm in zip(sums[1:], norms)
            )

        sums = self.each(body, (jnp.zeros((8, chans), F32),) * 5, height=32)
        return [jnp.sum(value, axis=0, keepdims=True) for value in sums]

    def dense_weight(self, index):
        piece = self.piece[5]
        at = index * piece
        return self.full[5][:, :, at : at + piece, :].reshape(piece * 8, self.chans)

    def dense_forward(self, index):
        self.dense_outs[index][...] = jnp.dot(
            self.dense_source(index), self.dense_weight(index), preferred_element_type=F32
        ).astype(self.dense_outs[index].dtype)

    def write_frames(self, source, stage, target, place, extra=None):
        lanes = target.shape[1]

        def move(item, carry):
            for k in range(4):
                at = item * 4 + k
                rows = pl.ds(al(at * SEG), SEG)
                value = source[rows, 0:lanes]
                if extra is not None:
                    value = value + extra[rows, 0:lanes]
                self.frames_out(at, value * self.mask_of(rows, lanes), stage)
            return carry

        lax.fori_loop(0, self.span // 4, move, 0)
        sent = [
            self.out_copy(
                stage.at[part], target.at[:, pl.ds(128 * part, 128)], place + part
            )
            for part in range(lanes // 128)
        ]
        if extra is not None:
            self.input_sent = sent
        else:
            self.frames_sent += sent

    def out_copy(self, source, target, place):
        copy = pltpu.make_async_copy(source, target, self.out_sems.at[place])
        copy.start()
        return copy

    def write_output(self):
        def move(item, carry):
            for k in range(4):
                at = item * 4 + k
                value = self.dense_grad[pl.ds(al(at * SEG), SEG), :]
                self.frames_out(at, value.astype(F32), self.stage)
            return carry

        lax.fori_loop(0, self.span // 4, move, 0)

        def body(rows, item, carry):
            value = jnp.concatenate([self.stage[part, rows, :] for part in range(3)], axis=1)
            self.dense_grad[rows, :] = value.astype(BF)
            return carry

        self.each(body, 0)
        self.output_sent = self.out_copy(self.dense_grad, self.block_output, 0)

    def dense_field_grad(self, index):
        totals = self.totals[4]
        self.norm_grad(
            5 + index,
            self.dense_outs[index],
            self.grad,
            totals[0],
            totals[2 + index],
            self.dense_grad,
            0,
        )
        return self.dense_grad[...]

    def dense_source(self, index):
        if index == 0:
            return self.hidden[0][self.halo : self.halo + self.frames, :]
        return self.sources[index - 1][...]

    def dense_weight_grad(self, index):
        if self.output_sent is not None:
            self.output_sent.wait()
            self.output_sent = None
        grad = self.dense_field_grad(index)
        piece = self.piece[5]
        at = 4 * (self.units[0].depth + self.units[1].depth) + index * piece
        got = lax.dot_general(
            self.dense_source(index), grad, TN, preferred_element_type=F32
        ).astype(BF)
        self.homes[0][:, :, at : at + piece, :] = got.reshape(4, 2, piece, self.chans)

    def dense_source_grad(self, index):
        grad = self.dense_field_grad(index)
        got = lax.dot_general(grad, self.dense_weight(index), NT, preferred_element_type=F32)
        spare = self.outs[3]
        spare[:, 0 : got.shape[1]] = got
        if index == 1:
            self.write_frames(spare, self.second_stage, self.first_grad, 3)
        if index == 2:
            for copy in self.input_sent:
                copy.wait()
            self.write_frames(spare, self.stage, self.second_grad, 26)

    def share_norms(self):
        rows = jnp.concatenate(
            [self.held[8][...].astype(F32), self.held[9][...].astype(F32)], axis=0
        )
        rows = jnp.concatenate(
            [rows, jnp.zeros((rows.shape[0], 128 - self.width), F32)], axis=1
        ).astype(BF)
        self.norms[0] = jnp.dot(rows, self.pick(self.n), preferred_element_type=F32)

    def send_norms(self):
        return [
            self.remote(
                self.norms.at[0], self.norms.at[step], self.w, self.narrow_peer(step)
            )
            for step in range(1, 4)
        ]

    def own_channels(self, rows):
        pick = self.pick(self.n)
        total = None
        for _ in range(3):
            high = rows.astype(BF)
            part = lax.dot_general(high, pick, NT, preferred_element_type=F32)
            total = part if total is None else total + part
            rows = rows - high.astype(F32)
        return total[:, : self.width]

    def take_norms(self):
        self.land(self.norm_copies)
        both = self.norms[0] + self.norms[1] + self.norms[2] + self.norms[3]
        self.scales[...] = both[0:8]
        self.shifts[...] = both[8:16]

    def conv(self, layer):
        self.conv_forward(layer, self.hidden[layer], self.outs[layer])

    def moments_begin(self, layer):
        pairs, self.joined = [self.moments_of(self.outs[layer], True)], [layer]
        for index in {2: (0, 1), 3: (2,)}.get(layer, ()):
            pairs.append(self.moments_of(self.dense_outs[index], False))
            self.joined.append(5 + index)
        self.started = self.moments_start(pairs)

    def moments_pass(self, layer):
        started, fields, join = self.started
        self.started = self.sums_middle(started, join), fields, join

    def moments_end(self, layer):
        self.moments_finish(self.started, self.joined)

    def dense_all(self):
        for index in range(3):
            self.dense_forward(index)

    def totals_begin(self, layer):
        if layer == 4:
            parts = self.last_forward()
        else:
            parts = self.act_grad(layer, self.outs[layer], self.outs[layer + 1], True)
        self.started = self.totals_start(parts)

    def totals_pass(self, layer):
        self.started = self.totals_middle(self.started)

    def totals_end(self, layer):
        self.totals[layer] = self.totals_finish(self.started)

    def gather_done(self):
        self.settle()
        for place, unit in enumerate(self.units):
            unit.local_base = unit.base
            group, half = unit.group, place % 2
            base = unit.base
            if group == 5:
                base = 4 * (self.units[0].depth + self.units[1].depth)
            core = 4 if group == 5 else 2 * (group % 2) + half
            first = 8 if group == 5 else 6 + half if group == 0 else 2 * (group % 3) + half
            buffers = dict(self.landings[place])
            buffers.update(self.first_landing[first])
            unit.begin_scatter(
                self.homes[group % 5], base, self.by_core[core], buffers
            )

    def field_grad(self, layer):
        got = self.totals[layer]
        grad = self.grad if layer == 4 else self.outs[layer + 1]
        self.norm_grad(
            layer, self.outs[layer], grad, got[0], got[1], self.conv_grad, self.halo
        )
        self.fill_halo(self.conv_grad)

    def taps_grad(self, layer, item):
        height = self.piece[layer]
        first = 4 * self.units[2 * layer].depth
        middle = -(-first // height)
        low, high = (0, middle) if item == 0 else (middle, self.taps)
        self.weight_grad(
            layer, self.hidden[layer], self.conv_grad, self.homes[layer], low, high
        )

    def conv_back(self, layer):
        out = self.outs[max(layer, 1)]
        lanes = self.hidden[layer].shape[1]
        self.conv_backward(layer, self.conv_grad, out.at[:, pl.ds(0, lanes)])

    def write_input_grad(self):
        self.write_frames(self.outs[1], self.stage, self.input_grad, 1, self.outs[3])

    def write_norm_grads(self):
        rows = [self.totals[layer][1] for layer in range(4)] + self.totals[4][1:5]
        self.norm_grads[0] = self.own_channels(jnp.concatenate(rows, axis=0))
        rows = [self.totals[layer][0] for layer in range(4)] + [self.totals[4][0]] * 4
        self.norm_grads[1] = self.own_channels(jnp.concatenate(rows, axis=0))
        self.frames_sent.append(self.out_copy(self.norm_grads.at[0], self.scale_grad, 6))
        self.frames_sent.append(self.out_copy(self.norm_grads.at[1], self.shift_grad, 7))

    def run(self):
        self.totals = [None] * 5
        self.frames_sent, self.stage_sent, self.outgoing = [], {}, 0
        unit = self.units = [Unit(self, *spec) for spec in self.specs]
        self.homes = [self.full[4]] + list(self.full[1:4]) + [self.first_sum]
        greeted = self.greet()
        self.fetch()
        for copy in self.held_copies:
            copy.wait()
        for group in range(6):
            self.load_local(group)
        self.met(greeted)
        self.schedule(unit)
        self.settle()
        for copies in list(self.stage_sent.values()) + [self.frames_sent]:
            for copy in copies:
                copy.wait()
        if self.sems != SEMS:
            raise ValueError(self.sems)

    def own_part(self):
        self.share_norms()
        self.norm_copies = self.send_norms()
        self.make_mask()
        self.permute_in(0, self.hidden[0], self.halo, True)
        self.fill_halo(self.hidden[0])

    def schedule(self, unit):
        unit[0].exchange()
        unit[1].exchange()
        unit[10].exchange()
        unit[5].exchange()
        self.own_part()
        unit[1].spread()
        unit[10].spread()
        unit[0].spread()
        unit[3].exchange()
        unit[8].exchange()
        unit[5].spread()
        unit[3].spread()
        unit[2].exchange()
        unit[7].exchange()
        unit[1].second()
        unit[9].exchange()
        unit[2].spread()
        unit[10].second()
        self.take_norms()
        unit[4].exchange()
        unit[1].third()
        unit[6].exchange()
        unit[7].spread()
        self.permute_in(3, self.top_grad, 0, False)
        unit[2].side_second()
        unit[3].side_second()
        unit[0].second()
        unit[1].cores()
        unit[4].spread()
        unit[10].third()
        unit[5].side_second()
        unit[0].third()
        unit[2].second()
        unit[5].second()
        unit[3].second()
        unit[1].arrived()
        unit[2].third()
        unit[2].side_third()
        unit[0].cores()
        unit[3].third()
        unit[0].arrived()
        self.conv(0)
        unit[10].cores()
        self.moments_begin(0)
        unit[2].cores()
        unit[3].side_third()
        self.moments_pass(0)
        unit[7].second()
        unit[4].second()
        unit[4].side_second()
        unit[6].spread()
        unit[3].cores()
        unit[5].side_third()
        unit[2].arrived()
        unit[3].arrived()
        unit[5].third()
        unit[9].spread()
        self.permute_in(1, self.sources[0], 0, True)
        unit[6].side_second()
        self.permute_in(2, self.sources[1], 0, True)
        self.moments_end(0)
        unit[4].third()
        self.activate(0)
        unit[4].side_third()
        self.conv(1)
        self.moments_begin(1)
        unit[5].cores()
        self.moments_pass(1)
        unit[6].second()
        unit[7].side_second()
        unit[8].spread()
        unit[7].third()
        unit[9].second()
        unit[10].arrived()
        self.dense_all()
        unit[4].cores()
        unit[8].side_second()
        unit[4].arrived()
        unit[6].side_third()
        unit[6].third()
        unit[5].arrived()
        self.moments_end(1)
        self.activate(1)
        self.conv(2)
        unit[7].side_third()
        self.moments_begin(2)
        self.moments_pass(2)
        unit[9].side_second()
        unit[8].second()
        unit[9].third()
        unit[6].cores()
        unit[7].cores()
        unit[6].arrived()
        unit[8].side_third()
        unit[7].arrived()
        unit[8].third()
        self.moments_end(2)
        self.activate(2)
        self.conv(3)
        unit[9].side_third()
        self.moments_begin(3)
        self.moments_pass(3)
        unit[8].cores()
        unit[9].cores()
        unit[8].arrived()
        unit[9].arrived()
        self.moments_end(3)
        self.activate(3)
        self.conv(4)
        self.moments_begin(4)
        self.gather_done()
        self.moments_pass(4)
        self.moments_end(4)
        self.totals_begin(4)
        self.totals_pass(4)
        self.write_output()
        self.totals_end(4)
        self.field_grad(4)
        self.conv_back(4)
        self.totals_begin(3)
        self.taps_grad(4, 0)
        self.totals_pass(3)
        unit[8].back_cores()
        self.taps_grad(4, 1)
        unit[9].back_cores()
        unit[8].back_third()
        unit[9].back_third()
        self.totals_end(3)
        self.field_grad(3)
        self.conv_back(3)
        self.totals_begin(2)
        self.taps_grad(3, 0)
        self.totals_pass(2)
        unit[8].back_side_second()
        unit[8].back_second()
        unit[9].back_second()
        unit[6].back_cores()
        self.taps_grad(3, 1)
        unit[9].back_side_second()
        unit[7].back_cores()
        unit[6].back_third()
        self.totals_end(2)
        unit[8].back_first()
        self.field_grad(2)
        unit[7].back_third()
        self.conv_back(2)
        self.totals_begin(1)
        self.totals_pass(1)
        unit[6].back_side_second()
        unit[6].back_second()
        self.taps_grad(2, 0)
        unit[7].back_second()
        unit[4].back_cores()
        unit[7].back_side_second()
        self.taps_grad(2, 1)
        unit[6].back_first()
        self.totals_end(1)
        unit[4].back_third()
        unit[5].back_cores()
        self.field_grad(1)
        unit[9].back_first()
        self.conv_back(1)
        unit[8].back_side_first()
        unit[5].back_third()
        self.taps_grad(1, 0)
        unit[4].back_side_second()
        unit[4].back_second()
        unit[8].back_exchange()
        self.totals_begin(0)
        self.totals_pass(0)
        unit[2].back_cores()
        unit[7].back_first()
        unit[5].back_second()
        unit[5].back_side_second()
        unit[7].back_side_first()
        unit[2].back_third()
        self.taps_grad(1, 1)
        unit[3].back_cores()
        self.dense_weight_grad(0)
        self.totals_end(0)
        unit[9].back_side_first()
        unit[3].back_third()
        unit[4].back_first()
        self.field_grad(0)
        unit[5].back_first()
        self.taps_grad(0, 0)
        unit[4].back_side_first()
        unit[0].back_cores()
        self.taps_grad(0, 1)
        unit[6].back_side_first()
        unit[1].back_cores()
        unit[3].back_second()
        unit[0].back_third()
        unit[2].back_side_second()
        unit[5].back_side_first()
        self.dense_weight_grad(1)
        self.dense_source_grad(0)
        unit[3].back_side_second()
        unit[8].back_deliver()
        unit[2].back_second()
        self.dense_weight_grad(2)
        unit[3].back_first()
        unit[1].back_third()
        unit[0].back_second()
        self.write_norm_grads()
        unit[4].back_exchange()
        unit[10].back_cores()
        unit[9].back_exchange()
        self.conv_back(0)
        unit[2].back_first()
        unit[2].back_side_first()
        unit[1].back_second()
        unit[10].back_third()
        unit[5].back_exchange()
        self.write_input_grad()
        unit[0].back_first()
        self.dense_source_grad(1)
        unit[6].back_exchange()
        unit[10].back_second()
        unit[9].back_deliver()
        unit[1].back_first()
        unit[3].back_side_first()
        unit[6].back_deliver()
        unit[7].back_exchange()
        unit[10].back_first()
        unit[2].back_exchange()
        unit[3].back_exchange()
        unit[4].back_deliver()
        unit[1].back_exchange()
        unit[0].back_exchange()
        unit[7].back_deliver()
        unit[5].back_deliver()
        unit[2].back_deliver()
        unit[10].back_exchange()
        unit[3].back_deliver()
        self.dense_source_grad(2)
        unit[0].back_deliver()
        unit[1].back_deliver()
        unit[10].back_deliver()


INS = (
    "block_input",
    "prior_first",
    "prior_second",
    "raw_lengths",
    "speed_index",
    "conv_one",
    "conv_two",
    "conv_three",
    "conv_four",
    "conv_five",
    "dense_input",
    "dense_first",
    "dense_second",
    "norm_scale",
    "norm_shift",
    "out_grad",
)
OUTS = (
    ("block_output", "input_grad", "first_grad", "second_grad")
    + tuple(name + GRAD for name in INS[5:13])
    + ("scale_grad", "shift_grad")
)
FIRST_X, FIRST_Y, SIDE_X, SIDE_Y = Z + X + Y, Z + Y + X, X + Z + Y, Y + Z + X
SEMS = 193


PARTS = (
    ((32, 32, 0, 0), (32, 16, 0, 0)),
    ((32, 16, 16, 16), (16, 32, 16, 16)),
    ((32, 16, 16, 16), (16, 32, 16, 16)),
    ((32, 16, 16, 16), (16, 32, 16, 16)),
    ((32, 16, 16, 16), (16, 32, 16, 16)),
    ((16, 16, 0, 0),),
)


def hop_buffers(spec, stages, vmem, chans):
    _, _, _, parts = spec
    found = {}
    early = sum(size for order, size in parts if order[0] == Z)
    for order, size in parts:
        for stage in stages:
            if not size or (stage == 0 and order == FIRST_Y):
                continue
            keep, axis = order[:stage], order[stage]
            count = (3 if axis == Z else 1) * (2 if Y in keep else 1)
            inner = ((4,) if Z in keep else ()) + ((2,) if X in keep else ())
            rows = early if order == FIRST_X and stage == 0 else size
            found[order + str(stage)] = vmem((count,) + inner + (rows, chans), BF)
    return found


def device_program(*args):
    named = dict(zip(INS, args))
    frames, c_in = args[0].shape[1:]
    chans = named["out_grad"].shape[2]
    taps = named["conv_one"].shape[0]
    width = named["conv_one"].shape[2]
    piece = [c_in // 8] + [chans // 8] * 4
    height = [taps * part for part in piece] + [3 * piece[0]]
    piece.append(piece[0])
    specs = []
    for group, rows in enumerate(height):
        quarter = -(-rows // 64) * 16
        base = 0
        for parts in PARTS[group]:
            parts = tuple(zip((FIRST_X, FIRST_Y, SIDE_X, SIDE_Y), parts))
            depth = sum(size for _, size in parts)
            specs.append((group, base, depth, parts))
            base += 4 * depth
        if base != 4 * quarter:
            raise ValueError((group, base, quarter))
    tops = [max(base + 4 * depth for at, base, depth, _ in specs if at == g) for g in range(6)]
    halo = (taps // 2) * SEG
    tall = frames + 2 * halo

    shape = [args[spot].shape for spot in (15, 0, 1, 2)]
    shape = [(frames, one[2]) for one in shape]
    shape += [args[spot].shape for spot in range(5, 13)] + [(8, width)] * 2
    kinds = [BF] + [F32] * 13
    vmem = pltpu.VMEM
    groups = range(6)
    scratch = {
        "full": [vmem((4, 2, tops[g], chans), BF) for g in groups],
        "local": [vmem((tops[g], 128), BF) for g in groups],
        "landing": [vmem((3, spec[2], 128), BF) for spec in specs],
        "by_core": [vmem((2, 4, 2, spec[2], chans), BF) for spec in specs[2:6]]
        + [vmem((2, 4, 2, specs[10][2], chans), BF)],
        "first_landing": [hop_buffers(specs[at], (2,), vmem, chans) for at in (2, 3, 4, 5, 6, 7, 0, 1, 10)],
        "landings": [hop_buffers(spec, (0, 1), vmem, chans) for spec in specs],
        "first_sum": vmem((4, 2, tops[4], chans), BF),
        "stage": vmem((chans // 128, frames, 128), F32),
        "second_stage": vmem((c_in // 128, frames, 128), F32),
        "grad_stage": [vmem(args[5 + g].shape, F32) for g in (1, 2, 0)]
        + [vmem((3, c_in // 8, width), F32)],
        "held": [vmem(args[5 + at].shape, BF) for at in range(10)],
        "norm_grads": vmem((2, 8, width), F32),
        "out_sems": pltpu.SemaphoreType.DMA((28,)),
        "hidden": [vmem((tall, c_in), BF)] + [vmem((tall, chans), BF)] * 4,
        "outs": [vmem((frames, chans), F32)] * 5,
        "dense_outs": [vmem((frames, chans), BF)] * 3,
        "sources": [vmem((frames, c_in), BF)] * 2,
        "top_grad": vmem((frames, chans), BF),
        "conv_grad": vmem((tall, chans), BF),
        "dense_grad": vmem((frames, chans), BF),
        "grad": vmem((frames, chans), F32),
        "paired": vmem((frames + SEG, 256), F32),
        "valid": vmem((frames, 128), F32),
        "mine": vmem((2, 2, 24, 128), F32),
        "others": vmem((2, 16, 24, 128), F32),
        "norms": vmem((4, 16, chans), F32),
        "scales": vmem((8, chans), F32),
        "shifts": vmem((8, chans), F32),
        "means": vmem((8, chans), F32),
        "invs": vmem((8, chans), F32),
        "send_sems": pltpu.SemaphoreType.DMA((SEMS,)),
        "recv_sems": pltpu.SemaphoreType.DMA((SEMS,)),
        "fetch_sems": pltpu.SemaphoreType.DMA((14,)),
        "sum_send": pltpu.SemaphoreType.DMA((4,)),
        "sum_recv": pltpu.SemaphoreType.DMA((4,)),
    }
    flat, tree = jax.tree.flatten(scratch, is_leaf=lambda leaf: not isinstance(leaf, (dict, list)))

    def body(*refs):
        refs, rest = dict(zip(INS + OUTS, refs)), refs[len(INS) + len(OUTS) :]
        refs.update(jax.tree.unflatten(tree, rest))
        refs["given"] = [refs[name] for name in INS[5:15]]
        refs["pieces"] = [refs["held"][at : at + 1] for at in range(5)] + [refs["held"][5:8]]
        refs["grad_outs"] = [[refs[name + GRAD]] for name in INS[5:10]] + [
            [refs[name + GRAD] for name in INS[10:13]]
        ]
        refs["piece"], refs["specs"] = piece, specs
        kernel = Kernel(refs, (taps, frames, chans, width))
        kernel.run()

    outside = pl.BlockSpec(memory_space=pl.ANY)
    small = pl.BlockSpec(memory_space=pltpu.SMEM)
    outs = pl.pallas_call(
        body,
        out_shape=[jax.ShapeDtypeStruct(dims, kind) for dims, kind in zip(shape, kinds)],
        in_specs=[small if spot in (3, 4) else outside for spot in range(16)],
        out_specs=[outside] * 14,
        scratch_shapes=flat,
        compiler_params=pltpu.CompilerParams(
            collective_id=0, has_side_effects=True, vmem_limit_bytes=63 * 2**20
        ),
    )(*args)
    outs = hand_over(outs)
    return tuple(out[None] if place < 4 else out for place, out in enumerate(outs))


def hand_over(arrays):
    count = len(arrays)
    parts = []
    for place, one in enumerate(arrays):
        size = one.shape[0] // 4 if one.shape[0] % 64 == 0 else one.shape[0]
        parts += [(place, at, size) for at in range(0, one.shape[0], size)]

    def body(*refs):
        sems = refs[-1]
        def cut(part, place):
            rows = pl.ds(*parts[part][1:])
            return refs[place].at[rows]

        first = [
            pltpu.make_async_copy(
                cut(part, place), cut(part, 2 * count + place), sems.at[part]
            )
            for part, (place, _, _) in enumerate(parts)
        ]
        for copy in first:
            copy.start()
        second = [
            pltpu.make_async_copy(
                cut(part, 2 * count + place), cut(part, count + place), sems.at[len(parts) + part]
            )
            for part, (place, _, _) in enumerate(parts)
        ]
        for came, copy in zip(first, second):
            came.wait()
            copy.start()
        for copy in second:
            copy.wait()

    return pl.pallas_call(
        body,
        out_shape=[jax.ShapeDtypeStruct(one.shape, one.dtype) for one in arrays],
        in_specs=[pl.BlockSpec(memory_space=pl.ANY)] * count,
        out_specs=[pl.BlockSpec(memory_space=pl.ANY)] * count,
        scratch_shapes=[pltpu.VMEM(one.shape, one.dtype) for one in arrays]
        + [pltpu.SemaphoreType.DMA((2 * len(parts),))],
        compiler_params=pltpu.CompilerParams(vmem_limit_bytes=62 * 2**20),
    )(*arrays)


def silu_slope(value):
    sigmoid = jax.nn.sigmoid(value)
    return sigmoid * (1.0 + value * (1.0 - sigmoid))


def padded_time(field, extent):
    half = extent // 2
    return jnp.pad(field, ((0, 0), (half, half), (0, 0)))


def conv_apply(field, weight):
    extent = weight.shape[0]
    length = field.shape[1]
    padded = padded_time(field, extent)
    total = jnp.einsum(
        APPLY, padded[:, 0:length], weight[0], preferred_element_type=jnp.float32
    )
    for offset in range(1, extent):
        total = total + jnp.einsum(
            APPLY,
            padded[:, offset : offset + length],
            weight[offset],
            preferred_element_type=jnp.float32,
        )
    return total


def conv_grads(field, grad_out, weight):
    extent = weight.shape[0]
    length = field.shape[1]
    padded = padded_time(field, extent)
    padded_grad = padded_time(grad_out, extent)
    taps = []
    grad_in = None
    for offset in range(extent):
        taps.append(
            jnp.einsum(
                OUTER,
                padded[:, offset : offset + length],
                grad_out,
                preferred_element_type=jnp.float32,
            )
        )
        back = extent - 1 - offset
        term = jnp.einsum(
            BACK,
            padded_grad[:, back : back + length],
            weight[offset],
            preferred_element_type=jnp.float32,
        )
        grad_in = term if grad_in is None else grad_in + term
    return (jnp.stack(taps), grad_in)


def moments(fields, mask, local_count):
    firsts = jnp.stack([jnp.sum(field * mask, axis=(0, 1)) for field in fields])
    firsts, count = lax.psum((firsts, local_count), (WIDE, NARROW))
    means = firsts / count
    seconds = jnp.stack(
        [
            jnp.sum(mask * jnp.square(field - means[place]), axis=(0, 1))
            for place, field in enumerate(fields)
        ]
    )
    spread = lax.psum(seconds, (WIDE, NARROW)) / count
    return (means, lax.rsqrt(spread + EPS), count)


def norm_backward(grad_act, norms, scales, inv_std, mask, count):
    shift_part = jnp.sum(grad_act, axis=(0, 1))
    scale_parts = jnp.stack([jnp.sum(grad_act * norm, axis=(0, 1)) for norm in norms])
    shift_sum, scale_sum = lax.psum((shift_part, scale_parts), (WIDE, NARROW))
    grads = []
    for place in range(len(norms)):
        centered = grad_act - mask * (shift_sum + norms[place] * scale_sum[place]) / count
        grads.append((scales[place] * inv_std[place] * centered).astype(jnp.bfloat16))
    return (grads, shift_sum, scale_sum)


def collect(item):
    return lax.all_gather(
        lax.all_gather(item, WIDE, axis=1, tiled=True), NARROW, axis=2, tiled=True
    )


def spread(item):
    item = lax.psum_scatter(item.astype(BF), NARROW, scatter_dimension=2, tiled=True)
    return lax.psum_scatter(item.astype(F32), WIDE, scatter_dimension=1, tiled=True)


def shards(
    block_input,
    prior_first,
    prior_second,
    raw_lengths,
    speed_index,
    conv_one,
    conv_two,
    conv_three,
    conv_four,
    conv_five,
    dense_input,
    dense_first,
    dense_second,
    norm_scale,
    norm_shift,
    out_grad,
):
    utter, length = (block_input.shape[0], block_input.shape[1])
    lengths = raw_lengths * 10 // (9 + speed_index)
    frames = lax.broadcasted_iota(jnp.int32, (utter, length), 1)
    mask = (frames < lengths[:, None]).astype(jnp.float32)[:, :, None]
    mask_low = mask.astype(jnp.bfloat16)
    local_count = jnp.sum(lengths).astype(jnp.float32)
    weights = (
        conv_one,
        conv_two,
        conv_three,
        conv_four,
        conv_five,
        dense_input,
        dense_first,
        dense_second,
    )
    full_weights = [collect(weight) for weight in weights]
    scales = lax.all_gather(norm_scale, NARROW, axis=1, tiled=True).astype(F32)
    shifts = lax.all_gather(norm_shift, NARROW, axis=1, tiled=True).astype(F32)
    sources = (block_input * mask_low, prior_first * mask_low, prior_second * mask_low)
    hidden = sources[0]
    inputs_kept, norms_kept, acts_kept, inv_kept = ([], [], [], [])
    for index in range(4):
        conv_out = conv_apply(hidden, full_weights[index])
        means, inv_std, count = moments((conv_out,), mask, local_count)
        norm = (conv_out - means[0]) * inv_std[0]
        act = scales[index] * norm + shifts[index]
        inputs_kept.append(hidden)
        norms_kept.append(norm)
        acts_kept.append(act)
        inv_kept.append(inv_std[0])
        hidden = (jax.nn.silu(act) * mask).astype(jnp.bfloat16)
    last_out = conv_apply(hidden, full_weights[4])
    dense_outs = tuple(
        (
            jnp.einsum(
                APPLY,
                sources[place],
                full_weights[5 + place][0],
                preferred_element_type=jnp.float32,
            )
            for place in range(3)
        )
    )
    fields = (last_out,) + dense_outs
    means, inv_std, count = moments(fields, mask, local_count)
    last_norms = tuple(((fields[place] - means[place]) * inv_std[place] for place in range(4)))
    total = scales[4] * last_norms[0] + shifts[4]
    for place in range(1, 4):
        total = total + scales[4 + place] * last_norms[place] + shifts[4 + place]
    block_output = (jax.nn.silu(total) * mask).astype(jnp.bfloat16)
    grad_total = out_grad.astype(jnp.float32) * mask * silu_slope(total)
    field_grads, shift_sum, scale_sum = norm_backward(
        grad_total, last_norms, scales[4:8], inv_std, mask, count
    )
    weight_grads = [None] * 8
    scale_rows = [None] * 8
    shift_rows = [None] * 8
    for place in range(4):
        scale_rows[4 + place] = scale_sum[place]
        shift_rows[4 + place] = shift_sum
    weight_grads[4], grad_hidden = conv_grads(hidden, field_grads[0], full_weights[4])
    source_grads = []
    for place in range(3):
        weight_grads[5 + place] = jnp.einsum(
            OUTER,
            sources[place],
            field_grads[1 + place],
            preferred_element_type=jnp.float32,
        )[None]
        source_grads.append(
            jnp.einsum(
                BACK,
                field_grads[1 + place],
                full_weights[5 + place][0],
                preferred_element_type=jnp.float32,
            )
        )
    for index in (3, 2, 1, 0):
        grad_act = grad_hidden * mask * silu_slope(acts_kept[index])
        grads_one, shift_one, scale_one = norm_backward(
            grad_act,
            (norms_kept[index],),
            scales[index : index + 1],
            inv_kept[index][None],
            mask,
            count,
        )
        scale_rows[index] = scale_one[0]
        shift_rows[index] = shift_one
        weight_grads[index], grad_hidden = conv_grads(
            inputs_kept[index], grads_one[0], full_weights[index]
        )
    input_grad = mask * (grad_hidden + source_grads[0])
    first_grad = mask * source_grads[1]
    second_grad = mask * source_grads[2]
    owned = [spread(grad) for grad in weight_grads]
    portion = scales.shape[1] // lax.axis_size(NARROW)
    start = lax.axis_index(NARROW) * portion
    scale_grad = lax.dynamic_slice_in_dim(jnp.stack(scale_rows), start, portion, 1)
    shift_grad = lax.dynamic_slice_in_dim(jnp.stack(shift_rows), start, portion, 1)
    return (
        block_output,
        input_grad,
        first_grad,
        second_grad,
        owned[0],
        owned[1],
        owned[2],
        owned[3],
        owned[4],
        owned[5],
        owned[6],
        owned[7],
        scale_grad,
        shift_grad,
    )


def solution(mesh):
    by_utterance = P((WIDE, NARROW), None, None)
    lengths = P((WIDE, NARROW))
    weight = P(None, WIDE, NARROW)
    norm = P(None, NARROW)
    kernel_fits = (mesh.shape[WIDE], mesh.shape[NARROW]) == (8, 4)
    return jax.shard_map(
        device_program if kernel_fits else shards,
        mesh=mesh,
        in_specs=(by_utterance,) * 3
        + (lengths,) * 2
        + (weight,) * 8
        + (norm,) * 2
        + (by_utterance,),
        out_specs=(by_utterance,) * 4 + (weight,) * 8 + (norm,) * 2,
        check_vma=False,
    )
```
